32 devices in a mesh: dp: 8 (over y, x, core), tensor: 4 (over z).
Axes of the slice: x: 2, y: 2, z: 4, core: 2. Of those that a mesh axis runs over, the one named last changes fastest.
Arguments:
- tokens: bfloat16 [8, 1024, 1536], P('dp', 'tensor'), may hold values from -6 to 6
- segments: int32 [8, 1024], P('dp'), may hold values from 0 to 4, as said below
- positions: int32 [8, 1024], P('dp'), may hold values from 0 to 2047, as said below
- gain_attn: bfloat16 [1536], P('dp'), may hold values from 0.5 to 1.5
- w_query: bfloat16 [1536, 1536], P('dp', 'tensor'), may hold values from -0.15625 to 0.15625
- w_key: bfloat16 [1536, 768], P('dp', 'tensor'), may hold values from -0.15625 to 0.15625
- w_value: bfloat16 [1536, 768], P('dp', 'tensor'), may hold values from -0.15625 to 0.15625
- w_out: bfloat16 [1536, 1536], P('tensor', 'dp'), may hold values from -0.625 to 0.625
- gain_mlp: bfloat16 [1536], P('dp'), may hold values from 0.5 to 1.5
- w_gate: bfloat16 [1536, 4096], P('dp', 'tensor'), may hold values from -0.15625 to 0.15625
- w_up: bfloat16 [1536, 4096], P('dp', 'tensor'), may hold values from -0.15625 to 0.15625
- w_down: bfloat16 [4096, 1536], P('tensor', 'dp'), may hold values from -0.09375 to 0.09375
- cotangent: bfloat16 [8, 1024, 1536], P('dp', 'tensor'), may hold values from -6 to 6
Outputs:
- mixed: bfloat16 [8, 1024, 1536], P('dp', 'tensor')
- grad_tokens: bfloat16 [8, 1024, 1536], P('dp', 'tensor')
- grad_gain_attn: float32 [1536], P('dp')
- grad_query: float32 [1536, 1536], P('dp', 'tensor')
- grad_key: float32 [1536, 768], P('dp', 'tensor')
- grad_value: float32 [1536, 768], P('dp', 'tensor')
- grad_out: float32 [1536, 1536], P('tensor', 'dp')
- grad_gain_mlp: float32 [1536], P('dp')
- grad_gate: float32 [1536, 4096], P('dp', 'tensor')
- grad_up: float32 [1536, 4096], P('dp', 'tensor')
- grad_down: float32 [4096, 1536], P('tensor', 'dp')
The draws below stay inside these ranges and needn't reach their ends.
Inputs may be any that keep to these rules, and one draw needn't show every extreme that they name: `segments`: document numbers never fall along a packed sequence and every one of the five is present in each sequence. Inside a document positions rise by one from token to token.
All inputs are finite; a program needn't handle non-finite values.
Results may differ from the reference program's by a relative error of at most 0.023.
Values may be sent and summed in bfloat16 or wider, within the bound.
No kernel may reach another device: no remote copies, remote signals or barrier semaphores. Data moves between devices by JAX's collectives and lax.ppermute only.
A program may use at most 192 MiB of HBM per device.

```python
import math
import jax
import jax.numpy as jnp
from jax import lax

D = 1536
HEADS = 16
KV_HEADS = 8
HEAD = 96
FF = 4096
LEN = 1024
QBLOCK = 512
QW = 1536
KVW = 768
SEQS = 8


def pack_layout(key):
    keys = jax.random.split(key, 5)
    shape = (SEQS,)
    long_first = jax.random.randint(keys[0], shape, 2, LEN // 8)
    early_cut = jax.random.randint(keys[1], shape, 1, long_first)
    long_last = jax.random.randint(keys[2], shape, 7 * LEN // 8, LEN - 2)
    late_cut = jax.random.randint(keys[3], shape, long_last + 1, LEN)
    bounds = jnp.stack([early_cut, long_first, long_last, late_cut], axis=1).astype(jnp.int32)
    places = jnp.arange(LEN, dtype=jnp.int32)
    segment_rows = jnp.sum((places[None, :, None] >= bounds[:, None, :]).astype(jnp.int32), axis=2).astype(jnp.int32)
    starts = jnp.concatenate([jnp.zeros((SEQS, 1), jnp.int32), bounds], axis=1)
    offsets = jax.random.randint(keys[4], (SEQS, 5), 0, LEN).astype(jnp.int32)
    offsets = offsets.at[:, 0].set(0)
    offsets = offsets.at[:, 2].set((2 * LEN - (long_last - long_first)).astype(jnp.int32))
    position_rows = places[None, :] - jnp.take_along_axis(starts, segment_rows, axis=1) + jnp.take_along_axis(offsets, segment_rows, axis=1)
    return (segment_rows, position_rows.astype(jnp.int32))


def draw_segments(key, part):
    return pack_layout(key)[0]


def draw_positions(key, part):
    return pack_layout(key)[1]


def block_levels(stream_key, extent, pieces, least, top_value):
    def one(dim, shards_of):
        steps = jax.random.uniform(jax.random.fold_in(jax.random.fold_in(stream_key, 6), dim), (shards_of,), jnp.float32, least / len(pieces), top_value / len(pieces))
        return jnp.repeat(jnp.exp(steps), extent[dim] // shards_of).reshape((-1,) + (1,) * (len(extent) - dim - 1))

    factor_of = one(*pieces[0])
    for cut in pieces[1:]:
        factor_of = factor_of * one(*cut)
    return factor_of


def normal_values(key, extent, width, reach, cuts=(), kind=jnp.bfloat16):
    drawn = jax.random.normal(key, extent, jnp.float32) * width
    if len(cuts) > 0:
        drawn = block_levels(key, extent, cuts, -0.22, 0.18) * drawn
    return jnp.clip(drawn, min=-reach, max=reach).astype(kind)


def setup_inputs(seed: int = 0) -> dict:
    splits = jax.random.split(jax.random.key(seed), 14)
    tokens = normal_values(splits[0], (SEQS, LEN, D), 1.0, 6.0, ((0, 8), (1, 4)))
    segments = draw_segments(jax.random.fold_in(splits[13], 71), 0)
    positions = draw_positions(jax.random.fold_in(splits[13], 71), 0)
    gain_attn = jnp.clip(1.0 + 0.1 * jax.random.normal(splits[3], (D,), jnp.float32), 0.5, 1.5).astype(jnp.bfloat16)
    w_query = normal_values(splits[4], (D, QW), D ** -0.5, 0.15625, ((0, 8), (1, 4)))
    w_key = normal_values(splits[5], (D, KVW), D ** -0.5, 0.15625, ((0, 8), (1, 4)))
    w_value = normal_values(splits[6], (D, KVW), D ** -0.5, 0.15625, ((0, 8), (1, 4)))
    w_out = normal_values(splits[7], (QW, D), (QW // 16) ** -0.5, 0.625, ((0, 4), (1, 8)))
    gain_mlp = jnp.clip(1.0 + 0.1 * jax.random.normal(splits[8], (D,), jnp.float32), 0.5, 1.5).astype(jnp.bfloat16)
    w_gate = normal_values(splits[9], (D, FF), D ** -0.5, 0.15625, ((0, 8), (1, 4)))
    w_up = normal_values(splits[10], (D, FF), D ** -0.5, 0.15625, ((0, 8), (1, 4)))
    w_down = normal_values(splits[11], (FF, D), FF ** -0.5, 0.09375, ((0, 4), (1, 8)))
    cotangent = normal_values(splits[12], (SEQS, LEN, D), 1.0, 6.0, ((0, 8), (1, 4)))
    return dict(tokens=tokens, segments=segments, positions=positions, gain_attn=gain_attn, w_query=w_query, w_key=w_key, w_value=w_value, w_out=w_out, gain_mlp=gain_mlp, w_gate=w_gate, w_up=w_up, w_down=w_down, cotangent=cotangent)


EPSILON = 1e-05
ROTARY_BASE = 100000.0
MASKED = -1e+30

@jax.custom_vjp
def low(v):
    return lax.optimization_barrier(v.astype(jnp.bfloat16)).astype(jnp.float32)

@jax.custom_vjp
def low_back(v):
    return v

def low_keep(v):
    return (low(v), None)

def low_pass(kept, grad):
    return (grad,)

def back_keep(v):
    return (v, None)

def back_low(kept, grad):
    return (low(grad),)
low.defvjp(low_keep, low_pass)
low_back.defvjp(back_keep, back_low)

def matmul_high(left_operand, right_operand):
    return jnp.matmul(left_operand, right_operand, precision=lax.Precision.HIGHEST)

def normalize(values, gain):
    scaling = lax.rsqrt(lax.optimization_barrier(jnp.mean(values * values, axis=-1, keepdims=True)) + EPSILON)
    return values * scaling * gain

def rotary_tables(place_row):
    halves = jnp.arange(HEAD // 2, dtype=jnp.float32)
    inverse = ROTARY_BASE ** (-2.0 * halves / HEAD)
    angles = place_row.astype(jnp.float32)[:, None] * inverse[None, :]
    return (jnp.cos(angles)[:, None, :], jnp.sin(angles)[:, None, :])

def rotate(values, cosine, sine):
    leading = values[..., :HEAD // 2]
    trailing = values[..., HEAD // 2:]
    return jnp.concatenate([leading * cosine - trailing * sine, trailing * cosine + leading * sine], axis=-1)

def attend_sequence(queries, keys, values, segment_row):
    grouped = HEADS // KV_HEADS
    keys_all = jnp.repeat(keys, grouped, axis=1)
    values_all = jnp.repeat(values, grouped, axis=1)
    places = jnp.arange(LEN, dtype=jnp.int32)
    scaling = HEAD ** (-0.5)

    def one_block(offset):
        block_rows = lax.dynamic_slice_in_dim(queries, offset, QBLOCK, 0)
        block_places = lax.dynamic_slice_in_dim(places, offset, QBLOCK, 0)
        segment_ids_per_block = lax.dynamic_slice_in_dim(segment_row, offset, QBLOCK, 0)
        raw = jnp.einsum('qhd,khd->hqk', block_rows, keys_all, precision=lax.Precision.HIGHEST)
        scores = low_back(raw) * scaling
        allowed = (segment_ids_per_block[:, None] == segment_row[None, :]) & (places[None, :] <= block_places[:, None])
        scores = jnp.where(allowed[None], scores, MASKED)
        totals = jax.nn.logsumexp(scores, axis=-1, keepdims=True)
        weights = low(jnp.exp(scores - totals))
        return jnp.einsum('hqk,khd->qhd', weights, values_all, precision=lax.Precision.HIGHEST)
    offsets = (jnp.arange(LEN // QBLOCK) * QBLOCK).astype(jnp.int32)
    blocks = lax.map(jax.checkpoint(one_block), offsets)
    return blocks.reshape(LEN, HEADS, HEAD)

def layer_forward(weight_set, inputs, segment_rows, position_rows):
    gain_first, query_w, key_w, value_w, output_w, gain_second, gate_weight, upward_w, down_w = weight_set
    count = inputs.shape[0]
    normed_first = low(normalize(inputs, gain_first))
    queries = low_back(matmul_high(normed_first, query_w)).reshape(count, LEN, HEADS, HEAD)
    keys = low_back(matmul_high(normed_first, key_w)).reshape(count, LEN, KV_HEADS, HEAD)
    values = low(low_back(matmul_high(normed_first, value_w))).reshape(count, LEN, KV_HEADS, HEAD)

    def one_sequence(batch_item):
        seq_queries, seq_keys, seq_values, segment_row, position_row = batch_item
        cosine, sine = rotary_tables(position_row)
        return attend_sequence(low(rotate(seq_queries, cosine, sine)), low(rotate(seq_keys, cosine, sine)), seq_values, segment_row)
    attended = lax.map(one_sequence, (queries, keys, values, segment_rows, position_rows))
    attended = low(low_back(attended.reshape(count, LEN, QW)))
    hidden_state = inputs + low_back(matmul_high(attended, output_w))
    normed_second = low(normalize(hidden_state, gain_second))
    gating = low_back(matmul_high(normed_second, gate_weight))
    upward = low_back(matmul_high(normed_second, upward_w))
    activation = low(jax.nn.silu(gating) * upward)
    return hidden_state + low_back(matmul_high(activation, down_w))

def reference(tokens, segments, positions, gain_attn, w_query, w_key, w_value, w_out, gain_mlp, w_gate, w_up, w_down, cotangent):
    weight_set = tuple((argument.astype(jnp.float32) for argument in (gain_attn, w_query, w_key, w_value, w_out, gain_mlp, w_gate, w_up, w_down)))
    grouped = math.gcd(SEQS, 4)
    batches = SEQS // grouped

    def reshape_groups(array):
        return array.reshape((batches, grouped) + array.shape[1:])

    def group_step(totals, batch_item):
        inputs, segment_rows, position_rows, incoming = batch_item

        def forward(current_weights, values_now):
            return layer_forward(current_weights, values_now, segment_rows, position_rows)
        outcome, pullback = jax.vjp(forward, weight_set, inputs.astype(jnp.float32))
        weight_grads, input_grads = pullback(incoming.astype(jnp.float32))
        totals = jax.tree.map(jnp.add, totals, weight_grads)
        return (totals, (outcome.astype(jnp.bfloat16), input_grads.astype(jnp.bfloat16)))
    zeros = jax.tree.map(jnp.zeros_like, weight_set)
    totals, (mixed, grad_tokens) = lax.scan(group_step, zeros, (reshape_groups(tokens), reshape_groups(segments), reshape_groups(positions), reshape_groups(cotangent)))
    mixed = mixed.reshape(SEQS, LEN, D)
    grad_tokens = grad_tokens.reshape(SEQS, LEN, D)
    return (mixed, grad_tokens, totals[0], totals[1], totals[2], totals[3], totals[4], totals[5], totals[6], totals[7], totals[8])
```

```python
import functools
import jax
import jax.numpy as jnp
import numpy as np
from jax import lax
from jax.experimental import pallas as pl
from jax.experimental.pallas import tpu as pltpu
from jax.sharding import PartitionSpec as P

HEADS = 16
KV_HEADS = 8
HEAD = 96
HALF = 48
LANES = 128
LEN = 1024
QBLOCK = 256
EPSILON = 1e-05
ROTARY_BASE = 100000.0
MASKED = -1e30
SCALE = HEAD ** (-0.5)
LOG2E = 1.4426950408889634
VMEM = 56 * 2**20
F32 = jnp.float32
BF16 = jnp.bfloat16
NT = (((1,), (1,)), ((), ()))
TN = (((0,), (0,)), ((), ()))


def dot(a, b, dims=(((1,), (0,)), ((), ()))):
    return lax.dot_general(a, b, dims, preferred_element_type=F32)


def params():
    return pltpu.CompilerParams(vmem_limit_bytes=VMEM)


def rotary_select(heads):
    out = np.zeros((heads * HEAD, heads * LANES), np.float32)
    for h in range(heads):
        for i in range(HALF):
            out[h * HEAD + i, h * LANES + i] = 1
            out[h * HEAD + HALF + i, h * LANES + 64 + i] = 1
    return out


def plain_select(heads):
    out = np.zeros((heads * HEAD, heads * LANES), np.float32)
    for h in range(heads):
        for i in range(HEAD):
            out[h * HEAD + i, h * LANES + i] = 1
    return out


def rotary_tables(positions):
    halves = jnp.arange(HALF, dtype=F32)
    inverse = ROTARY_BASE ** (-2.0 * halves / HEAD)
    angles = positions.astype(F32)[:, None] * inverse
    cosine, sine = jnp.cos(angles), jnp.sin(angles)
    gap = jnp.zeros((positions.shape[0], 16), F32)
    return (
        jnp.concatenate([cosine, gap, cosine, gap], axis=1),
        jnp.concatenate([-sine, gap, sine, gap], axis=1),
    )


def turn(values, cosine, sine):
    return values * cosine + pltpu.roll(values, 64, 1) * sine


def qkv_kernel(tok_ref, gain_ref, w_ref, cos_ref, sin_ref, n_ref, q_ref, k_ref, v_ref):
    resid = tok_ref[...].astype(F32)
    scaling = lax.rsqrt(jnp.mean(resid * resid, axis=1, keepdims=True) + EPSILON)
    normed = (resid * scaling * gain_ref[...].astype(F32)).astype(BF16)
    n_ref[...] = normed
    raw = dot(normed, w_ref[...])
    cosine, sine = cos_ref[...], sin_ref[...]
    nq, nk = q_ref.shape[1] // LANES, k_ref.shape[1] // LANES
    for h in range(nq):
        part = raw[:, h * LANES : (h + 1) * LANES]
        q_ref[:, h * LANES : (h + 1) * LANES] = turn(part, cosine, sine).astype(BF16)
    for h in range(nk):
        part = raw[:, (nq + h) * LANES : (nq + h + 1) * LANES]
        k_ref[:, h * LANES : (h + 1) * LANES] = turn(part, cosine, sine).astype(BF16)
    v_ref[...] = raw[:, (nq + nk) * LANES :].astype(BF16)


def qkv(tokens, gain, weights, cosine, sine, nq, nk):
    rows, width = tokens.shape
    block = lambda n: pl.BlockSpec((256, n), lambda i: (i, 0))
    whole = lambda a: pl.BlockSpec(a.shape, lambda i: (0, 0))
    sizes = (width, nq * LANES, nk * LANES, nk * LANES)
    return pl.pallas_call(
        qkv_kernel,
        grid=(rows // 256,),
        in_specs=[block(width), whole(gain), whole(weights), block(LANES), block(LANES)],
        out_specs=[block(n) for n in sizes],
        out_shape=[jax.ShapeDtypeStruct((rows, n), BF16) for n in sizes],
        compiler_params=params(),
        cost_estimate=pl.CostEstimate(
            flops=2 * rows * width * weights.shape[1], bytes_accessed=12 * 2**20, transcendentals=0
        ),
    )(tokens, gain, weights, cosine, sine)


def allowed(segc, segr, i, kn):
    same = segc == segr[:, :kn]
    rows = lax.broadcasted_iota(jnp.int32, (QBLOCK, kn), 0) + i * QBLOCK
    cols = lax.broadcasted_iota(jnp.int32, (QBLOCK, kn), 1)
    return same & (cols <= rows)


def attn_fwd_kernel(nq, nk, q_ref, k_ref, v_ref, segc_ref, segr_ref, sel_ref, o_ref, lse_ref):
    grouped = nq // nk

    def body(i):
        kn = (i + 1) * QBLOCK
        mask = allowed(segc_ref[...], segr_ref[...], i, kn)
        outs = []
        for h in range(nq):
            g = h // grouped
            lanes = slice(g * LANES, (g + 1) * LANES)
            raw = dot(q_ref[:, h * LANES : (h + 1) * LANES], k_ref[:kn, lanes], NT)
            raw = jnp.where(mask, raw, MASKED)
            top = jnp.max(raw, axis=1, keepdims=True)
            e = jnp.exp2((raw - top) * (SCALE * LOG2E))
            total = jnp.sum(e, axis=1, keepdims=True)
            p = (e * (1.0 / total)).astype(BF16)
            outs.append(dot(p, v_ref[:kn, lanes]).astype(BF16))
            lse_ref[:, h : h + 1] = top * (SCALE * LOG2E) + jnp.log2(total)
        o_ref[...] = dot(jnp.concatenate(outs, axis=1), sel_ref[...], NT).astype(BF16)

    for i in range(LEN // QBLOCK):
        pl.when(pl.program_id(0) == i)(functools.partial(body, i))


def attn_fwd(q, k, v, segc, segr, sel, nq, nk):
    block = lambda n: pl.BlockSpec((QBLOCK, n), lambda i: (i, 0))
    whole = lambda a: pl.BlockSpec(a.shape, lambda i: (0, 0))
    return pl.pallas_call(
        functools.partial(attn_fwd_kernel, nq, nk),
        grid=(LEN // QBLOCK,),
        in_specs=[block(nq * LANES), whole(k), whole(v), block(1), whole(segr), whole(sel)],
        out_specs=[block(nq * HEAD), block(8)],
        out_shape=[
            jax.ShapeDtypeStruct((LEN, nq * HEAD), BF16),
            jax.ShapeDtypeStruct((LEN, 8), F32),
        ],
        compiler_params=params(),
        cost_estimate=pl.CostEstimate(
            flops=4 * nq * LEN * LEN * LANES, bytes_accessed=6 * 2**20, transcendentals=nq * LEN * LEN
        ),
    )(q, k, v, segc, segr, sel)


def attn_bwd_kernel(
    nq, nk, q_ref, k_ref, v_ref, segc_ref, segr_ref, lse_ref, o_ref, do_ref, cos_ref, sin_ref,
    cosa_ref, sina_ref, selv_ref, selr_ref, g_ref, dk_ref, dv_ref,
):
    grouped = nq // nk
    wide = nq * HEAD

    @pl.when(pl.program_id(0) == 0)
    def _():
        dk_ref[...] = jnp.zeros_like(dk_ref)
        dv_ref[...] = jnp.zeros_like(dv_ref)

    def body(i):
        kn = (i + 1) * QBLOCK
        mask = allowed(segc_ref[...], segr_ref[...], i, kn)
        do_all = dot(do_ref[...], selv_ref[...]).astype(BF16)
        prod = do_ref[...].astype(F32) * o_ref[...].astype(F32)
        turned = []
        for h in range(nq):
            g = h // grouped
            lanes = slice(g * LANES, (g + 1) * LANES)
            q = q_ref[:, h * LANES : (h + 1) * LANES]
            grad = do_all[:, h * LANES : (h + 1) * LANES]
            raw = dot(q, k_ref[:kn, lanes], NT)
            p = jnp.exp2(raw * (SCALE * LOG2E) - lse_ref[:, h : h + 1])
            p = jnp.where(mask, p, 0.0)
            dp = dot(grad, v_ref[:kn, lanes], NT)
            delta = jnp.sum(p * dp, axis=1, keepdims=True)
            ds = (p * (dp - delta) * SCALE).astype(BF16)
            dq = dot(ds, k_ref[:kn, lanes])
            turned.append(turn(dq, cos_ref[...], -sin_ref[...]).astype(BF16))
            dk_ref[:kn, lanes] += dot(ds, q, TN)
            dv_ref[:kn, lanes] += dot(p.astype(BF16), grad, TN)
        rows = slice(i * QBLOCK, (i + 1) * QBLOCK)
        g_ref[rows, :wide] = dot(jnp.concatenate(turned, axis=1), selr_ref[...], NT).astype(BF16)

    blocks = LEN // QBLOCK
    for i in range(blocks):
        pl.when(pl.program_id(0) == i)(functools.partial(body, i))

    @pl.when(pl.program_id(0) == blocks - 1)
    def _():
        turned = []
        for g in range(nk):
            lanes = slice(g * LANES, (g + 1) * LANES)
            turned.append(turn(dk_ref[:, lanes], cosa_ref[...], -sina_ref[...]).astype(BF16))
        kw = nk * HEAD
        gk = dot(jnp.concatenate(turned, axis=1), selr_ref[:kw, : nk * LANES], NT)
        gv = dot(dv_ref[...].astype(BF16), selv_ref[:kw, : nk * LANES], NT)
        both = jnp.concatenate([gk, gv], axis=1).astype(BF16)
        g_ref[:, wide:] = both


def attn_bwd(q, k, v, segc, segr, lse, o, do, cosine, sine, selv, selr, nq, nk):
    block = lambda n: pl.BlockSpec((QBLOCK, n), lambda i: (i, 0))
    whole = lambda a: pl.BlockSpec(a.shape, lambda i: (0, 0))
    total = (nq + 2 * nk) * HEAD
    return pl.pallas_call(
        functools.partial(attn_bwd_kernel, nq, nk),
        grid=(LEN // QBLOCK,),
        in_specs=[
            block(nq * LANES), whole(k), whole(v), block(1), whole(segr), block(8), block(nq * HEAD),
            block(nq * HEAD), block(LANES), block(LANES), whole(cosine), whole(sine), whole(selv), whole(selr),
        ],
        out_specs=pl.BlockSpec((LEN, total), lambda i: (0, 0)),
        out_shape=jax.ShapeDtypeStruct((LEN, total), BF16),
        scratch_shapes=[pltpu.VMEM((LEN, nk * LANES), F32), pltpu.VMEM((LEN, nk * LANES), F32)],
        compiler_params=params(),
        cost_estimate=pl.CostEstimate(
            flops=10 * nq * LEN * LEN * LANES, bytes_accessed=8 * 2**20, transcendentals=nq * LEN * LEN
        ),
    )(q, k, v, segc, segr, lse, o, do, cosine, sine, cosine, sine, selv, selr)


def outproj_kernel(me_ref, att_ref, w_ref, tok_ref, gain_ref, n_ref, hid_ref):
    hidden = tok_ref[...].astype(F32)
    wide = att_ref.shape[2]
    for z in range(att_ref.shape[0]):
        hidden = hidden + dot(att_ref[z], w_ref[:, z * wide : (z + 1) * wide], NT)
    scaling = lax.rsqrt(jnp.mean(hidden * hidden, axis=1, keepdims=True) + EPSILON)
    n_ref[...] = (hidden * scaling * gain_ref[...].astype(F32)).astype(BF16)
    hid_ref[...] = hidden


def outproj(me, att, weights, tokens, gain):
    parts, rows, wide = att.shape
    width = tokens.shape[1]
    piece = rows // parts
    at = lambda i, me: lax.rem(me[0] + 1 + i, parts)
    whole = lambda a: pl.BlockSpec(a.shape, lambda i, me: (0,) * a.ndim)
    return pl.pallas_call(
        outproj_kernel,
        grid_spec=pltpu.PrefetchScalarGridSpec(
            num_scalar_prefetch=1,
            grid=(parts,),
            in_specs=[
                pl.BlockSpec((parts, piece, wide), lambda i, me: (0, at(i, me), 0)),
                pl.BlockSpec((width, parts * wide), lambda i, me: (0, 0)),
                pl.BlockSpec((piece, width), lambda i, me: (at(i, me), 0)),
                whole(gain),
            ],
            out_specs=[
                pl.BlockSpec((piece, width), lambda i, me: (at(i, me), 0)),
                pl.BlockSpec((piece, width), lambda i, me: (0, 0)),
            ],
        ),
        out_shape=[
            jax.ShapeDtypeStruct((rows, width), BF16),
            jax.ShapeDtypeStruct((piece, width), F32),
        ],
        compiler_params=params(),
        cost_estimate=pl.CostEstimate(
            flops=2 * rows * width * width, bytes_accessed=16 * 2**20, transcendentals=0
        ),
    )(me, att, weights, tokens, gain)


def mlp_kernel(n_ref, cot_ref, wg_ref, wu_ref, wd_ref, out_ref, gn_ref, sum_ref):
    gate = dot(n_ref[...], wg_ref[...])
    upward = dot(n_ref[...], wu_ref[...])
    g_act = dot(cot_ref[...], wd_ref[...])
    sigma = jax.nn.sigmoid(gate)
    silu = gate * sigma
    out_ref[2] = (silu * upward).astype(BF16)
    g_gate = (g_act * upward * sigma * (1.0 + gate * (1.0 - sigma))).astype(BF16)
    g_up = (g_act * silu).astype(BF16)
    out_ref[0] = g_gate
    out_ref[1] = g_up
    part = dot(g_gate, wg_ref[...], NT) + dot(g_up, wu_ref[...], NT)

    @pl.when(pl.program_id(0) == 0)
    def _():
        sum_ref[...] = part

    @pl.when(pl.program_id(0) > 0)
    def _():
        sum_ref[...] += part

    @pl.when(pl.program_id(0) == pl.num_programs(0) - 1)
    def _():
        gn_ref[...] = sum_ref[...].astype(BF16)


def mlp(normed, cot, weights):
    rows, width = normed.shape
    units = weights.shape[1] // 3
    chunk = 256
    steps = units // chunk
    whole = pl.BlockSpec((rows, width), lambda j: (0, 0))
    column = lambda k: pl.BlockSpec((width, chunk), lambda j: (0, k * steps + j))
    return pl.pallas_call(
        mlp_kernel,
        grid=(steps,),
        in_specs=[whole, whole, column(0), column(1), column(2)],
        out_specs=[pl.BlockSpec((3, rows, chunk), lambda j: (0, 0, j)), whole],
        out_shape=[
            jax.ShapeDtypeStruct((3, rows, units), BF16),
            jax.ShapeDtypeStruct((rows, width), BF16),
        ],
        scratch_shapes=[pltpu.VMEM((rows, width), F32)],
        compiler_params=params(),
        cost_estimate=pl.CostEstimate(
            flops=10 * rows * width * units, bytes_accessed=30 * 2**20, transcendentals=rows * units
        ),
    )(normed, cot, weights, weights, weights)


def wgrad_kernel(uses, core_ref, *refs):
    keep_ref, send_ref = refs[-2:]
    rights = refs[-2 - len(uses) : -2]
    half = keep_ref.shape[1]
    at = 0
    for left, right in zip(uses, rights):
        pieces = [right[...]] if len(right.shape) == 2 else [right[k] for k in range(right.shape[0])]
        for piece in pieces:
            block = dot(refs[left][...], piece, TN).astype(BF16)
            columns = slice(at, at + piece.shape[1])

            @pl.when(core_ref[0] == 0)
            def _():
                keep_ref[0, :, columns] = block[:half]
                send_ref[0, :, columns] = block[half:]

            @pl.when(core_ref[0] == 1)
            def _():
                keep_ref[0, :, columns] = block[half:]
                send_ref[0, :, columns] = block[:half]

            at += piece.shape[1]


def wgrad(core, lefts, uses, rights, dp):
    rows, width = lefts[0].shape
    shard = width // dp
    columns = sum(r.shape[-1] * (r.shape[0] if r.ndim == 3 else 1) for r in rights)
    pairs = dp // 2
    out = jax.ShapeDtypeStruct((pairs, shard, columns), BF16)
    out_spec = pl.BlockSpec((1, shard, columns), lambda i, core: (i, 0, 0))
    return pl.pallas_call(
        functools.partial(wgrad_kernel, uses),
        grid_spec=pltpu.PrefetchScalarGridSpec(
            num_scalar_prefetch=1,
            grid=(pairs,),
            in_specs=[pl.BlockSpec((rows, 2 * shard), lambda i, core: (0, i)) for _ in lefts]
            + [pl.BlockSpec(r.shape, lambda i, core, d=r.ndim: (0,) * d) for r in rights],
            out_specs=[out_spec, out_spec],
        ),
        out_shape=[out, out],
        compiler_params=params(),
        cost_estimate=pl.CostEstimate(
            flops=2 * rows * width * columns, bytes_accessed=20 * 2**20, transcendentals=0
        ),
    )(core, *lefts, *rights)


def tie(value, *others):
    return lax.optimization_barrier((value, *others))[0]


def swap(value, axis, size, bit):
    return lax.ppermute(value, axis, [(k, k ^ bit) for k in range(size)])


def place(buffer, value, index, axis):
    return lax.dynamic_update_slice_in_dim(buffer, value, index, axis)


class Rows:
    def __init__(self, size):
        self.size = size
        self.index = lax.axis_index("dp")
        self.grid = size == 8
        self.core = lax.rem(self.index, 2)
        self.x = lax.rem(self.index // 2, 2)
        self.y = self.index // 4

    def gather(self, shard, after=()):
        if after:
            shard = tie(shard, *after)
        if not self.grid:
            return lax.all_gather(shard, "dp", axis=0, tiled=True), shard
        rows, columns = shard.shape
        half = rows // 2
        by_x, by_y = swap(shard, "dp", 8, 2), swap(shard, "dp", 8, 4)
        far_top, far_low = swap(by_x[:half], "dp", 8, 4), swap(by_y[half:], "dp", 8, 2)
        x, y = self.x, self.y
        mine = jnp.zeros((4 * rows, columns), shard.dtype)
        mine = place(mine, shard, (2 * y + x) * rows, 0)
        mine = place(mine, by_x, (2 * y + 1 - x) * rows, 0)
        mine = place(mine, by_y, (2 - 2 * y + x) * rows, 0)
        far = (3 - 2 * y - x) * rows
        mine = place(mine, far_top, far, 0)
        mine = place(mine, far_low, far + half, 0)
        other = swap(mine, "dp", 8, 1)
        full = jnp.zeros((4, 2, rows, columns), shard.dtype)
        full = place(full, mine.reshape(4, 1, rows, columns), self.core, 1)
        full = place(full, other.reshape(4, 1, rows, columns), 1 - self.core, 1)
        return full.reshape(8 * rows, columns), by_x

    def scatter(self, lefts, uses, rights):
        if not self.grid:
            parts = []
            for use, right in zip(uses, rights):
                for piece in [right] if right.ndim == 2 else list(right):
                    parts.append(dot(lefts[use], piece, TN).astype(BF16))
            whole = jnp.concatenate(parts, axis=1)
            return lax.psum_scatter(whole, "dp", scatter_dimension=0, tiled=True).astype(F32)
        keep, send = wgrad(self.core.astype(jnp.int32).reshape(1), lefts, uses, rights, 8)
        got = swap(send, "dp", 8, 1)
        both = (keep.astype(F32) + got.astype(F32)).astype(BF16)
        rows, columns = both.shape[1:]
        both = both.reshape(2, 2, rows, columns)
        pick = lambda a, i, axis: lax.dynamic_index_in_dim(a, i, axis, keepdims=False)
        left, right = both[..., : columns // 2], both[..., columns // 2 :]
        x, y = self.x, self.y
        got_left = swap(pick(left, 1 - x, 1), "dp", 8, 2)
        got_right = swap(pick(right, 1 - y, 0), "dp", 8, 4)
        left = (pick(left, x, 1).astype(F32) + got_left.astype(F32)).astype(BF16)
        right = (pick(right, y, 0).astype(F32) + got_right.astype(F32)).astype(BF16)
        got_left = swap(pick(left, 1 - y, 0), "dp", 8, 4)
        got_right = swap(pick(right, 1 - x, 0), "dp", 8, 2)
        left = pick(left, y, 0).astype(F32) + got_left.astype(F32)
        right = pick(right, x, 0).astype(F32) + got_right.astype(F32)
        return jnp.concatenate([left, right], axis=1)


def on_device(
    dp,
    tensor,
    tokens,
    segments,
    positions,
    gain_attn,
    w_query,
    w_key,
    w_value,
    w_out,
    gain_mlp,
    w_gate,
    w_up,
    w_down,
    cotangent,
):
    piece, width = tokens.shape[1:]
    nq, nk = w_query.shape[1] // HEAD, w_key.shape[1] // HEAD
    qw, kw = nq * HEAD, nk * HEAD
    shard = w_query.shape[0]
    rows = Rows(dp)
    z = lax.axis_index("tensor")
    tokens, cotangent = tokens[0], cotangent[0]

    def exchange(block_for):
        return {d: swap(block_for(d), "tensor", tensor, d) for d in reversed(range(1, tensor))}

    def gather_z(value, axis):
        sizes = list(value.shape)
        sizes[axis] *= tensor
        got = exchange(lambda d: value)
        full = place(jnp.zeros(sizes, value.dtype), value, z * value.shape[axis], axis)
        for d, block in got.items():
            full = place(full, block, (z ^ d) * value.shape[axis], axis)
        return full

    def sum_z(partial):
        return lax.psum_scatter(partial, "tensor", scatter_dimension=0, tiled=True).astype(F32)

    all_tokens = lax.all_gather(tokens, "tensor", axis=0, tiled=True)

    gains = jnp.pad(jnp.stack([gain_attn, gain_mlp], axis=1), ((0, 0), (0, LANES - 2)))
    out_shard = gather_z(w_out.T, 1)
    attn_shard = jnp.concatenate([out_shard, w_query, w_key, w_value, gains], axis=1)
    attn_full, arrived = rows.gather(attn_shard)
    mlp_shard = jnp.concatenate([w_gate, w_up, w_down.T], axis=1)
    mlp_full, _ = rows.gather(mlp_shard, (arrived,))
    w_qkv = attn_full[:, width : width + qw + 2 * kw]
    gain_rows = attn_full[:, width + qw + 2 * kw : width + qw + 2 * kw + 2].T
    gain_first, gain_second = gain_rows[:1], gain_rows[1:]

    select = np.zeros((qw + 2 * kw, (nq + 2 * nk) * LANES), np.float32)
    select[:qw, : nq * LANES] = rotary_select(nq)
    select[qw : qw + kw, nq * LANES : (nq + nk) * LANES] = rotary_select(nk)
    select[qw + kw :, (nq + nk) * LANES :] = plain_select(nk)
    w_spread = dot(w_qkv, jnp.asarray(select, BF16)).astype(BF16)
    sel_plain, sel_turn = jnp.asarray(plain_select(nq), BF16), jnp.asarray(rotary_select(nq), BF16)
    cosine, sine = rotary_tables(positions[0])
    segc, segr = segments[0][:, None], segments

    normed, q, k, v = qkv(all_tokens, gain_first, w_spread, cosine, sine, nq, nk)
    cot_own = tie(cotangent, all_tokens)
    cot_all = gather_z(cot_own, 0)
    att, lse = attn_fwd(q, k, v, segc, segr, sel_plain, nq, nk)
    att_all = lax.all_gather(att, "tensor", axis=0, tiled=False)
    me = z.astype(jnp.int32).reshape(1)
    normed_mlp, hidden = outproj(me, att_all, attn_full, all_tokens, gain_second)

    units, g_nmlp = mlp(normed_mlp, cot_all, mlp_full)
    g_nmlp = sum_z(g_nmlp)
    grads_mlp = rows.scatter([normed_mlp, cot_all], [0, 1], [units[:2], units[2]])
    ff = w_gate.shape[1]
    mixed_part = dot(units[2], mlp_full[:, 2 * ff :], NT).astype(BF16)
    mixed = (hidden + sum_z(mixed_part)).astype(BF16)

    def norm_back(incoming, values, gain):
        scaling = lax.rsqrt(jnp.mean(values * values, axis=1, keepdims=True) + EPSILON)
        unit = values * scaling
        tilted = incoming * gain.astype(F32)
        return scaling * (tilted - unit * jnp.mean(tilted * unit, axis=1, keepdims=True))

    g_hidden = cotangent.astype(F32) + norm_back(g_nmlp, hidden, gain_second)
    g_branch = g_hidden.astype(BF16)
    g_att = dot(g_branch, attn_full[:, :width]).astype(BF16).reshape(piece, tensor, qw)

    block = lambda d: lax.dynamic_index_in_dim(g_att, z ^ d, 1, keepdims=False)
    got = exchange(block)
    g_heads = place(jnp.zeros((LEN, qw), BF16), block(0), z * piece, 0)
    for d, value in got.items():
        g_heads = place(g_heads, value, (z ^ d) * piece, 0)
    g_qkv = attn_bwd(q, k, v, segc, segr, lse, att, g_heads, cosine, sine, sel_plain, sel_turn, nq, nk)
    g_nattn = sum_z(dot(g_qkv, w_qkv, NT).astype(BF16))
    att_own = lax.dynamic_slice_in_dim(att_all, z * piece, piece, 1)
    grads_out = rows.scatter([g_branch], [0], [att_own])
    grads_attn = rows.scatter([normed], [0], [g_qkv])
    g_tokens = g_hidden + norm_back(g_nattn, tokens.astype(F32), gain_first)

    out_block = lambda d: lax.dynamic_slice_in_dim(grads_out, (z ^ d) * qw, qw, 1)
    grad_out = out_block(0)
    for value in exchange(lambda d: out_block(d).astype(BF16)).values():
        grad_out = grad_out + value.astype(F32)

    def gain_part(weights, grads, gain):
        total = sum(jnp.sum(w.astype(F32) * g, axis=1) for w, g in zip(weights, grads))
        return total / gain.astype(F32)

    g_query, g_key, g_value = grads_attn[:, :qw], grads_attn[:, qw : qw + kw], grads_attn[:, qw + kw :]
    g_gate, g_up, g_down = grads_mlp[:, :ff], grads_mlp[:, ff : 2 * ff], grads_mlp[:, 2 * ff :]
    both = jnp.stack(
        [
            gain_part((w_query, w_key, w_value), (g_query, g_key, g_value), gain_attn),
            gain_part((w_gate, w_up), (g_gate, g_up), gain_mlp),
        ]
    )
    step = 1
    while step < tensor:
        both = both + swap(both, "tensor", tensor, step)
        step *= 2
    return (
        mixed[None],
        g_tokens.astype(BF16)[None],
        both[0],
        g_query,
        g_key,
        g_value,
        grad_out.T,
        both[1],
        g_gate,
        g_up,
        g_down.T,
    )


def solution(mesh):
    split, whole_rows = P("dp", "tensor", None), P("dp", None)
    by_row, by_column, gain = P("dp", "tensor"), P("tensor", "dp"), P("dp")
    weights = (by_row, by_row, by_row, by_column, gain, by_row, by_row, by_column)
    step = functools.partial(on_device, mesh.shape["dp"], mesh.shape["tensor"])
    return jax.shard_map(
        step,
        mesh=mesh,
        in_specs=(split, whole_rows, whole_rows, gain, *weights, split),
        out_specs=(split, split, gain, *weights),
        check_vma=False,
    )
```

```python
import functools
import jax
import jax.numpy as jnp
import numpy as np
from jax import lax
from jax.experimental import pallas as pl
from jax.experimental.pallas import tpu as pltpu
from jax.sharding import PartitionSpec as P

HEADS = 16
KV_HEADS = 8
HEAD = 96
HALF = 48
LANES = 128
LEN = 1024
QBLOCK = 256
EPSILON = 1e-05
ROTARY_BASE = 100000.0
MASKED = -1e30
SCALE = HEAD ** (-0.5)
LOG2E = 1.4426950408889634
VMEM = 56 * 2**20
F32 = jnp.float32
BF16 = jnp.bfloat16
NT = (((1,), (1,)), ((), ()))
TN = (((0,), (0,)), ((), ()))


def dot(a, b, dims=(((1,), (0,)), ((), ()))):
    return lax.dot_general(a, b, dims, preferred_element_type=F32)


def params():
    return pltpu.CompilerParams(vmem_limit_bytes=VMEM)


def rotary_select(heads):
    out = np.zeros((heads * HEAD, heads * LANES), np.float32)
    for h in range(heads):
        for i in range(HALF):
            out[h * HEAD + i, h * LANES + i] = 1
            out[h * HEAD + HALF + i, h * LANES + 64 + i] = 1
    return out


def plain_select(heads):
    out = np.zeros((heads * HEAD, heads * LANES), np.float32)
    for h in range(heads):
        for i in range(HEAD):
            out[h * HEAD + i, h * LANES + i] = 1
    return out


def rotary_tables(positions):
    halves = jnp.arange(HALF, dtype=F32)
    inverse = ROTARY_BASE ** (-2.0 * halves / HEAD)
    angles = positions.astype(F32)[:, None] * inverse
    cosine, sine = jnp.cos(angles), jnp.sin(angles)
    gap = jnp.zeros((positions.shape[0], 16), F32)
    return (
        jnp.concatenate([cosine, gap, cosine, gap], axis=1),
        jnp.concatenate([-sine, gap, sine, gap], axis=1),
    )


def turn(values, cosine, sine):
    return values * cosine + pltpu.roll(values, 64, 1) * sine


def qkv_kernel(tok_ref, gain_ref, w_ref, cos_ref, sin_ref, n_ref, q_ref, k_ref, v_ref):
    resid = tok_ref[...].astype(F32)
    scaling = lax.rsqrt(jnp.mean(resid * resid, axis=1, keepdims=True) + EPSILON)
    normed = (resid * scaling * gain_ref[...].astype(F32)).astype(BF16)
    n_ref[...] = normed
    raw = dot(normed, w_ref[...])
    cosine, sine = cos_ref[...], sin_ref[...]
    nq, nk = q_ref.shape[1] // LANES, k_ref.shape[1] // LANES
    for h in range(nq):
        part = raw[:, h * LANES : (h + 1) * LANES]
        q_ref[:, h * LANES : (h + 1) * LANES] = turn(part, cosine, sine).astype(BF16)
    for h in range(nk):
        part = raw[:, (nq + h) * LANES : (nq + h + 1) * LANES]
        k_ref[:, h * LANES : (h + 1) * LANES] = turn(part, cosine, sine).astype(BF16)
    v_ref[...] = raw[:, (nq + nk) * LANES :].astype(BF16)


def qkv(tokens, gain, weights, cosine, sine, nq, nk):
    rows, width = tokens.shape
    block = lambda n: pl.BlockSpec((256, n), lambda i: (i, 0))
    whole = lambda a: pl.BlockSpec(a.shape, lambda i: (0, 0))
    sizes = (width, nq * LANES, nk * LANES, nk * LANES)
    return pl.pallas_call(
        qkv_kernel,
        grid=(rows // 256,),
        in_specs=[
            block(width),
            whole(gain),
            pl.BlockSpec((width, (nq + 2 * nk) * LANES), lambda i: (0, 0)),
            block(LANES),
            block(LANES),
        ],
        out_specs=[block(n) for n in sizes],
        out_shape=[jax.ShapeDtypeStruct((rows, n), BF16) for n in sizes],
        compiler_params=params(),
        cost_estimate=pl.CostEstimate(
            flops=2 * rows * width * weights.shape[1], bytes_accessed=12 * 2**20, transcendentals=0
        ),
    )(tokens, gain, weights, cosine, sine)


def allowed(segc, segr, i, kn):
    same = segc == segr[:, :kn]
    rows = lax.broadcasted_iota(jnp.int32, (QBLOCK, kn), 0) + i * QBLOCK
    cols = lax.broadcasted_iota(jnp.int32, (QBLOCK, kn), 1)
    return same & (cols <= rows)


def attn_fwd_kernel(nq, nk, q_ref, k_ref, v_ref, segc_ref, segr_ref, sel_ref, o_ref, lse_ref):
    grouped = nq // nk

    def body(i):
        kn = (i + 1) * QBLOCK
        mask = allowed(segc_ref[...], segr_ref[...], i, kn)
        outs = []
        for h in range(nq):
            g = h // grouped
            lanes = slice(g * LANES, (g + 1) * LANES)
            raw = dot(q_ref[:, h * LANES : (h + 1) * LANES], k_ref[:kn, lanes], NT)
            raw = jnp.where(mask, raw, MASKED)
            top = jnp.max(raw, axis=1, keepdims=True)
            e = jnp.exp2((raw - top) * (SCALE * LOG2E))
            total = jnp.sum(e, axis=1, keepdims=True)
            p = (e * (1.0 / total)).astype(BF16)
            outs.append(dot(p, v_ref[:kn, lanes]).astype(BF16))
            lse_ref[:, h : h + 1] = top * (SCALE * LOG2E) + jnp.log2(total)
        o_ref[...] = dot(jnp.concatenate(outs, axis=1), sel_ref[...], NT).astype(BF16)

    for i in range(LEN // QBLOCK):
        pl.when(pl.program_id(0) == i)(functools.partial(body, i))


def attn_fwd(q, k, v, segc, segr, sel, nq, nk):
    block = lambda n: pl.BlockSpec((QBLOCK, n), lambda i: (i, 0))
    whole = lambda a: pl.BlockSpec(a.shape, lambda i: (0, 0))
    return pl.pallas_call(
        functools.partial(attn_fwd_kernel, nq, nk),
        grid=(LEN // QBLOCK,),
        in_specs=[block(nq * LANES), whole(k), whole(v), block(1), whole(segr), whole(sel)],
        out_specs=[block(nq * HEAD), block(8)],
        out_shape=[
            jax.ShapeDtypeStruct((LEN, nq * HEAD), BF16),
            jax.ShapeDtypeStruct((LEN, 8), F32),
        ],
        compiler_params=params(),
        cost_estimate=pl.CostEstimate(
            flops=4 * nq * LEN * LEN * LANES, bytes_accessed=6 * 2**20, transcendentals=nq * LEN * LEN
        ),
    )(q, k, v, segc, segr, sel)


def attn_bwd_kernel(
    nq, nk, at_ref, q_ref, k_ref, v_ref, segc_ref, segr_ref, lse_ref, do_ref, cos_ref, sin_ref,
    cosa_ref, sina_ref, selv_ref, selr_ref, g_ref, dk_ref, dv_ref,
):
    grouped = nq // nk
    wide = nq * HEAD

    @pl.when(pl.program_id(0) == 0)
    def _():
        dk_ref[...] = jnp.zeros_like(dk_ref)
        dv_ref[...] = jnp.zeros_like(dv_ref)

    def body(i):
        kn = (i + 1) * QBLOCK
        mask = allowed(segc_ref[...], segr_ref[...], i, kn)
        do_all = dot(do_ref[0], selv_ref[...]).astype(BF16)
        turned = []
        for h in range(nq):
            g = h // grouped
            lanes = slice(g * LANES, (g + 1) * LANES)
            q = q_ref[:, h * LANES : (h + 1) * LANES]
            grad = do_all[:, h * LANES : (h + 1) * LANES]
            raw = dot(q, k_ref[:kn, lanes], NT)
            p = jnp.exp2(raw * (SCALE * LOG2E) - lse_ref[:, h : h + 1])
            p = jnp.where(mask, p, 0.0)
            dp = dot(grad, v_ref[:kn, lanes], NT)
            delta = jnp.sum(p * dp, axis=1, keepdims=True)
            ds = (p * (dp - delta) * SCALE).astype(BF16)
            dq = dot(ds, k_ref[:kn, lanes])
            turned.append(turn(dq, cos_ref[...], -sin_ref[...]).astype(BF16))
            dk_ref[:kn, lanes] += dot(ds, q, TN)
            dv_ref[:kn, lanes] += dot(p.astype(BF16), grad, TN)
        rows = slice(i * QBLOCK, (i + 1) * QBLOCK)
        g_ref[rows, :wide] = dot(jnp.concatenate(turned, axis=1), selr_ref[...], NT).astype(BF16)

    blocks = LEN // QBLOCK
    for i in range(blocks):
        pl.when(pl.program_id(0) == i)(functools.partial(body, i))

    @pl.when(pl.program_id(0) == blocks - 1)
    def _():
        turned = []
        for g in range(nk):
            lanes = slice(g * LANES, (g + 1) * LANES)
            turned.append(turn(dk_ref[:, lanes], cosa_ref[...], -sina_ref[...]).astype(BF16))
        kw = nk * HEAD
        gk = dot(jnp.concatenate(turned, axis=1), selr_ref[:kw, : nk * LANES], NT)
        gv = dot(dv_ref[...].astype(BF16), selv_ref[:kw, : nk * LANES], NT)
        both = jnp.concatenate([gk, gv], axis=1).astype(BF16)
        g_ref[:, wide:] = both


def attn_bwd(at, q, k, v, segc, segr, lse, do, cosine, sine, selv, selr, nq, nk):
    block = lambda n: pl.BlockSpec((QBLOCK, n), lambda i, at: (i, 0))
    whole = lambda a: pl.BlockSpec(a.shape, lambda i, at: (0, 0))
    total = (nq + 2 * nk) * HEAD
    return pl.pallas_call(
        functools.partial(attn_bwd_kernel, nq, nk),
        grid_spec=pltpu.PrefetchScalarGridSpec(
            num_scalar_prefetch=1,
            grid=(LEN // QBLOCK,),
            in_specs=[
                block(nq * LANES), whole(k), whole(v), block(1), whole(segr), block(8),
                pl.BlockSpec((1, QBLOCK, nq * HEAD), lambda i, at: (at[i], 0, 0)),
                block(LANES), block(LANES), whole(cosine), whole(sine), whole(selv), whole(selr),
            ],
            out_specs=pl.BlockSpec((LEN, total), lambda i, at: (0, 0)),
            scratch_shapes=[pltpu.VMEM((LEN, nk * LANES), F32), pltpu.VMEM((LEN, nk * LANES), F32)],
        ),
        out_shape=jax.ShapeDtypeStruct((LEN, total), BF16),
        compiler_params=params(),
        cost_estimate=pl.CostEstimate(
            flops=10 * nq * LEN * LEN * LANES, bytes_accessed=8 * 2**20, transcendentals=nq * LEN * LEN
        ),
    )(at, q, k, v, segc, segr, lse, do, cosine, sine, cosine, sine, selv, selr)


def cost(flops, megabytes):
    return pl.CostEstimate(flops=flops, bytes_accessed=megabytes * 2**20, transcendentals=0)


def outproj_kernel(me_ref, att_ref, w_ref, tok_ref, gain_ref, n_ref, hid_ref):
    hidden = tok_ref[...].astype(F32)
    wide = att_ref.shape[2]
    for z in range(att_ref.shape[0]):
        hidden = hidden + dot(att_ref[z], w_ref[:, z * wide : (z + 1) * wide], NT)
    scaling = lax.rsqrt(jnp.mean(hidden * hidden, axis=1, keepdims=True) + EPSILON)
    n_ref[...] = (hidden * scaling * gain_ref[...].astype(F32)).astype(BF16)
    hid_ref[...] = hidden


def outproj(me, att, weights, tokens, gain):
    parts, rows, wide = att.shape
    width = tokens.shape[1]
    piece = rows // parts
    at = lambda i, me: lax.rem(me[0] + 1 + i, parts)
    return pl.pallas_call(
        outproj_kernel,
        grid_spec=pltpu.PrefetchScalarGridSpec(
            num_scalar_prefetch=1,
            grid=(parts,),
            in_specs=[
                pl.BlockSpec((parts, piece, wide), lambda i, me: (0, at(i, me), 0)),
                pl.BlockSpec((width, parts * wide), lambda i, me: (0, 0)),
                pl.BlockSpec((piece, width), lambda i, me: (at(i, me), 0)),
                pl.BlockSpec(gain.shape, lambda i, me: (0, 0)),
            ],
            out_specs=[
                pl.BlockSpec((piece, width), lambda i, me: (at(i, me), 0)),
                pl.BlockSpec((piece, width), lambda i, me: (0, 0)),
            ],
        ),
        out_shape=[jax.ShapeDtypeStruct((rows, width), BF16), jax.ShapeDtypeStruct((piece, width), F32)],
        compiler_params=params(),
        cost_estimate=cost(2 * rows * width * width, 16),
    )(me, att, weights, tokens, gain)


def mlp_kernel(n_ref, cot_ref, wg_ref, wu_ref, wd_ref, out_ref, gn_ref, sum_ref):
    step = pl.program_id(0)
    rows, width = sum_ref.shape
    normed = n_ref[...].reshape(rows, width)
    gate = dot(normed, wg_ref[...])
    upward = dot(normed, wu_ref[...])
    g_act = dot(cot_ref[...].reshape(rows, width), wd_ref[...])
    sigma = jax.nn.sigmoid(gate)
    silu = gate * sigma
    out_ref[2] = (silu * upward).astype(BF16)
    g_gate = (g_act * upward * (sigma + silu * (1.0 - sigma))).astype(BF16)
    g_up = (g_act * silu).astype(BF16)
    out_ref[0] = g_gate
    out_ref[1] = g_up
    part = dot(g_gate, wg_ref[...], NT) + dot(g_up, wu_ref[...], NT)

    @pl.when(step == 0)
    def _():
        sum_ref[...] = part

    @pl.when(step > 0)
    def _():
        sum_ref[...] += part

    @pl.when(step == pl.num_programs(0) - 1)
    def _():
        gn_ref[...] = sum_ref[...].astype(BF16)


def mlp(normed, cot, weights, half):
    parts, piece, width = normed.shape
    rows = parts * piece // 2
    units = weights.shape[1] // 3
    chunk = 512
    steps = units // chunk
    some = pl.BlockSpec((parts, piece // 2, width), lambda j: (0, half, 0))
    column = lambda k: pl.BlockSpec((width, chunk), lambda j: (0, k * steps + j))
    return pl.pallas_call(
        mlp_kernel,
        grid=(steps,),
        in_specs=[some, pl.BlockSpec(cot.shape, lambda j: (0, 0, 0)), column(0), column(1), column(2)],
        out_specs=[
            pl.BlockSpec((3, rows, chunk), lambda j: (0, 0, j)),
            pl.BlockSpec((rows, width), lambda j: (0, 0)),
        ],
        out_shape=[
            jax.ShapeDtypeStruct((3, rows, units), BF16),
            jax.ShapeDtypeStruct((rows, width), BF16),
        ],
        scratch_shapes=[pltpu.VMEM((rows, width), F32)],
        compiler_params=params(),
        cost_estimate=cost(10 * rows * width * units, 24),
    )(normed, cot, weights, weights, weights)


def down_kernel(low_ref, high_ref, w_ref, out_ref):
    @pl.when(pl.program_id(0) == 0)
    def _():
        out_ref[...] = dot(low_ref[0], w_ref[...], NT).astype(BF16).reshape(out_ref.shape)

    @pl.when(pl.program_id(0) == 1)
    def _():
        out_ref[...] = dot(high_ref[0], w_ref[...], NT).astype(BF16).reshape(out_ref.shape)


def down(low, high, weights, parts):
    rows, units = low.shape[1:]
    width = weights.shape[0]
    piece = 2 * rows // parts
    return pl.pallas_call(
        down_kernel,
        grid=(2,),
        in_specs=[
            pl.BlockSpec((1, rows, units), lambda h: (2, 0, 0)),
            pl.BlockSpec((1, rows, units), lambda h: (2, 0, 0)),
            pl.BlockSpec((width, units), lambda h: (0, 2)),
        ],
        out_specs=pl.BlockSpec((parts, piece // 2, width), lambda h: (0, h, 0)),
        out_shape=jax.ShapeDtypeStruct((parts, piece, width), BF16),
        compiler_params=params(),
        cost_estimate=cost(4 * rows * width * units, 12),
    )(low, high, weights)


def norm_back(incoming, values, gain):
    scaling = lax.rsqrt(jnp.mean(values * values, axis=1, keepdims=True) + EPSILON)
    unit = values * scaling
    tilted = incoming * gain
    return scaling * (tilted - unit * jnp.mean(tilted * unit, axis=1, keepdims=True))


def branch_kernel(at_ref, low_ref, high_ref, hid_ref, cot_ref, gain_ref, w_ref, gh_ref, gb_ref, ga_ref):
    @pl.when(pl.program_id(0) == 0)
    def _():
        incoming = jnp.concatenate([low_ref[...], high_ref[...]], axis=0).astype(F32)
        back = norm_back(incoming, hid_ref[...], gain_ref[...].astype(F32))
        g_hidden = cot_ref[...].astype(F32) + back
        gh_ref[...] = g_hidden
        gb_ref[...] = g_hidden.astype(BF16)

    ga_ref[0] = dot(gb_ref[...], w_ref[...]).astype(BF16)


def branch(at, low, high, hidden, cot, gain, weights, parts):
    rows, width = hidden.shape
    wide = weights.shape[1] // parts
    whole = pl.BlockSpec((rows, width), lambda i, at: (0, 0))
    half = pl.BlockSpec((rows // 2, width), lambda i, at: (0, 0))
    return pl.pallas_call(
        branch_kernel,
        grid_spec=pltpu.PrefetchScalarGridSpec(
            num_scalar_prefetch=1,
            grid=(parts,),
            in_specs=[
                half,
                half,
                whole,
                whole,
                pl.BlockSpec(gain.shape, lambda i, at: (0, 0)),
                pl.BlockSpec((width, wide), lambda i, at: (0, at[i])),
            ],
            out_specs=[whole, whole, pl.BlockSpec((1, rows, wide), lambda i, at: (i, 0, 0))],
        ),
        out_shape=[
            jax.ShapeDtypeStruct((rows, width), F32),
            jax.ShapeDtypeStruct((rows, width), BF16),
            jax.ShapeDtypeStruct((parts, rows, wide), BF16),
        ],
        compiler_params=params(),
        cost_estimate=cost(2 * rows * width * parts * wide, 10),
    )(at, low, high, hidden, cot, gain, weights)


def wgrad_kernel(uses, count, core_ref, *refs):
    keep_ref, send_ref = refs[-2:]
    lefts, rights = refs[:count], refs[count:-2]
    half = keep_ref.shape[1]
    at = 0
    for terms in uses:
        total = None
        for left, part, parts, right, k in terms:
            rows = lefts[left].shape[1] // parts
            a = lefts[left][:, part * rows : (part + 1) * rows].reshape(-1, lefts[left].shape[2])
            b = rights[right][...] if k is None else rights[right][k]
            product = dot(a, b, TN)
            total = product if total is None else total + product
        block = total.astype(BF16)
        columns = slice(at, at + block.shape[1])

        @pl.when(core_ref[0] == 0)
        def _():
            keep_ref[0, :, columns] = block[:half]
            send_ref[0, :, columns] = block[half:]

        @pl.when(core_ref[0] == 1)
        def _():
            keep_ref[0, :, columns] = block[half:]
            send_ref[0, :, columns] = block[:half]

        at += block.shape[1]


def wgrad(core, lefts, uses, rights, dp):
    pieces, rows, width = lefts[0].shape
    shard = width // dp
    columns = sum(rights[terms[0][3]].shape[-1] for terms in uses)
    pairs = dp // 2
    out = jax.ShapeDtypeStruct((pairs, shard, columns), BF16)
    out_spec = pl.BlockSpec((1, shard, columns), lambda i, core: (i, 0, 0))
    return pl.pallas_call(
        functools.partial(wgrad_kernel, uses, len(lefts)),
        grid_spec=pltpu.PrefetchScalarGridSpec(
            num_scalar_prefetch=1,
            grid=(pairs,),
            in_specs=[pl.BlockSpec((*a.shape[:2], 2 * shard), lambda i, core: (0, 0, i)) for a in lefts]
            + [pl.BlockSpec(r.shape, lambda i, core, d=r.ndim: (0,) * d) for r in rights],
            out_specs=[out_spec, out_spec],
        ),
        out_shape=[out, out],
        compiler_params=params(),
        cost_estimate=cost(2 * pieces * rows * width * columns, 16),
    )(core, *lefts, *rights)


def assemble_kernel(at_ref, *refs):
    pieces, out_ref = refs[:-1], refs[-1]
    for i, piece in enumerate(pieces):
        rows = piece.shape[0]
        out_ref[pl.ds(pl.multiple_of(at_ref[i], rows), rows)] = piece[...]


def assemble(starts, pieces):
    rows, columns = sum(p.shape[0] for p in pieces), pieces[0].shape[1]
    chunk = max(c for c in range(128, 769, 128) if columns % c == 0)
    block = lambda n: pl.BlockSpec((n, chunk), lambda j, at: (0, j))
    return pl.pallas_call(
        assemble_kernel,
        grid_spec=pltpu.PrefetchScalarGridSpec(
            num_scalar_prefetch=1,
            grid=(columns // chunk,),
            in_specs=[block(p.shape[0]) for p in pieces],
            out_specs=block(rows),
        ),
        out_shape=jax.ShapeDtypeStruct((rows, columns), pieces[0].dtype),
        compiler_params=params(),
        cost_estimate=pl.CostEstimate(flops=0, bytes_accessed=4 * rows * columns, transcendentals=0),
    )(jnp.stack(starts).astype(jnp.int32), *pieces)


def blend_kernel(core_ref, mine_ref, other_ref, out_ref):
    half = mine_ref.shape[0]

    @pl.when(core_ref[0] == 0)
    def _():
        out_ref[:half] = mine_ref[...]
        out_ref[half:] = other_ref[...]

    @pl.when(core_ref[0] == 1)
    def _():
        out_ref[:half] = other_ref[...]
        out_ref[half:] = mine_ref[...]


def blend(core, mine, other, chips):
    rows, columns = mine.shape
    shard = rows // chips
    block = pl.BlockSpec((shard, columns), lambda i, core: (i, 0))
    return pl.pallas_call(
        blend_kernel,
        grid_spec=pltpu.PrefetchScalarGridSpec(
            num_scalar_prefetch=1,
            grid=(chips,),
            in_specs=[block, block],
            out_specs=pl.BlockSpec((2 * shard, columns), lambda i, core: (i, 0)),
        ),
        out_shape=jax.ShapeDtypeStruct((2 * rows, columns), mine.dtype),
        compiler_params=params(),
        cost_estimate=pl.CostEstimate(flops=0, bytes_accessed=8 * rows * columns, transcendentals=0),
    )(core, mine, other)


def swap(value, axis, size, bit):
    return lax.ppermute(value, axis, [(k, k ^ bit) for k in range(size)])


class Phases(dict):
    def step(self, **more):
        self.update(more)
        names = [name for name in self if self[name] is not None]
        self.update(zip(names, lax.optimization_barrier([self[name] for name in names])))

    def drop(self, *names):
        for name in names:
            del self[name]


class Gather:
    def __init__(self, place, v, name):
        self.place, self.v, self.names = place, v, [name + str(i) for i in range(12)]

    def get(self, first, last):
        return [self.v[name] for name in self.names[first:last]]

    def put(self, first, values):
        self.v.update(zip(self.names[first:], values))

    def shard(self, value):
        self.put(0, [value])

    def near(self):
        if not self.place.grid:
            return []
        (value,) = self.get(0, 1)
        return [swap(value, "dp", 8, 2), swap(value, "dp", 8, 4)]

    def halves(self):
        if not self.place.grid:
            return []
        by_x, by_y = self.get(1, 3)
        half = by_x.shape[0] // 2
        return [by_x[:half], by_y[half:]]

    def far(self):
        if not self.place.grid:
            return []
        top, low = self.get(10, 12)
        self.v.drop(*self.names[10:12])
        return [swap(top, "dp", 8, 4), swap(low, "dp", 8, 2)]

    def stack(self):
        if not self.place.grid:
            return []
        pieces = self.get(0, 5)
        rows = pieces[0].shape[0]
        x, y = self.place.x, self.place.y
        chips = [2 * y + x, 2 * y + 1 - x, 2 - 2 * y + x, 3 - 2 * y - x, 3 - 2 * y - x]
        below = [0, 0, 0, 0, rows // 2]
        self.v.drop(*self.names[1:5])
        return [assemble([chip * rows + low for chip, low in zip(chips, below)], pieces)]

    def cores(self):
        return [swap(self.get(5, 6)[0], "dp", 8, 1)] if self.place.grid else []

    def each(self, first, last):
        return [swap(value, "dp", 8, 1) for value in self.get(first, last)] if self.place.grid else []

    def whole_of_pieces(self):
        if not self.place.grid:
            return lax.all_gather(self.get(0, 1)[0], "dp", axis=0, tiled=True)
        pieces = self.get(0, 10)
        rows = pieces[0].shape[0]
        x, y, core = self.place.x, self.place.y, self.place.core
        chips = [2 * y + x, 2 * y + 1 - x, 2 - 2 * y + x, 3 - 2 * y - x, 3 - 2 * y - x]
        below = [0, 0, 0, 0, rows // 2]
        starts = [(2 * chip + core) * rows + low for chip, low in zip(chips, below)]
        starts += [(2 * chip + 1 - core) * rows + low for chip, low in zip(chips, below)]
        self.v.drop(*self.names)
        return assemble(starts, pieces)

    def whole(self):
        if not self.place.grid:
            return lax.all_gather(self.get(0, 1)[0], "dp", axis=0, tiled=True)
        mine, other = self.get(5, 7)
        self.v.drop(*self.names[5:7])
        return blend(self.place.core.astype(jnp.int32).reshape(1), mine, other, 4)


class Scatter:
    def __init__(self, place, v, name):
        self.place, self.v, self.names = place, v, [name + str(i) for i in range(4)]

    def get(self, count):
        return [self.v[name] for name in self.names[:count]]

    def put(self, first, values):
        self.v.update(zip(self.names[first:], values))

    def product(self, lefts, uses, rights):
        if self.place.grid:
            core = self.place.core.astype(jnp.int32).reshape(1)
            self.put(0, wgrad(core, lefts, uses, rights, 8))
            return
        groups = []
        for terms in uses:
            total = 0.0
            for left, part, parts, right, k in terms:
                rows = lefts[left].shape[1] // parts
                a = lefts[left][:, part * rows : (part + 1) * rows].reshape(-1, lefts[left].shape[2])
                total = total + dot(a, rights[right] if k is None else rights[right][k], TN)
            groups.append(total.astype(BF16))
        self.put(0, [jnp.concatenate(groups, axis=1)])

    def cores(self):
        if self.place.grid:
            self.put(1, [swap(self.get(2)[1], "dp", 8, 1)])

    def add(self):
        if not self.place.grid:
            return
        keep, got = self.get(2)
        both = (keep.astype(F32) + got.astype(F32)).astype(BF16)
        rows, columns = both.shape[1:]
        both = both.reshape(2, 2, rows, columns)
        left, right = both[..., : columns // 2], both[..., columns // 2 :]
        x, y = self.place.x, self.place.y
        self.put(0, [pick(left, x, 1), pick(right, y, 0), pick(left, 1 - x, 1), pick(right, 1 - y, 0)])

    def near(self):
        if not self.place.grid:
            return []
        _, _, left, right = self.get(4)
        return [swap(left, "dp", 8, 2), swap(right, "dp", 8, 4)]

    def add_near(self):
        if not self.place.grid:
            return
        left, right, got_left, got_right = self.get(4)
        left = (left.astype(F32) + got_left.astype(F32)).astype(BF16)
        right = (right.astype(F32) + got_right.astype(F32)).astype(BF16)
        x, y = self.place.x, self.place.y
        self.put(0, [pick(left, y, 0), pick(right, x, 0), pick(left, 1 - y, 0), pick(right, 1 - x, 0)])

    def far(self):
        if not self.place.grid:
            return []
        _, _, left, right = self.get(4)
        return [swap(left, "dp", 8, 4), swap(right, "dp", 8, 2)]

    def total(self):
        if not self.place.grid:
            whole = self.get(1)[0]
            return lax.psum_scatter(whole, "dp", scatter_dimension=0, tiled=True).astype(F32)
        left, right, got_left, got_right = (value.astype(F32) for value in self.get(4))
        self.v.drop(*self.names)
        return jnp.concatenate([left + got_left, right + got_right], axis=1)


def pick(value, index, axis):
    return lax.dynamic_index_in_dim(value, index, axis, keepdims=False)


class Place:
    def __init__(self, size):
        index = lax.axis_index("dp")
        self.grid = size == 8
        self.core = lax.rem(index, 2)
        self.x = lax.rem(index // 2, 2)
        self.y = index // 4


def on_device(
    dp,
    tensor,
    tokens,
    segments,
    positions,
    gain_attn,
    w_query,
    w_key,
    w_value,
    w_out,
    gain_mlp,
    w_gate,
    w_up,
    w_down,
    cotangent,
):
    piece, width = tokens.shape[1:]
    nq, nk = w_query.shape[1] // HEAD, w_key.shape[1] // HEAD
    qw, kw = nq * HEAD, nk * HEAD
    wide = qw + 2 * kw
    ff = w_gate.shape[1]
    place = Place(dp)
    z = lax.axis_index("tensor")
    at = jnp.arange(tensor, dtype=jnp.int32) ^ z.astype(jnp.int32)
    across = lambda value, bit: swap(value, "tensor", tensor, bit)

    def exchange(block_for):
        got = {d: across(block_for(d), d) for d in reversed(range(1, tensor))}
        return [block_for(0)] + [got[d] for d in range(1, tensor)]

    def piece_of(value, d):
        return lax.dynamic_slice_in_dim(value, (z ^ d) * piece, piece, 0)

    select = np.zeros((wide, (nq + 2 * nk) * LANES), np.float32)
    select[:qw, : nq * LANES] = rotary_select(nq)
    select[qw : qw + kw, nq * LANES : (nq + nk) * LANES] = rotary_select(nk)
    select[qw + kw :, (nq + nk) * LANES :] = plain_select(nk)
    select = jnp.asarray(select, BF16)
    sel_plain, sel_turn = jnp.asarray(plain_select(nq), BF16), jnp.asarray(rotary_select(nq), BF16)

    v = Phases()
    heads = Gather(place, v, "heads")
    back = Gather(place, v, "back")
    own = Gather(place, v, "own")
    d_own = Scatter(place, v, "d_own")
    d_out = Scatter(place, v, "d_out")
    d_attn = Scatter(place, v, "d_attn")

    all_tokens = lax.all_gather(tokens[0], "tensor", axis=0, tiled=True)
    gains = jnp.pad(jnp.stack([gain_attn, gain_mlp], axis=1), ((0, 0), (0, LANES - 2)))
    w_heads = jnp.concatenate([w_query, w_key, w_value], axis=1)
    spread = dot(w_heads, select).astype(BF16)
    heads.shard(jnp.concatenate([spread, gains], axis=1))
    heads.put(1, heads.near())
    out_turned = w_out.T
    out_blocks = exchange(lambda d: out_turned)
    mlp_shard = jnp.concatenate([w_gate, w_up, w_down.T], axis=1)
    own.shard(mlp_shard)
    v.step(tokens=tokens[0], cot=cotangent[0], at=at)

    heads.put(10, heads.halves())
    heads.put(3, heads.far())
    cosine, sine = rotary_tables(positions[0])
    v.step(
        cosine=cosine, sine=sine, segc=segments[0][:, None], segr=segments, **{"out%d" % d: out_blocks[d] for d in range(tensor)}
    )

    half = piece // 2
    cot_low = lax.all_gather(v["cot"][:half], "tensor", axis=0, tiled=False)
    own.put(1, own.near())
    heads.put(5, heads.stack())
    heads.put(6, heads.cores())
    w_spread = heads.whole()
    shard = jnp.zeros((out_turned.shape[0], width), BF16)
    for d in range(tensor):
        shard = lax.dynamic_update_slice_in_dim(shard, v.pop("out%d" % d), (z ^ d) * qw, 1)
    back.shard(shard)
    v.step(w_spread=w_spread)

    back.put(1, back.near())
    own.put(10, own.halves())
    v.step()
    back.put(10, back.halves())
    picked = dot(jnp.eye(8, LANES, dtype=BF16), v["w_spread"][:, spread.shape[1] :], NT).astype(BF16)
    v.step(all_tokens=all_tokens, gain_first=picked[:1], gain_second=picked[1:2])

    own.put(3, own.far())
    back.put(3, back.far())
    normed, q, k, val = qkv(v["all_tokens"], v["gain_first"], v["w_spread"], v["cosine"], v["sine"], nq, nk)
    att, lse = attn_fwd(q, k, val, v["segc"], v["segr"], sel_plain, nq, nk)
    v.step(normed=normed, q=q, k=k, v=val, att=att, lse=lse, cot_low=cot_low)

    att_all = lax.all_gather(v["att"], "tensor", axis=0, tiled=False)
    back.put(5, back.stack())
    back.put(6, back.cores())
    own.put(5, own.stack())
    own.put(6, own.cores())
    w_back = back.whole()
    w_own = own.whole()
    v.step(att_all=att_all, w_back=w_back, w_own=w_own)

    cot_high = lax.all_gather(v["cot"][half:], "tensor", axis=0, tiled=False)
    me = z.astype(jnp.int32).reshape(1)
    normed_mlp, hidden = outproj(me, v["att_all"], v["w_back"], v["all_tokens"], v["gain_second"])
    v.step(normed_mlp=normed_mlp.reshape(tensor, piece, width), hidden=hidden)

    units_low, g_low = mlp(v["normed_mlp"], v["cot_low"], v["w_own"], 0)
    v.step(units_low=units_low, g_low=g_low, cot_high=cot_high)
    got_low = lax.psum_scatter(v["g_low"], "tensor", scatter_dimension=0, tiled=True)
    units_high, g_high = mlp(v["normed_mlp"], v["cot_high"], v["w_own"], 1)
    v.step(units_high=units_high, g_high=g_high)

    got_high = lax.psum_scatter(v["g_high"], "tensor", scatter_dimension=0, tiled=True)
    lefts, rights = [v["normed_mlp"], v["cot_low"], v["cot_high"]], [v["units_low"], v["units_high"]]
    gate_up = [[(0, h, 2, h, k) for h in range(2)] for k in range(2)]
    d_own.product(lefts, gate_up + [[(1 + h, 0, 1, h, 2) for h in range(2)]], rights)
    w_compact = dot(v["w_spread"][:, : spread.shape[1]], select, NT).astype(BF16)
    v.step(got_low=got_low, w_compact=w_compact)
    d_own.cores()
    mixed_part = down(v["units_low"], v["units_high"], v["w_own"], tensor)
    v.step(mixed_part=mixed_part)
    d_own.add()
    v.step(got_high=got_high)

    mixed_got = lax.psum_scatter(v["mixed_part"].reshape(LEN, width), "tensor", scatter_dimension=0, tiled=True)
    near = d_own.near()
    g_hidden, g_branch, g_att = branch(
        v["at"], v["got_low"], v["got_high"], v["hidden"], v["cot"], v["gain_second"], v["w_back"], tensor
    )
    v.step(g_hidden=g_hidden, g_branch=g_branch, g_att=g_att)

    blocks = exchange(lambda d: v["g_att"][d])
    att_own = lax.dynamic_slice_in_dim(v["att_all"], z * piece, piece, 1)
    d_out.product([v["g_branch"][None]], [[(0, 0, 1, 0, k)] for k in range(tensor)], [att_own])
    d_own.put(2, near)
    v.step(g_heads=jnp.stack(blocks))
    d_own.add_near()
    v.step()

    d_out.cores()
    d_own.put(2, d_own.far())
    g_qkv = attn_bwd(
        v["at"], v["q"], v["k"], v["v"], v["segc"], v["segr"], v["lse"], v["g_heads"], v["cosine"], v["sine"],
        sel_plain, sel_turn, nq, nk,
    )
    g_nattn = dot(g_qkv, v["w_compact"], NT).astype(BF16)
    v.step(g_qkv=g_qkv, g_nattn=g_nattn)

    g_nattn = lax.psum_scatter(v["g_nattn"], "tensor", scatter_dimension=0, tiled=True)
    d_out.add()
    v.step()
    d_out.put(2, d_out.near())
    d_attn.product([v["normed"][None]], [[(0, 0, 1, 0, None)]], [v["g_qkv"]])
    grads_own = d_own.total()
    v.step(grads_own=grads_own)

    def gain_part(weights, grads, gain):
        total = sum(jnp.sum(w.astype(F32) * g, axis=1) for w, g in zip(weights, grads))
        return total / gain.astype(F32)

    d_attn.cores()
    d_out.add_near()
    v.step()
    d_out.put(2, d_out.far())
    d_attn.add()
    g_gate, g_up, g_down = (v["grads_own"][:, i * ff : (i + 1) * ff] for i in range(3))
    mlp_gain = gain_part((w_gate, w_up), (g_gate, g_up), gain_mlp)
    v.step(mlp_gain=mlp_gain)
    d_attn.put(2, d_attn.near())
    grads_out = d_out.total()
    v.step(grads_out=grads_out)
    d_attn.add_near()
    out_block = lambda d: lax.dynamic_slice_in_dim(v["grads_out"], (z ^ d) * qw, qw, 1)
    out_blocks = exchange(lambda d: out_block(d).astype(F32 if d == 0 else BF16))
    mixed = (v["hidden"] + mixed_got.astype(F32)).astype(BF16)
    v.step(mixed=mixed)
    d_attn.put(2, d_attn.far())
    v.step(grad_out=sum(block.astype(F32) for block in out_blocks), g_nattn=g_nattn)

    grads_attn = d_attn.total()
    g_query, g_key, g_value = grads_attn[:, :qw], grads_attn[:, qw : qw + kw], grads_attn[:, qw + kw :]
    both = jnp.stack([gain_part((w_query, w_key, w_value), (g_query, g_key, g_value), gain_attn), v["mlp_gain"]])
    tokens, gain_first = v["tokens"].astype(F32), v["gain_first"].astype(F32)
    g_tokens = (v["g_hidden"] + norm_back(v["g_nattn"].astype(F32), tokens, gain_first)).astype(BF16)
    step = 1
    while step < tensor:
        both = both + across(both, step)
        step *= 2
    return (
        v["mixed"][None],
        g_tokens[None],
        both[0],
        g_query,
        g_key,
        g_value,
        v["grad_out"].T,
        both[1],
        g_gate,
        g_up,
        g_down.T,
    )


def solution(mesh):
    split, whole_rows = P("dp", "tensor", None), P("dp", None)
    by_row, by_column, gain = P("dp", "tensor"), P("tensor", "dp"), P("dp")
    weights = (by_row, by_row, by_row, by_column, gain, by_row, by_row, by_column)
    step = functools.partial(on_device, mesh.shape["dp"], mesh.shape["tensor"])
    return jax.shard_map(
        step,
        mesh=mesh,
        in_specs=(split, whole_rows, whole_rows, gain, *weights, split),
        out_specs=(split, split, gain, *weights),
        check_vma=False,
    )
```

```python
import functools
import jax
import jax.numpy as jnp
import numpy as np
from jax import lax
from jax.experimental import pallas as pl
from jax.experimental.pallas import tpu as pltpu
from jax.sharding import PartitionSpec as P

HEADS = 16
KV_HEADS = 8
HEAD = 96
HALF = 48
LANES = 128
LEN = 1024
QBLOCK = 256
EPSILON = 1e-05
ROTARY_BASE = 100000.0
MASKED = -1e30
SCALE = HEAD ** (-0.5)
LOG2E = 1.4426950408889634
VMEM = 56 * 2**20
F32 = jnp.float32
BF16 = jnp.bfloat16
NT = (((1,), (1,)), ((), ()))
TN = (((0,), (0,)), ((), ()))


def dot(a, b, dims=(((1,), (0,)), ((), ()))):
    return lax.dot_general(a, b, dims, preferred_element_type=F32)


def params():
    return pltpu.CompilerParams(vmem_limit_bytes=VMEM)


def rotary_select(heads):
    out = np.zeros((heads * HEAD, heads * LANES), np.float32)
    for h in range(heads):
        for i in range(HALF):
            out[h * HEAD + i, h * LANES + i] = 1
            out[h * HEAD + HALF + i, h * LANES + 64 + i] = 1
    return out


def plain_select(heads):
    out = np.zeros((heads * HEAD, heads * LANES), np.float32)
    for h in range(heads):
        for i in range(HEAD):
            out[h * HEAD + i, h * LANES + i] = 1
    return out


def rotary_tables(positions):
    halves = jnp.arange(HALF, dtype=F32)
    inverse = ROTARY_BASE ** (-2.0 * halves / HEAD)
    angles = positions.astype(F32)[:, None] * inverse
    cosine, sine = jnp.cos(angles), jnp.sin(angles)
    gap = jnp.zeros((positions.shape[0], 16), F32)
    return (
        jnp.concatenate([cosine, gap, cosine, gap], axis=1),
        jnp.concatenate([-sine, gap, sine, gap], axis=1),
    )


def turn(values, cosine, sine):
    return values * cosine + pltpu.roll(values, 64, 1) * sine


def qkv_kernel(tok_ref, gain_ref, w_ref, cos_ref, sin_ref, n_ref, q_ref, k_ref, v_ref):
    resid = tok_ref[...].astype(F32)
    scaling = lax.rsqrt(jnp.mean(resid * resid, axis=1, keepdims=True) + EPSILON)
    normed = (resid * scaling * gain_ref[...].astype(F32)).astype(BF16)
    n_ref[...] = normed
    raw = dot(normed, w_ref[...])
    cosine, sine = cos_ref[...], sin_ref[...]
    nq, nk = q_ref.shape[1] // LANES, k_ref.shape[1] // LANES
    for h in range(nq):
        part = raw[:, h * LANES : (h + 1) * LANES]
        q_ref[:, h * LANES : (h + 1) * LANES] = turn(part, cosine, sine).astype(BF16)
    for h in range(nk):
        part = raw[:, (nq + h) * LANES : (nq + h + 1) * LANES]
        k_ref[:, h * LANES : (h + 1) * LANES] = turn(part, cosine, sine).astype(BF16)
    v_ref[...] = raw[:, (nq + nk) * LANES :].astype(BF16)


def qkv(tokens, gain, weights, cosine, sine, nq, nk):
    rows, width = tokens.shape
    block = lambda n: pl.BlockSpec((256, n), lambda i: (i, 0))
    whole = lambda a: pl.BlockSpec(a.shape, lambda i: (0, 0))
    sizes = (width, nq * LANES, nk * LANES, nk * LANES)
    return pl.pallas_call(
        qkv_kernel,
        grid=(rows // 256,),
        in_specs=[
            block(width),
            whole(gain),
            pl.BlockSpec((width, (nq + 2 * nk) * LANES), lambda i: (0, 0)),
            block(LANES),
            block(LANES),
        ],
        out_specs=[block(n) for n in sizes],
        out_shape=[jax.ShapeDtypeStruct((rows, n), BF16) for n in sizes],
        compiler_params=params(),
        cost_estimate=pl.CostEstimate(
            flops=2 * rows * width * weights.shape[1], bytes_accessed=12 * 2**20, transcendentals=0
        ),
    )(tokens, gain, weights, cosine, sine)


def allowed(segc, segr, i, kn):
    same = segc == segr[:, :kn]
    rows = lax.broadcasted_iota(jnp.int32, (QBLOCK, kn), 0) + i * QBLOCK
    cols = lax.broadcasted_iota(jnp.int32, (QBLOCK, kn), 1)
    return same & (cols <= rows)


def attn_fwd_kernel(nq, nk, q_ref, k_ref, v_ref, segc_ref, segr_ref, sel_ref, o_ref, lse_ref):
    grouped = nq // nk

    def body(i):
        kn = (i + 1) * QBLOCK
        mask = allowed(segc_ref[...], segr_ref[...], i, kn)
        outs = []
        for h in range(nq):
            g = h // grouped
            lanes = slice(g * LANES, (g + 1) * LANES)
            raw = dot(q_ref[:, h * LANES : (h + 1) * LANES], k_ref[:kn, lanes], NT)
            raw = jnp.where(mask, raw, MASKED)
            top = jnp.max(raw, axis=1, keepdims=True)
            e = jnp.exp2((raw - top) * (SCALE * LOG2E))
            total = jnp.sum(e, axis=1, keepdims=True)
            p = (e * (1.0 / total)).astype(BF16)
            outs.append(dot(p, v_ref[:kn, lanes]).astype(BF16))
            lse_ref[:, h : h + 1] = top * (SCALE * LOG2E) + jnp.log2(total)
        o_ref[...] = dot(jnp.concatenate(outs, axis=1), sel_ref[...], NT).astype(BF16)

    for i in range(LEN // QBLOCK):
        pl.when(pl.program_id(0) == i)(functools.partial(body, i))


def attn_fwd(q, k, v, segc, segr, sel, nq, nk):
    block = lambda n: pl.BlockSpec((QBLOCK, n), lambda i: (i, 0))
    whole = lambda a: pl.BlockSpec(a.shape, lambda i: (0, 0))
    return pl.pallas_call(
        functools.partial(attn_fwd_kernel, nq, nk),
        grid=(LEN // QBLOCK,),
        in_specs=[block(nq * LANES), whole(k), whole(v), block(1), whole(segr), whole(sel)],
        out_specs=[block(nq * HEAD), block(8)],
        out_shape=[
            jax.ShapeDtypeStruct((LEN, nq * HEAD), BF16),
            jax.ShapeDtypeStruct((LEN, 8), F32),
        ],
        compiler_params=params(),
        cost_estimate=pl.CostEstimate(
            flops=4 * nq * LEN * LEN * LANES, bytes_accessed=6 * 2**20, transcendentals=nq * LEN * LEN
        ),
    )(q, k, v, segc, segr, sel)


def attn_bwd_kernel(
    nq, nk, at_ref, q_ref, k_ref, v_ref, segc_ref, segr_ref, lse_ref, do_ref, cos_ref, sin_ref,
    cosa_ref, sina_ref, selv_ref, selr_ref, g_ref, dk_ref, dv_ref,
):
    grouped = nq // nk
    wide = nq * HEAD

    @pl.when(pl.program_id(0) == 0)
    def _():
        dk_ref[...] = jnp.zeros_like(dk_ref)
        dv_ref[...] = jnp.zeros_like(dv_ref)

    def body(i):
        kn = (i + 1) * QBLOCK
        mask = allowed(segc_ref[...], segr_ref[...], i, kn)
        do_all = dot(do_ref[0], selv_ref[...]).astype(BF16)
        turned = []
        for h in range(nq):
            g = h // grouped
            lanes = slice(g * LANES, (g + 1) * LANES)
            q = q_ref[:, h * LANES : (h + 1) * LANES]
            grad = do_all[:, h * LANES : (h + 1) * LANES]
            raw = dot(q, k_ref[:kn, lanes], NT)
            p = jnp.exp2(raw * (SCALE * LOG2E) - lse_ref[:, h : h + 1])
            p = jnp.where(mask, p, 0.0)
            dp = dot(grad, v_ref[:kn, lanes], NT)
            delta = jnp.sum(p * dp, axis=1, keepdims=True)
            ds = (p * (dp - delta) * SCALE).astype(BF16)
            dq = dot(ds, k_ref[:kn, lanes])
            turned.append(turn(dq, cos_ref[...], -sin_ref[...]).astype(BF16))
            dk_ref[:kn, lanes] += dot(ds, q, TN)
            dv_ref[:kn, lanes] += dot(p.astype(BF16), grad, TN)
        rows = slice(i * QBLOCK, (i + 1) * QBLOCK)
        g_ref[rows, :wide] = dot(jnp.concatenate(turned, axis=1), selr_ref[...], NT).astype(BF16)

    blocks = LEN // QBLOCK
    for i in range(blocks):
        pl.when(pl.program_id(0) == i)(functools.partial(body, i))

    @pl.when(pl.program_id(0) == blocks - 1)
    def _():
        turned = []
        for g in range(nk):
            lanes = slice(g * LANES, (g + 1) * LANES)
            turned.append(turn(dk_ref[:, lanes], cosa_ref[...], -sina_ref[...]).astype(BF16))
        kw = nk * HEAD
        gk = dot(jnp.concatenate(turned, axis=1), selr_ref[:kw, : nk * LANES], NT)
        gv = dot(dv_ref[...].astype(BF16), selv_ref[:kw, : nk * LANES], NT)
        both = jnp.concatenate([gk, gv], axis=1).astype(BF16)
        g_ref[:, wide:] = both


def attn_bwd(at, q, k, v, segc, segr, lse, do, cosine, sine, selv, selr, nq, nk):
    block = lambda n: pl.BlockSpec((QBLOCK, n), lambda i, at: (i, 0))
    whole = lambda a: pl.BlockSpec(a.shape, lambda i, at: (0, 0))
    total = (nq + 2 * nk) * HEAD
    return pl.pallas_call(
        functools.partial(attn_bwd_kernel, nq, nk),
        grid_spec=pltpu.PrefetchScalarGridSpec(
            num_scalar_prefetch=1,
            grid=(LEN // QBLOCK,),
            in_specs=[
                block(nq * LANES), whole(k), whole(v), block(1), whole(segr), block(8),
                pl.BlockSpec((1, QBLOCK, nq * HEAD), lambda i, at: (at[i], 0, 0)),
                block(LANES), block(LANES), whole(cosine), whole(sine), whole(selv), whole(selr),
            ],
            out_specs=pl.BlockSpec((LEN, total), lambda i, at: (0, 0)),
            scratch_shapes=[pltpu.VMEM((LEN, nk * LANES), F32), pltpu.VMEM((LEN, nk * LANES), F32)],
        ),
        out_shape=jax.ShapeDtypeStruct((LEN, total), BF16),
        compiler_params=params(),
        cost_estimate=pl.CostEstimate(
            flops=10 * nq * LEN * LEN * LANES, bytes_accessed=8 * 2**20, transcendentals=nq * LEN * LEN
        ),
    )(at, q, k, v, segc, segr, lse, do, cosine, sine, cosine, sine, selv, selr)


def cost(flops, megabytes):
    return pl.CostEstimate(flops=flops, bytes_accessed=megabytes * 2**20, transcendentals=0)


def outproj_kernel(me_ref, att_ref, w_ref, tok_ref, gain_ref, n_ref, hid_ref):
    hidden = tok_ref[...].astype(F32)
    wide = att_ref.shape[2]
    for z in range(att_ref.shape[0]):
        hidden = hidden + dot(att_ref[z], w_ref[:, z * wide : (z + 1) * wide], NT)
    scaling = lax.rsqrt(jnp.mean(hidden * hidden, axis=1, keepdims=True) + EPSILON)
    n_ref[...] = (hidden * scaling * gain_ref[...].astype(F32)).astype(BF16)
    hid_ref[...] = hidden


def outproj(me, att, weights, tokens, gain):
    parts, rows, wide = att.shape
    width = tokens.shape[1]
    piece = rows // parts
    at = lambda i, me: lax.rem(me[0] + 1 + i, parts)
    return pl.pallas_call(
        outproj_kernel,
        grid_spec=pltpu.PrefetchScalarGridSpec(
            num_scalar_prefetch=1,
            grid=(parts,),
            in_specs=[
                pl.BlockSpec((parts, piece, wide), lambda i, me: (0, at(i, me), 0)),
                pl.BlockSpec((width, parts * wide), lambda i, me: (0, 0)),
                pl.BlockSpec((piece, width), lambda i, me: (at(i, me), 0)),
                pl.BlockSpec(gain.shape, lambda i, me: (0, 0)),
            ],
            out_specs=[
                pl.BlockSpec((piece, width), lambda i, me: (at(i, me), 0)),
                pl.BlockSpec((piece, width), lambda i, me: (0, 0)),
            ],
        ),
        out_shape=[jax.ShapeDtypeStruct((rows, width), BF16), jax.ShapeDtypeStruct((piece, width), F32)],
        compiler_params=params(),
        cost_estimate=cost(2 * rows * width * width, 16),
    )(me, att, weights, tokens, gain)


def mlp_kernel(n_ref, cot_ref, wg_ref, wu_ref, wd_ref, out_ref, gn_ref, sum_ref):
    step = pl.program_id(0)
    rows, width = sum_ref.shape
    normed = n_ref[...].reshape(rows, width)
    gate = dot(normed, wg_ref[...])
    upward = dot(normed, wu_ref[...])
    g_act = dot(cot_ref[...].reshape(rows, width), wd_ref[...])
    sigma = jax.nn.sigmoid(gate)
    silu = gate * sigma
    out_ref[2] = (silu * upward).astype(BF16)
    g_gate = (g_act * upward * (sigma + silu * (1.0 - sigma))).astype(BF16)
    g_up = (g_act * silu).astype(BF16)
    out_ref[0] = g_gate
    out_ref[1] = g_up
    part = dot(g_gate, wg_ref[...], NT) + dot(g_up, wu_ref[...], NT)

    @pl.when(step == 0)
    def _():
        sum_ref[...] = part

    @pl.when(step > 0)
    def _():
        sum_ref[...] += part

    @pl.when(step == pl.num_programs(0) - 1)
    def _():
        gn_ref[...] = sum_ref[...].astype(BF16)


def mlp(normed, cot, weights, half):
    parts, piece, width = normed.shape
    rows = parts * piece // 2
    units = weights.shape[1] // 3
    chunk = 512
    steps = units // chunk
    some = pl.BlockSpec((parts, piece // 2, width), lambda j: (0, half, 0))
    column = lambda k: pl.BlockSpec((width, chunk), lambda j: (0, k * steps + j))
    return pl.pallas_call(
        mlp_kernel,
        grid=(steps,),
        in_specs=[some, pl.BlockSpec(cot.shape, lambda j: (0, 0, 0)), column(0), column(1), column(2)],
        out_specs=[
            pl.BlockSpec((3, rows, chunk), lambda j: (0, 0, j)),
            pl.BlockSpec((rows, width), lambda j: (0, 0)),
        ],
        out_shape=[
            jax.ShapeDtypeStruct((3, rows, units), BF16),
            jax.ShapeDtypeStruct((rows, width), BF16),
        ],
        scratch_shapes=[pltpu.VMEM((rows, width), F32)],
        compiler_params=params(),
        cost_estimate=cost(10 * rows * width * units, 24),
    )(normed, cot, weights, weights, weights)


def down_kernel(low_ref, high_ref, w_ref, out_ref):
    @pl.when(pl.program_id(0) == 0)
    def _():
        out_ref[...] = dot(low_ref[0], w_ref[...], NT).astype(BF16).reshape(out_ref.shape)

    @pl.when(pl.program_id(0) == 1)
    def _():
        out_ref[...] = dot(high_ref[0], w_ref[...], NT).astype(BF16).reshape(out_ref.shape)


def down(low, high, weights, parts):
    rows, units = low.shape[1:]
    width = weights.shape[0]
    piece = 2 * rows // parts
    return pl.pallas_call(
        down_kernel,
        grid=(2,),
        in_specs=[
            pl.BlockSpec((1, rows, units), lambda h: (2, 0, 0)),
            pl.BlockSpec((1, rows, units), lambda h: (2, 0, 0)),
            pl.BlockSpec((width, units), lambda h: (0, 2)),
        ],
        out_specs=pl.BlockSpec((parts, piece // 2, width), lambda h: (0, h, 0)),
        out_shape=jax.ShapeDtypeStruct((parts, piece, width), BF16),
        compiler_params=params(),
        cost_estimate=cost(4 * rows * width * units, 12),
    )(low, high, weights)


def norm_back(incoming, values, gain):
    scaling = lax.rsqrt(jnp.mean(values * values, axis=1, keepdims=True) + EPSILON)
    unit = values * scaling
    tilted = incoming * gain
    return scaling * (tilted - unit * jnp.mean(tilted * unit, axis=1, keepdims=True))


def branch_kernel(at_ref, low_ref, high_ref, hid_ref, cot_ref, gain_ref, w_ref, gh_ref, gb_ref, ga_ref):
    @pl.when(pl.program_id(0) == 0)
    def _():
        incoming = jnp.concatenate([low_ref[...], high_ref[...]], axis=0).astype(F32)
        back = norm_back(incoming, hid_ref[...], gain_ref[...].astype(F32))
        g_hidden = cot_ref[...].astype(F32) + back
        gh_ref[...] = g_hidden
        gb_ref[...] = g_hidden.astype(BF16)

    ga_ref[0] = dot(gb_ref[...], w_ref[...]).astype(BF16)


def branch(at, low, high, hidden, cot, gain, weights, parts):
    rows, width = hidden.shape
    wide = weights.shape[1] // parts
    whole = pl.BlockSpec((rows, width), lambda i, at: (0, 0))
    half = pl.BlockSpec((rows // 2, width), lambda i, at: (0, 0))
    return pl.pallas_call(
        branch_kernel,
        grid_spec=pltpu.PrefetchScalarGridSpec(
            num_scalar_prefetch=1,
            grid=(parts,),
            in_specs=[
                half,
                half,
                whole,
                whole,
                pl.BlockSpec(gain.shape, lambda i, at: (0, 0)),
                pl.BlockSpec((width, wide), lambda i, at: (0, at[i])),
            ],
            out_specs=[whole, whole, pl.BlockSpec((1, rows, wide), lambda i, at: (i, 0, 0))],
        ),
        out_shape=[
            jax.ShapeDtypeStruct((rows, width), F32),
            jax.ShapeDtypeStruct((rows, width), BF16),
            jax.ShapeDtypeStruct((parts, rows, wide), BF16),
        ],
        compiler_params=params(),
        cost_estimate=cost(2 * rows * width * parts * wide, 10),
    )(at, low, high, hidden, cot, gain, weights)


def wgrad_kernel(uses, count, core_ref, *refs):
    keep_ref, send_ref = refs[-2:]
    lefts, rights = refs[:count], refs[count:-2]
    half = keep_ref.shape[1]
    at = 0
    for terms in uses:
        total = None
        for left, part, parts, right, k in terms:
            rows = lefts[left].shape[1] // parts
            a = lefts[left][:, part * rows : (part + 1) * rows].reshape(-1, lefts[left].shape[2])
            b = rights[right][...] if k is None else rights[right][k]
            product = dot(a, b, TN)
            total = product if total is None else total + product
        block = total.astype(BF16)
        columns = slice(at, at + block.shape[1])

        @pl.when(core_ref[0] == 0)
        def _():
            keep_ref[0, :, columns] = block[:half]
            send_ref[0, :, columns] = block[half:]

        @pl.when(core_ref[0] == 1)
        def _():
            keep_ref[0, :, columns] = block[half:]
            send_ref[0, :, columns] = block[:half]

        at += block.shape[1]


def wgrad(core, lefts, uses, rights, dp):
    pieces, rows, width = lefts[0].shape
    shard = width // dp
    columns = sum(rights[terms[0][3]].shape[-1] for terms in uses)
    pairs = dp // 2
    out = jax.ShapeDtypeStruct((pairs, shard, columns), BF16)
    out_spec = pl.BlockSpec((1, shard, columns), lambda i, core: (i, 0, 0))
    return pl.pallas_call(
        functools.partial(wgrad_kernel, uses, len(lefts)),
        grid_spec=pltpu.PrefetchScalarGridSpec(
            num_scalar_prefetch=1,
            grid=(pairs,),
            in_specs=[pl.BlockSpec((*a.shape[:2], 2 * shard), lambda i, core: (0, 0, i)) for a in lefts]
            + [pl.BlockSpec(r.shape, lambda i, core, d=r.ndim: (0,) * d) for r in rights],
            out_specs=[out_spec, out_spec],
        ),
        out_shape=[out, out],
        compiler_params=params(),
        cost_estimate=cost(2 * pieces * rows * width * columns, 16),
    )(core, *lefts, *rights)


def assemble_kernel(at_ref, *refs):
    pieces, out_ref = refs[:-1], refs[-1]
    for i, piece in enumerate(pieces):
        rows = piece.shape[0]
        out_ref[pl.ds(pl.multiple_of(at_ref[i], rows), rows)] = piece[...]


def assemble(starts, pieces):
    rows, columns = sum(p.shape[0] for p in pieces), pieces[0].shape[1]
    chunk = max(c for c in range(128, 769, 128) if columns % c == 0)
    block = lambda n: pl.BlockSpec((n, chunk), lambda j, at: (0, j))
    return pl.pallas_call(
        assemble_kernel,
        grid_spec=pltpu.PrefetchScalarGridSpec(
            num_scalar_prefetch=1,
            grid=(columns // chunk,),
            in_specs=[block(p.shape[0]) for p in pieces],
            out_specs=block(rows),
        ),
        out_shape=jax.ShapeDtypeStruct((rows, columns), pieces[0].dtype),
        compiler_params=params(),
        cost_estimate=pl.CostEstimate(flops=0, bytes_accessed=4 * rows * columns, transcendentals=0),
    )(jnp.stack(starts).astype(jnp.int32), *pieces)


def blend_kernel(core_ref, mine_ref, other_ref, out_ref):
    half = mine_ref.shape[0]

    @pl.when(core_ref[0] == 0)
    def _():
        out_ref[:half] = mine_ref[...]
        out_ref[half:] = other_ref[...]

    @pl.when(core_ref[0] == 1)
    def _():
        out_ref[:half] = other_ref[...]
        out_ref[half:] = mine_ref[...]


def blend(core, mine, other, chips):
    rows, columns = mine.shape
    shard = rows // chips
    block = pl.BlockSpec((shard, columns), lambda i, core: (i, 0))
    return pl.pallas_call(
        blend_kernel,
        grid_spec=pltpu.PrefetchScalarGridSpec(
            num_scalar_prefetch=1,
            grid=(chips,),
            in_specs=[block, block],
            out_specs=pl.BlockSpec((2 * shard, columns), lambda i, core: (i, 0)),
        ),
        out_shape=jax.ShapeDtypeStruct((2 * rows, columns), mine.dtype),
        compiler_params=params(),
        cost_estimate=pl.CostEstimate(flops=0, bytes_accessed=8 * rows * columns, transcendentals=0),
    )(core, mine, other)


def swap(value, axis, size, bit):
    return lax.ppermute(value, axis, [(k, k ^ bit) for k in range(size)])


class Phases(dict):
    def step(self, **more):
        self.update(more)
        names = [name for name in self if self[name] is not None]
        self.update(zip(names, lax.optimization_barrier([self[name] for name in names])))

    def drop(self, *names):
        for name in names:
            del self[name]


class Gather:
    def __init__(self, place, v, name):
        self.place, self.v, self.names = place, v, [name + str(i) for i in range(12)]

    def get(self, first, last):
        return [self.v[name] for name in self.names[first:last]]

    def put(self, first, values):
        self.v.update(zip(self.names[first:], values))

    def shard(self, value):
        self.put(0, [value])

    def near(self):
        if not self.place.grid:
            return []
        (value,) = self.get(0, 1)
        return [swap(value, "dp", 8, 2), swap(value, "dp", 8, 4)]

    def halves(self):
        if not self.place.grid:
            return []
        by_x, by_y = self.get(1, 3)
        half = by_x.shape[0] // 2
        return [by_x[:half], by_y[half:]]

    def far(self):
        if not self.place.grid:
            return []
        top, low = self.get(10, 12)
        self.v.drop(*self.names[10:12])
        return [swap(top, "dp", 8, 4), swap(low, "dp", 8, 2)]

    def stack(self):
        if not self.place.grid:
            return []
        pieces = self.get(0, 5)
        rows = pieces[0].shape[0]
        x, y = self.place.x, self.place.y
        chips = [2 * y + x, 2 * y + 1 - x, 2 - 2 * y + x, 3 - 2 * y - x, 3 - 2 * y - x]
        below = [0, 0, 0, 0, rows // 2]
        self.v.drop(*self.names[1:5])
        return [assemble([chip * rows + low for chip, low in zip(chips, below)], pieces)]

    def cores(self):
        return [swap(self.get(5, 6)[0], "dp", 8, 1)] if self.place.grid else []

    def each(self, first, last):
        return [swap(value, "dp", 8, 1) for value in self.get(first, last)] if self.place.grid else []

    def whole_of_pieces(self):
        if not self.place.grid:
            return lax.all_gather(self.get(0, 1)[0], "dp", axis=0, tiled=True)
        pieces = self.get(0, 10)
        rows = pieces[0].shape[0]
        x, y, core = self.place.x, self.place.y, self.place.core
        chips = [2 * y + x, 2 * y + 1 - x, 2 - 2 * y + x, 3 - 2 * y - x, 3 - 2 * y - x]
        below = [0, 0, 0, 0, rows // 2]
        starts = [(2 * chip + core) * rows + low for chip, low in zip(chips, below)]
        starts += [(2 * chip + 1 - core) * rows + low for chip, low in zip(chips, below)]
        self.v.drop(*self.names)
        return assemble(starts, pieces)

    def whole(self):
        if not self.place.grid:
            return lax.all_gather(self.get(0, 1)[0], "dp", axis=0, tiled=True)
        mine, other = self.get(5, 7)
        self.v.drop(*self.names[5:7])
        return blend(self.place.core.astype(jnp.int32).reshape(1), mine, other, 4)


class Scatter:
    def __init__(self, place, v, name):
        self.place, self.v, self.names = place, v, [name + str(i) for i in range(4)]

    def get(self, count):
        return [self.v[name] for name in self.names[:count]]

    def put(self, first, values):
        self.v.update(zip(self.names[first:], values))

    def product(self, lefts, uses, rights):
        if self.place.grid:
            core = self.place.core.astype(jnp.int32).reshape(1)
            self.put(0, wgrad(core, lefts, uses, rights, 8))
            return
        groups = []
        for terms in uses:
            total = 0.0
            for left, part, parts, right, k in terms:
                rows = lefts[left].shape[1] // parts
                a = lefts[left][:, part * rows : (part + 1) * rows].reshape(-1, lefts[left].shape[2])
                total = total + dot(a, rights[right] if k is None else rights[right][k], TN)
            groups.append(total.astype(BF16))
        self.put(0, [jnp.concatenate(groups, axis=1)])

    def cores(self):
        if self.place.grid:
            self.put(1, [swap(self.get(2)[1], "dp", 8, 1)])

    def add(self):
        if not self.place.grid:
            return
        keep, got = self.get(2)
        both = (keep.astype(F32) + got.astype(F32)).astype(BF16)
        rows, columns = both.shape[1:]
        both = both.reshape(2, 2, rows, columns)
        left, right = both[..., : columns // 2], both[..., columns // 2 :]
        x, y = self.place.x, self.place.y
        self.put(0, [pick(left, x, 1), pick(right, y, 0), pick(left, 1 - x, 1), pick(right, 1 - y, 0)])

    def near(self):
        if not self.place.grid:
            return []
        _, _, left, right = self.get(4)
        return [swap(left, "dp", 8, 2), swap(right, "dp", 8, 4)]

    def add_near(self):
        if not self.place.grid:
            return
        left, right, got_left, got_right = self.get(4)
        left = (left.astype(F32) + got_left.astype(F32)).astype(BF16)
        right = (right.astype(F32) + got_right.astype(F32)).astype(BF16)
        x, y = self.place.x, self.place.y
        self.put(0, [pick(left, y, 0), pick(right, x, 0), pick(left, 1 - y, 0), pick(right, 1 - x, 0)])

    def far(self):
        if not self.place.grid:
            return []
        _, _, left, right = self.get(4)
        return [swap(left, "dp", 8, 4), swap(right, "dp", 8, 2)]

    def total(self):
        if not self.place.grid:
            whole = self.get(1)[0]
            return lax.psum_scatter(whole, "dp", scatter_dimension=0, tiled=True).astype(F32)
        left, right, got_left, got_right = (value.astype(F32) for value in self.get(4))
        self.v.drop(*self.names)
        return jnp.concatenate([left + got_left, right + got_right], axis=1)


def pick(value, index, axis):
    return lax.dynamic_index_in_dim(value, index, axis, keepdims=False)


class Place:
    def __init__(self, size):
        index = lax.axis_index("dp")
        self.grid = size == 8
        self.core = lax.rem(index, 2)
        self.x = lax.rem(index // 2, 2)
        self.y = index // 4


def on_device(
    dp,
    tensor,
    tokens,
    segments,
    positions,
    gain_attn,
    w_query,
    w_key,
    w_value,
    w_out,
    gain_mlp,
    w_gate,
    w_up,
    w_down,
    cotangent,
):
    piece, width = tokens.shape[1:]
    nq, nk = w_query.shape[1] // HEAD, w_key.shape[1] // HEAD
    qw, kw = nq * HEAD, nk * HEAD
    wide = qw + 2 * kw
    ff = w_gate.shape[1]
    place = Place(dp)
    z = lax.axis_index("tensor")
    at = jnp.arange(tensor, dtype=jnp.int32) ^ z.astype(jnp.int32)
    across = lambda value, bit: swap(value, "tensor", tensor, bit)

    def exchange(block_for):
        got = {d: across(block_for(d), d) for d in reversed(range(1, tensor))}
        return [block_for(0)] + [got[d] for d in range(1, tensor)]

    def piece_of(value, d):
        return lax.dynamic_slice_in_dim(value, (z ^ d) * piece, piece, 0)

    select = np.zeros((wide, (nq + 2 * nk) * LANES), np.float32)
    select[:qw, : nq * LANES] = rotary_select(nq)
    select[qw : qw + kw, nq * LANES : (nq + nk) * LANES] = rotary_select(nk)
    select[qw + kw :, (nq + nk) * LANES :] = plain_select(nk)
    select = jnp.asarray(select, BF16)
    sel_plain, sel_turn = jnp.asarray(plain_select(nq), BF16), jnp.asarray(rotary_select(nq), BF16)

    v = Phases()
    heads = Gather(place, v, "heads")
    back = Gather(place, v, "back")
    own = Gather(place, v, "own")
    d_own = Scatter(place, v, "d_own")
    d_out = Scatter(place, v, "d_out")
    d_attn = Scatter(place, v, "d_attn")

    all_tokens = lax.all_gather(tokens[0], "tensor", axis=0, tiled=True)
    gains = jnp.pad(jnp.stack([gain_attn, gain_mlp], axis=1), ((0, 0), (0, LANES - 2)))
    w_heads = jnp.concatenate([w_query, w_key, w_value], axis=1)
    spread = dot(w_heads, select).astype(BF16)
    heads.shard(jnp.concatenate([spread, gains], axis=1))
    heads.put(1, heads.near())
    mlp_shard = jnp.concatenate([w_gate, w_up, w_down.T], axis=1)
    own.shard(mlp_shard)
    v.step(tokens=tokens[0], cot=cotangent[0], at=at, out_turned=w_out.T)

    heads.put(10, heads.halves())
    heads.put(3, heads.far())
    own_near = own.near()
    cosine, sine = rotary_tables(positions[0])
    v.step(cosine=cosine, sine=sine, segc=segments[0][:, None], segr=segments)

    half = piece // 2
    cot_low = lax.all_gather(v["cot"][:half], "tensor", axis=0, tiled=False)
    heads.put(5, heads.stack())
    heads.put(6, heads.cores())
    w_spread = heads.whole()
    own.put(1, own_near)
    v.step(w_spread=w_spread)

    out_blocks = exchange(lambda d: v["out_turned"])
    own.put(10, own.halves())
    own.put(3, own.far())
    picked = dot(jnp.eye(8, LANES, dtype=BF16), v["w_spread"][:, spread.shape[1] :], NT).astype(BF16)
    v.step(all_tokens=all_tokens, gain_first=picked[:1], gain_second=picked[1:2])

    normed, q, k, val = qkv(v["all_tokens"], v["gain_first"], v["w_spread"], v["cosine"], v["sine"], nq, nk)
    att, lse = attn_fwd(q, k, val, v["segc"], v["segr"], sel_plain, nq, nk)
    own.put(5, own.stack())
    v.step(
        normed=normed, q=q, k=k, v=val, att=att, lse=lse, cot_low=cot_low, **{"out%d" % d: out_blocks[d] for d in range(tensor)}
    )

    att_all = lax.all_gather(v["att"], "tensor", axis=0, tiled=False)
    shard = jnp.zeros((w_out.shape[1], width), BF16)
    for d in range(tensor):
        shard = lax.dynamic_update_slice_in_dim(shard, v.pop("out%d" % d), (z ^ d) * qw, 1)
    back.shard(shard)
    back.put(1, back.near())
    own.put(6, own.cores())
    back.put(10, back.halves())
    back.put(3, back.far())
    back.put(5, back.stack())
    back.put(6, back.cores())
    w_own = own.whole()
    w_back = back.whole()
    v.step(att_all=att_all, w_back=w_back, w_own=w_own)

    cot_high = lax.all_gather(v["cot"][half:], "tensor", axis=0, tiled=False)
    me = z.astype(jnp.int32).reshape(1)
    normed_mlp, hidden = outproj(me, v["att_all"], v["w_back"], v["all_tokens"], v["gain_second"])
    v.step(normed_mlp=normed_mlp.reshape(tensor, piece, width), hidden=hidden)

    units_low, g_low = mlp(v["normed_mlp"], v["cot_low"], v["w_own"], 0)
    v.step(units_low=units_low, g_low=g_low, cot_high=cot_high)
    got_low = lax.psum_scatter(v["g_low"], "tensor", scatter_dimension=0, tiled=True)
    units_high, g_high = mlp(v["normed_mlp"], v["cot_high"], v["w_own"], 1)
    v.step(units_high=units_high, g_high=g_high)

    got_high = lax.psum_scatter(v["g_high"], "tensor", scatter_dimension=0, tiled=True)
    lefts, rights = [v["normed_mlp"], v["cot_low"], v["cot_high"]], [v["units_low"], v["units_high"]]
    gate_up = [[(0, h, 2, h, k) for h in range(2)] for k in range(2)]
    d_own.product(lefts, gate_up + [[(1 + h, 0, 1, h, 2) for h in range(2)]], rights)
    w_compact = dot(v["w_spread"][:, : spread.shape[1]], select, NT).astype(BF16)
    v.step(got_low=got_low, w_compact=w_compact)
    d_own.cores()
    mixed_part = down(v["units_low"], v["units_high"], v["w_own"], tensor)
    v.step(mixed_part=mixed_part)
    d_own.add()
    v.step(got_high=got_high)

    mixed_got = lax.psum_scatter(v["mixed_part"].reshape(LEN, width), "tensor", scatter_dimension=0, tiled=True)
    near = d_own.near()
    g_hidden, g_branch, g_att = branch(
        v["at"], v["got_low"], v["got_high"], v["hidden"], v["cot"], v["gain_second"], v["w_back"], tensor
    )
    v.step(g_hidden=g_hidden, g_branch=g_branch, g_att=g_att)

    blocks = exchange(lambda d: v["g_att"][d])
    att_own = lax.dynamic_slice_in_dim(v["att_all"], z * piece, piece, 1)
    d_out.product([v["g_branch"][None]], [[(0, 0, 1, 0, k)] for k in range(tensor)], [att_own])
    d_own.put(2, near)
    v.step(g_heads=jnp.stack(blocks))
    d_own.add_near()
    v.step()

    d_out.cores()
    d_own.put(2, d_own.far())
    g_qkv = attn_bwd(
        v["at"], v["q"], v["k"], v["v"], v["segc"], v["segr"], v["lse"], v["g_heads"], v["cosine"], v["sine"],
        sel_plain, sel_turn, nq, nk,
    )
    g_nattn = dot(g_qkv, v["w_compact"], NT).astype(BF16)
    v.step(g_qkv=g_qkv, g_nattn=g_nattn)

    g_nattn = lax.psum_scatter(v["g_nattn"], "tensor", scatter_dimension=0, tiled=True)
    d_out.add()
    v.step()
    d_out.put(2, d_out.near())
    d_attn.product([v["normed"][None]], [[(0, 0, 1, 0, None)]], [v["g_qkv"]])
    grads_own = d_own.total()
    v.step(grads_own=grads_own)

    def gain_part(weights, grads, gain):
        total = sum(jnp.sum(w.astype(F32) * g, axis=1) for w, g in zip(weights, grads))
        return total / gain.astype(F32)

    d_attn.cores()
    d_out.add_near()
    v.step()
    d_out.put(2, d_out.far())
    d_attn.add()
    g_gate, g_up, g_down = (v["grads_own"][:, i * ff : (i + 1) * ff] for i in range(3))
    mlp_gain = gain_part((w_gate, w_up), (g_gate, g_up), gain_mlp)
    v.step(mlp_gain=mlp_gain)
    d_attn.put(2, d_attn.near())
    grads_out = d_out.total()
    v.step(grads_out=grads_out)
    d_attn.add_near()
    out_block = lambda d: lax.dynamic_slice_in_dim(v["grads_out"], (z ^ d) * qw, qw, 1)
    out_blocks = exchange(lambda d: out_block(d).astype(F32 if d == 0 else BF16))
    mixed = (v["hidden"] + mixed_got.astype(F32)).astype(BF16)
    v.step(mixed=mixed)
    d_attn.put(2, d_attn.far())
    v.step(grad_out=sum(block.astype(F32) for block in out_blocks))
    grads_attn = d_attn.total()
    g_query, g_key, g_value = grads_attn[:, :qw], grads_attn[:, qw : qw + kw], grads_attn[:, qw + kw :]
    attn_gain = gain_part((w_query, w_key, w_value), (g_query, g_key, g_value), gain_attn)
    v.step(attn_gain=attn_gain, g_query=g_query, g_key=g_key, g_value=g_value, g_nattn=g_nattn)
    both = jnp.stack([v["attn_gain"], v["mlp_gain"]])
    step = 1
    while step < tensor:
        both = both + across(both, step)
        step *= 2
    tokens, gain_first = v["tokens"].astype(F32), v["gain_first"].astype(F32)
    g_tokens = (v["g_hidden"] + norm_back(v["g_nattn"].astype(F32), tokens, gain_first)).astype(BF16)
    return (
        v["mixed"][None],
        g_tokens[None],
        both[0],
        v["g_query"],
        v["g_key"],
        v["g_value"],
        v["grad_out"].T,
        both[1],
        g_gate,
        g_up,
        g_down.T,
    )


def solution(mesh):
    split, whole_rows = P("dp", "tensor", None), P("dp", None)
    by_row, by_column, gain = P("dp", "tensor"), P("tensor", "dp"), P("dp")
    weights = (by_row, by_row, by_row, by_column, gain, by_row, by_row, by_column)
    step = functools.partial(on_device, mesh.shape["dp"], mesh.shape["tensor"])
    return jax.shard_map(
        step,
        mesh=mesh,
        in_specs=(split, whole_rows, whole_rows, gain, *weights, split),
        out_specs=(split, split, gain, *weights),
        check_vma=False,
    )
```

```python
import functools
import jax
import jax.numpy as jnp
import numpy as np
from jax import lax
from jax.experimental import pallas as pl
from jax.experimental.pallas import tpu as pltpu
from jax.sharding import PartitionSpec as P

HEADS = 16
KV_HEADS = 8
HEAD = 96
HALF = 48
LANES = 128
LEN = 1024
QBLOCK = 256
EPSILON = 1e-05
ROTARY_BASE = 100000.0
MASKED = -1e30
SCALE = HEAD ** (-0.5)
LOG2E = 1.4426950408889634
VMEM = 56 * 2**20
F32 = jnp.float32
BF16 = jnp.bfloat16
NT = (((1,), (1,)), ((), ()))
TN = (((0,), (0,)), ((), ()))


def dot(a, b, dims=(((1,), (0,)), ((), ()))):
    return lax.dot_general(a, b, dims, preferred_element_type=F32)


def params():
    return pltpu.CompilerParams(vmem_limit_bytes=VMEM)


def rotary_select(heads):
    out = np.zeros((heads * HEAD, heads * LANES), np.float32)
    for h in range(heads):
        for i in range(HALF):
            out[h * HEAD + i, h * LANES + i] = 1
            out[h * HEAD + HALF + i, h * LANES + 64 + i] = 1
    return out


def plain_select(heads):
    out = np.zeros((heads * HEAD, heads * LANES), np.float32)
    for h in range(heads):
        for i in range(HEAD):
            out[h * HEAD + i, h * LANES + i] = 1
    return out


def rotary_tables(positions):
    halves = jnp.arange(HALF, dtype=F32)
    inverse = ROTARY_BASE ** (-2.0 * halves / HEAD)
    angles = positions.astype(F32)[:, None] * inverse
    cosine, sine = jnp.cos(angles), jnp.sin(angles)
    gap = jnp.zeros((positions.shape[0], 16), F32)
    return (
        jnp.concatenate([cosine, gap, cosine, gap], axis=1),
        jnp.concatenate([-sine, gap, sine, gap], axis=1),
    )


def turn(values, cosine, sine):
    return values * cosine + pltpu.roll(values, 64, 1) * sine


def qkv_kernel(tok_ref, gain_ref, w_ref, cos_ref, sin_ref, n_ref, q_ref, k_ref, v_ref):
    resid = tok_ref[...].astype(F32)
    scaling = lax.rsqrt(jnp.mean(resid * resid, axis=1, keepdims=True) + EPSILON)
    normed = (resid * scaling * gain_ref[...].astype(F32)).astype(BF16)
    n_ref[...] = normed
    raw = dot(normed, w_ref[...])
    cosine, sine = cos_ref[...], sin_ref[...]
    nq, nk = q_ref.shape[1] // LANES, k_ref.shape[1] // LANES
    for h in range(nq):
        part = raw[:, h * LANES : (h + 1) * LANES]
        q_ref[:, h * LANES : (h + 1) * LANES] = turn(part, cosine, sine).astype(BF16)
    for h in range(nk):
        part = raw[:, (nq + h) * LANES : (nq + h + 1) * LANES]
        k_ref[:, h * LANES : (h + 1) * LANES] = turn(part, cosine, sine).astype(BF16)
    v_ref[...] = raw[:, (nq + nk) * LANES :].astype(BF16)


def qkv(tokens, gain, weights, cosine, sine, nq, nk):
    rows, width = tokens.shape
    block = lambda n: pl.BlockSpec((256, n), lambda i: (i, 0))
    whole = lambda a: pl.BlockSpec(a.shape, lambda i: (0, 0))
    sizes = (width, nq * LANES, nk * LANES, nk * LANES)
    return pl.pallas_call(
        qkv_kernel,
        grid=(rows // 256,),
        in_specs=[
            block(width),
            whole(gain),
            pl.BlockSpec((width, (nq + 2 * nk) * LANES), lambda i: (0, 0)),
            block(LANES),
            block(LANES),
        ],
        out_specs=[block(n) for n in sizes],
        out_shape=[jax.ShapeDtypeStruct((rows, n), BF16) for n in sizes],
        compiler_params=params(),
        cost_estimate=pl.CostEstimate(
            flops=2 * rows * width * weights.shape[1], bytes_accessed=12 * 2**20, transcendentals=0
        ),
    )(tokens, gain, weights, cosine, sine)


def allowed(segc, segr, i, kn):
    same = segc == segr[:, :kn]
    rows = lax.broadcasted_iota(jnp.int32, (QBLOCK, kn), 0) + i * QBLOCK
    cols = lax.broadcasted_iota(jnp.int32, (QBLOCK, kn), 1)
    return same & (cols <= rows)


def attn_fwd_kernel(nq, nk, q_ref, k_ref, v_ref, segc_ref, segr_ref, sel_ref, o_ref, lse_ref):
    grouped = nq // nk

    def body(i):
        kn = (i + 1) * QBLOCK
        mask = allowed(segc_ref[...], segr_ref[...], i, kn)
        outs = []
        for h in range(nq):
            g = h // grouped
            lanes = slice(g * LANES, (g + 1) * LANES)
            raw = dot(q_ref[:, h * LANES : (h + 1) * LANES], k_ref[:kn, lanes], NT)
            raw = jnp.where(mask, raw, MASKED)
            top = jnp.max(raw, axis=1, keepdims=True)
            e = jnp.exp2((raw - top) * (SCALE * LOG2E))
            total = jnp.sum(e, axis=1, keepdims=True)
            p = (e * (1.0 / total)).astype(BF16)
            outs.append(dot(p, v_ref[:kn, lanes]).astype(BF16))
            lse_ref[:, h : h + 1] = top * (SCALE * LOG2E) + jnp.log2(total)
        o_ref[...] = dot(jnp.concatenate(outs, axis=1), sel_ref[...], NT).astype(BF16)

    for i in range(LEN // QBLOCK):
        pl.when(pl.program_id(0) == i)(functools.partial(body, i))


def attn_fwd(q, k, v, segc, segr, sel, nq, nk):
    block = lambda n: pl.BlockSpec((QBLOCK, n), lambda i: (i, 0))
    whole = lambda a: pl.BlockSpec(a.shape, lambda i: (0, 0))
    return pl.pallas_call(
        functools.partial(attn_fwd_kernel, nq, nk),
        grid=(LEN // QBLOCK,),
        in_specs=[block(nq * LANES), whole(k), whole(v), block(1), whole(segr), whole(sel)],
        out_specs=[block(nq * HEAD), block(8)],
        out_shape=[
            jax.ShapeDtypeStruct((LEN, nq * HEAD), BF16),
            jax.ShapeDtypeStruct((LEN, 8), F32),
        ],
        compiler_params=params(),
        cost_estimate=pl.CostEstimate(
            flops=4 * nq * LEN * LEN * LANES, bytes_accessed=6 * 2**20, transcendentals=nq * LEN * LEN
        ),
    )(q, k, v, segc, segr, sel)


def attn_bwd_kernel(
    nq, nk, at_ref, q_ref, k_ref, v_ref, segc_ref, segr_ref, lse_ref, o_ref, do_ref, cos_ref, sin_ref,
    cosa_ref, sina_ref, selv_ref, selr_ref, g_ref, dk_ref, dv_ref,
):
    grouped = nq // nk
    wide = nq * HEAD

    @pl.when(pl.program_id(0) == 0)
    def _():
        dk_ref[...] = jnp.zeros_like(dk_ref)
        dv_ref[...] = jnp.zeros_like(dv_ref)

    def body(i):
        kn = (i + 1) * QBLOCK
        mask = allowed(segc_ref[...], segr_ref[...], i, kn)
        mask = jnp.concatenate([mask] * grouped, axis=0)
        do_all = dot(do_ref[0], selv_ref[...]).astype(BF16)
        inner = do_all.astype(F32) * dot(o_ref[...], selv_ref[...])
        turned = []
        for g in range(nk):
            lanes = slice(g * LANES, (g + 1) * LANES)
            heads = range(g * grouped, (g + 1) * grouped)
            stack = lambda of: jnp.concatenate([of(slice(h * LANES, (h + 1) * LANES)) for h in heads], axis=0)
            q = stack(lambda part: q_ref[:, part])
            grad = stack(lambda part: do_all[:, part])
            delta = stack(lambda part: jnp.sum(inner[:, part], axis=1, keepdims=True))
            lse = jnp.concatenate([lse_ref[:, h : h + 1] for h in heads], axis=0)
            raw = dot(q, k_ref[:kn, lanes], NT)
            p = jnp.where(mask, jnp.exp2(raw * (SCALE * LOG2E) - lse), 0.0)
            ds = (p * (dot(grad, v_ref[:kn, lanes], NT) - delta)).astype(BF16)
            dq = dot(ds, k_ref[:kn, lanes]) * SCALE
            for j in range(grouped):
                rows = slice(j * QBLOCK, (j + 1) * QBLOCK)
                turned.append(turn(dq[rows], cos_ref[...], -sin_ref[...]).astype(BF16))
            dk_ref[:kn, lanes] += dot(ds, q, TN)
            dv_ref[:kn, lanes] += dot(p.astype(BF16), grad, TN)
        rows = slice(i * QBLOCK, (i + 1) * QBLOCK)
        g_ref[rows, :wide] = dot(jnp.concatenate(turned, axis=1), selr_ref[...], NT).astype(BF16)

    blocks = LEN // QBLOCK
    for i in range(blocks):
        pl.when(pl.program_id(0) == i)(functools.partial(body, i))

    @pl.when(pl.program_id(0) == blocks - 1)
    def _():
        turned = []
        for g in range(nk):
            lanes = slice(g * LANES, (g + 1) * LANES)
            turned.append(turn(dk_ref[:, lanes] * SCALE, cosa_ref[...], -sina_ref[...]).astype(BF16))
        kw = nk * HEAD
        gk = dot(jnp.concatenate(turned, axis=1), selr_ref[:kw, : nk * LANES], NT)
        gv = dot(dv_ref[...].astype(BF16), selv_ref[:kw, : nk * LANES], NT)
        g_ref[:, wide:] = jnp.concatenate([gk, gv], axis=1).astype(BF16)


def attn_bwd(at, q, k, v, segc, segr, lse, o, do, cosine, sine, selv, selr, nq, nk):
    block = lambda n: pl.BlockSpec((QBLOCK, n), lambda i, at: (i, 0))
    whole = lambda a: pl.BlockSpec(a.shape, lambda i, at: (0, 0))
    total = (nq + 2 * nk) * HEAD
    return pl.pallas_call(
        functools.partial(attn_bwd_kernel, nq, nk),
        grid_spec=pltpu.PrefetchScalarGridSpec(
            num_scalar_prefetch=1,
            grid=(LEN // QBLOCK,),
            in_specs=[
                block(nq * LANES), whole(k), whole(v), block(1), whole(segr), block(8), block(nq * HEAD),
                pl.BlockSpec((1, QBLOCK, nq * HEAD), lambda i, at: (at[i], 0, 0)),
                block(LANES), block(LANES), whole(cosine), whole(sine), whole(selv), whole(selr),
            ],
            out_specs=pl.BlockSpec((LEN, total), lambda i, at: (0, 0)),
            scratch_shapes=[pltpu.VMEM((LEN, nk * LANES), F32), pltpu.VMEM((LEN, nk * LANES), F32)],
        ),
        out_shape=jax.ShapeDtypeStruct((LEN, total), BF16),
        compiler_params=params(),
        cost_estimate=pl.CostEstimate(
            flops=10 * nq * LEN * LEN * LANES, bytes_accessed=8 * 2**20, transcendentals=nq * LEN * LEN
        ),
    )(at, q, k, v, segc, segr, lse, o, do, cosine, sine, cosine, sine, selv, selr)


def cost(flops, megabytes):
    return pl.CostEstimate(flops=flops, bytes_accessed=megabytes * 2**20, transcendentals=0)


def outproj_kernel(me_ref, att_ref, w_ref, tok_ref, gain_ref, n_ref, hid_ref):
    hidden = tok_ref[...].astype(F32)
    wide = att_ref.shape[2]
    for z in range(att_ref.shape[0]):
        hidden = hidden + dot(att_ref[z], w_ref[:, z * wide : (z + 1) * wide], NT)
    scaling = lax.rsqrt(jnp.mean(hidden * hidden, axis=1, keepdims=True) + EPSILON)
    n_ref[...] = (hidden * scaling * gain_ref[...].astype(F32)).astype(BF16)
    hid_ref[...] = hidden


def outproj(me, att, weights, tokens, gain):
    parts, rows, wide = att.shape
    width = tokens.shape[1]
    piece = rows // parts
    at = lambda i, me: lax.rem(me[0] + 1 + i, parts)
    return pl.pallas_call(
        outproj_kernel,
        grid_spec=pltpu.PrefetchScalarGridSpec(
            num_scalar_prefetch=1,
            grid=(parts,),
            in_specs=[
                pl.BlockSpec((parts, piece, wide), lambda i, me: (0, at(i, me), 0)),
                pl.BlockSpec((width, parts * wide), lambda i, me: (0, 0)),
                pl.BlockSpec((piece, width), lambda i, me: (at(i, me), 0)),
                pl.BlockSpec(gain.shape, lambda i, me: (0, 0)),
            ],
            out_specs=[
                pl.BlockSpec((piece, width), lambda i, me: (at(i, me), 0)),
                pl.BlockSpec((piece, width), lambda i, me: (0, 0)),
            ],
        ),
        out_shape=[jax.ShapeDtypeStruct((rows, width), BF16), jax.ShapeDtypeStruct((piece, width), F32)],
        compiler_params=params(),
        cost_estimate=cost(2 * rows * width * width, 16),
    )(me, att, weights, tokens, gain)


def mlp_kernel(n_ref, cot_ref, wg_ref, wu_ref, wd_ref, out_ref, gn_ref, sum_ref):
    step = pl.program_id(0)
    rows, width = sum_ref.shape
    normed = n_ref[...].reshape(rows, width)
    gate = dot(normed, wg_ref[...])
    upward = dot(normed, wu_ref[...])
    g_act = dot(cot_ref[...].reshape(rows, width), wd_ref[...])
    sigma = jax.nn.sigmoid(gate)
    silu = gate * sigma
    out_ref[2] = (silu * upward).astype(BF16)
    g_gate = (g_act * upward * (sigma + silu * (1.0 - sigma))).astype(BF16)
    g_up = (g_act * silu).astype(BF16)
    out_ref[0] = g_gate
    out_ref[1] = g_up
    part = dot(g_gate, wg_ref[...], NT) + dot(g_up, wu_ref[...], NT)

    @pl.when(step == 0)
    def _():
        sum_ref[...] = part

    @pl.when(step > 0)
    def _():
        sum_ref[...] += part

    @pl.when(step == pl.num_programs(0) - 1)
    def _():
        gn_ref[...] = sum_ref[...].astype(BF16)


def mlp(normed, cot, weights, half):
    parts, piece, width = normed.shape
    rows = parts * piece // 2
    units = weights.shape[1] // 3
    chunk = 512
    steps = units // chunk
    some = pl.BlockSpec((parts, piece // 2, width), lambda j: (0, half, 0))
    column = lambda k: pl.BlockSpec((width, chunk), lambda j: (0, k * steps + j))
    return pl.pallas_call(
        mlp_kernel,
        grid=(steps,),
        in_specs=[some, pl.BlockSpec(cot.shape, lambda j: (0, 0, 0)), column(0), column(1), column(2)],
        out_specs=[
            pl.BlockSpec((3, rows, chunk), lambda j: (0, 0, j)),
            pl.BlockSpec((rows, width), lambda j: (0, 0)),
        ],
        out_shape=[
            jax.ShapeDtypeStruct((3, rows, units), BF16),
            jax.ShapeDtypeStruct((rows, width), BF16),
        ],
        scratch_shapes=[pltpu.VMEM((rows, width), F32)],
        compiler_params=params(),
        cost_estimate=cost(10 * rows * width * units, 24),
    )(normed, cot, weights, weights, weights)


def down_kernel(low_ref, high_ref, w_ref, out_ref):
    @pl.when(pl.program_id(0) == 0)
    def _():
        out_ref[...] = dot(low_ref[0], w_ref[...], NT).astype(BF16).reshape(out_ref.shape)

    @pl.when(pl.program_id(0) == 1)
    def _():
        out_ref[...] = dot(high_ref[0], w_ref[...], NT).astype(BF16).reshape(out_ref.shape)


def down(low, high, weights, parts):
    rows, units = low.shape[1:]
    width = weights.shape[0]
    piece = 2 * rows // parts
    return pl.pallas_call(
        down_kernel,
        grid=(2,),
        in_specs=[
            pl.BlockSpec((1, rows, units), lambda h: (2, 0, 0)),
            pl.BlockSpec((1, rows, units), lambda h: (2, 0, 0)),
            pl.BlockSpec((width, units), lambda h: (0, 2)),
        ],
        out_specs=pl.BlockSpec((parts, piece // 2, width), lambda h: (0, h, 0)),
        out_shape=jax.ShapeDtypeStruct((parts, piece, width), BF16),
        compiler_params=params(),
        cost_estimate=cost(4 * rows * width * units, 12),
    )(low, high, weights)


def norm_back(incoming, values, gain):
    scaling = lax.rsqrt(jnp.mean(values * values, axis=1, keepdims=True) + EPSILON)
    unit = values * scaling
    tilted = incoming * gain
    return scaling * (tilted - unit * jnp.mean(tilted * unit, axis=1, keepdims=True))


def branch_kernel(at_ref, got_ref, hid_ref, cot_ref, gain_ref, w_ref, gh_ref, gb_ref, ga_ref):
    @pl.when(pl.program_id(0) == 0)
    def _():
        back = norm_back(got_ref[...].astype(F32), hid_ref[...], gain_ref[...].astype(F32))
        g_hidden = cot_ref[...].astype(F32) + back
        gh_ref[...] = g_hidden
        gb_ref[...] = g_hidden.astype(BF16)

    ga_ref[0] = dot(gb_ref[...], w_ref[...]).astype(BF16)


def branch(at, got, hidden, cot, gain, weights, parts, half):
    rows, width = got.shape
    wide = weights.shape[1] // parts
    whole = pl.BlockSpec((rows, width), lambda i, at: (0, 0))
    some = pl.BlockSpec((rows, width), lambda i, at: (half, 0))
    return pl.pallas_call(
        branch_kernel,
        grid_spec=pltpu.PrefetchScalarGridSpec(
            num_scalar_prefetch=1,
            grid=(parts,),
            in_specs=[
                whole,
                some,
                some,
                pl.BlockSpec(gain.shape, lambda i, at: (0, 0)),
                pl.BlockSpec((width, wide), lambda i, at: (0, at[i])),
            ],
            out_specs=[whole, whole, pl.BlockSpec((1, rows, wide), lambda i, at: (i, 0, 0))],
        ),
        out_shape=[
            jax.ShapeDtypeStruct((rows, width), F32),
            jax.ShapeDtypeStruct((rows, width), BF16),
            jax.ShapeDtypeStruct((parts, rows, wide), BF16),
        ],
        compiler_params=params(),
        cost_estimate=cost(2 * rows * width * parts * wide, 10),
    )(at, got, hidden, cot, gain, weights)


def wgrad_kernel(uses, count, core_ref, *refs):
    keep_ref, send_ref = refs[-2:]
    lefts, rights = refs[:count], refs[count:-2]
    half = keep_ref.shape[1]
    at = 0
    for terms in uses:
        total = None
        for left, part, parts, right, k in terms:
            rows = lefts[left].shape[1] // parts
            a = lefts[left][:, part * rows : (part + 1) * rows].reshape(-1, lefts[left].shape[2])
            b = rights[right][...] if k is None else rights[right][k]
            product = dot(a, b, TN)
            total = product if total is None else total + product
        block = total.astype(BF16)
        columns = slice(at, at + block.shape[1])

        @pl.when(core_ref[0] == 0)
        def _():
            keep_ref[0, :, columns] = block[:half]
            send_ref[0, :, columns] = block[half:]

        @pl.when(core_ref[0] == 1)
        def _():
            keep_ref[0, :, columns] = block[half:]
            send_ref[0, :, columns] = block[:half]

        at += block.shape[1]


def wgrad(core, lefts, uses, rights, dp):
    pieces, rows, width = lefts[0].shape
    shard = width // dp
    columns = sum(rights[terms[0][3]].shape[-1] for terms in uses)
    pairs = dp // 2
    out = jax.ShapeDtypeStruct((pairs, shard, columns), BF16)
    out_spec = pl.BlockSpec((1, shard, columns), lambda i, core: (i, 0, 0))
    return pl.pallas_call(
        functools.partial(wgrad_kernel, uses, len(lefts)),
        grid_spec=pltpu.PrefetchScalarGridSpec(
            num_scalar_prefetch=1,
            grid=(pairs,),
            in_specs=[pl.BlockSpec((*a.shape[:2], 2 * shard), lambda i, core: (0, 0, i)) for a in lefts]
            + [pl.BlockSpec(r.shape, lambda i, core, d=r.ndim: (0,) * d) for r in rights],
            out_specs=[out_spec, out_spec],
        ),
        out_shape=[out, out],
        compiler_params=params(),
        cost_estimate=cost(2 * pieces * rows * width * columns, 16),
    )(core, *lefts, *rights)


def assemble_kernel(at_ref, *refs):
    pieces, out_ref = refs[:-1], refs[-1]
    for i, piece in enumerate(pieces):
        rows = piece.shape[0]
        out_ref[pl.ds(pl.multiple_of(at_ref[i], rows), rows)] = piece[...]


def assemble(starts, pieces):
    rows, columns = sum(p.shape[0] for p in pieces), pieces[0].shape[1]
    chunk = max(c for c in range(128, 769, 128) if columns % c == 0)
    block = lambda n: pl.BlockSpec((n, chunk), lambda j, at: (0, j))
    return pl.pallas_call(
        assemble_kernel,
        grid_spec=pltpu.PrefetchScalarGridSpec(
            num_scalar_prefetch=1,
            grid=(columns // chunk,),
            in_specs=[block(p.shape[0]) for p in pieces],
            out_specs=block(rows),
        ),
        out_shape=jax.ShapeDtypeStruct((rows, columns), pieces[0].dtype),
        compiler_params=params(),
        cost_estimate=pl.CostEstimate(flops=0, bytes_accessed=4 * rows * columns, transcendentals=0),
    )(jnp.stack(starts).astype(jnp.int32), *pieces)


def blend_kernel(core_ref, mine_ref, other_ref, out_ref):
    half = mine_ref.shape[0]

    @pl.when(core_ref[0] == 0)
    def _():
        out_ref[:half] = mine_ref[...]
        out_ref[half:] = other_ref[...]

    @pl.when(core_ref[0] == 1)
    def _():
        out_ref[:half] = other_ref[...]
        out_ref[half:] = mine_ref[...]


def blend(core, mine, other, chips):
    rows, columns = mine.shape
    shard = rows // chips
    block = pl.BlockSpec((shard, columns), lambda i, core: (i, 0))
    return pl.pallas_call(
        blend_kernel,
        grid_spec=pltpu.PrefetchScalarGridSpec(
            num_scalar_prefetch=1,
            grid=(chips,),
            in_specs=[block, block],
            out_specs=pl.BlockSpec((2 * shard, columns), lambda i, core: (i, 0)),
        ),
        out_shape=jax.ShapeDtypeStruct((2 * rows, columns), mine.dtype),
        compiler_params=params(),
        cost_estimate=pl.CostEstimate(flops=0, bytes_accessed=8 * rows * columns, transcendentals=0),
    )(core, mine, other)


def swap(value, axis, size, bit):
    return lax.ppermute(value, axis, [(k, k ^ bit) for k in range(size)])


class Phases(dict):
    def step(self, **more):
        self.update(more)
        names = [name for name in self if self[name] is not None]
        self.update(zip(names, lax.optimization_barrier([self[name] for name in names])))

    def drop(self, *names):
        for name in names:
            del self[name]


class Gather:
    def __init__(self, place, v, name):
        self.place, self.v, self.names = place, v, [name + str(i) for i in range(12)]

    def get(self, first, last):
        return [self.v[name] for name in self.names[first:last]]

    def put(self, first, values):
        self.v.update(zip(self.names[first:], values))

    def shard(self, value):
        self.put(0, [value])

    def near(self):
        if not self.place.grid:
            return []
        (value,) = self.get(0, 1)
        return [swap(value, "dp", 8, 2), swap(value, "dp", 8, 4)]

    def halves(self):
        if not self.place.grid:
            return []
        by_x, by_y = self.get(1, 3)
        half = by_x.shape[0] // 2
        return [by_x[:half], by_y[half:]]

    def far(self):
        if not self.place.grid:
            return []
        top, low = self.get(10, 12)
        self.v.drop(*self.names[10:12])
        return [swap(top, "dp", 8, 4), swap(low, "dp", 8, 2)]

    def stack(self):
        if not self.place.grid:
            return []
        pieces = self.get(0, 5)
        rows = pieces[0].shape[0]
        x, y = self.place.x, self.place.y
        chips = [2 * y + x, 2 * y + 1 - x, 2 - 2 * y + x, 3 - 2 * y - x, 3 - 2 * y - x]
        below = [0, 0, 0, 0, rows // 2]
        self.v.drop(*self.names[1:5])
        return [assemble([chip * rows + low for chip, low in zip(chips, below)], pieces)]

    def cores(self):
        return [swap(self.get(5, 6)[0], "dp", 8, 1)] if self.place.grid else []

    def each(self, first, last):
        return [swap(value, "dp", 8, 1) for value in self.get(first, last)] if self.place.grid else []

    def whole_of_pieces(self):
        if not self.place.grid:
            return lax.all_gather(self.get(0, 1)[0], "dp", axis=0, tiled=True)
        pieces = self.get(0, 10)
        rows = pieces[0].shape[0]
        x, y, core = self.place.x, self.place.y, self.place.core
        chips = [2 * y + x, 2 * y + 1 - x, 2 - 2 * y + x, 3 - 2 * y - x, 3 - 2 * y - x]
        below = [0, 0, 0, 0, rows // 2]
        starts = [(2 * chip + core) * rows + low for chip, low in zip(chips, below)]
        starts += [(2 * chip + 1 - core) * rows + low for chip, low in zip(chips, below)]
        self.v.drop(*self.names)
        return assemble(starts, pieces)

    def whole(self):
        if not self.place.grid:
            return lax.all_gather(self.get(0, 1)[0], "dp", axis=0, tiled=True)
        mine, other = self.get(5, 7)
        self.v.drop(*self.names[5:7])
        return blend(self.place.core.astype(jnp.int32).reshape(1), mine, other, 4)


class Scatter:
    def __init__(self, place, v, name):
        self.place, self.v, self.names = place, v, [name + str(i) for i in range(4)]

    def get(self, count):
        return [self.v[name] for name in self.names[:count]]

    def put(self, first, values):
        self.v.update(zip(self.names[first:], values))

    def product(self, lefts, uses, rights):
        if self.place.grid:
            core = self.place.core.astype(jnp.int32).reshape(1)
            self.put(0, wgrad(core, lefts, uses, rights, 8))
            return
        groups = []
        for terms in uses:
            total = 0.0
            for left, part, parts, right, k in terms:
                rows = lefts[left].shape[1] // parts
                a = lefts[left][:, part * rows : (part + 1) * rows].reshape(-1, lefts[left].shape[2])
                total = total + dot(a, rights[right] if k is None else rights[right][k], TN)
            groups.append(total.astype(BF16))
        self.put(0, [jnp.concatenate(groups, axis=1)])

    def cores(self):
        if self.place.grid:
            self.put(1, [swap(self.get(2)[1], "dp", 8, 1)])

    def add(self):
        if not self.place.grid:
            return
        keep, got = self.get(2)
        both = (keep.astype(F32) + got.astype(F32)).astype(BF16)
        rows, columns = both.shape[1:]
        both = both.reshape(2, 2, rows, columns)
        left, right = both[..., : columns // 2], both[..., columns // 2 :]
        x, y = self.place.x, self.place.y
        self.put(0, [pick(left, x, 1), pick(right, y, 0), pick(left, 1 - x, 1), pick(right, 1 - y, 0)])

    def near(self):
        if not self.place.grid:
            return []
        _, _, left, right = self.get(4)
        return [swap(left, "dp", 8, 2), swap(right, "dp", 8, 4)]

    def add_near(self):
        if not self.place.grid:
            return
        left, right, got_left, got_right = self.get(4)
        left = (left.astype(F32) + got_left.astype(F32)).astype(BF16)
        right = (right.astype(F32) + got_right.astype(F32)).astype(BF16)
        x, y = self.place.x, self.place.y
        self.put(0, [pick(left, y, 0), pick(right, x, 0), pick(left, 1 - y, 0), pick(right, 1 - x, 0)])

    def far(self):
        if not self.place.grid:
            return []
        _, _, left, right = self.get(4)
        return [swap(left, "dp", 8, 4), swap(right, "dp", 8, 2)]

    def total(self):
        if not self.place.grid:
            whole = self.get(1)[0]
            return lax.psum_scatter(whole, "dp", scatter_dimension=0, tiled=True).astype(F32)
        left, right, got_left, got_right = (value.astype(F32) for value in self.get(4))
        self.v.drop(*self.names)
        return jnp.concatenate([left + got_left, right + got_right], axis=1)


def pick(value, index, axis):
    return lax.dynamic_index_in_dim(value, index, axis, keepdims=False)


class Place:
    def __init__(self, size):
        index = lax.axis_index("dp")
        self.grid = size == 8
        self.core = lax.rem(index, 2)
        self.x = lax.rem(index // 2, 2)
        self.y = index // 4


def on_device(
    dp,
    tensor,
    tokens,
    segments,
    positions,
    gain_attn,
    w_query,
    w_key,
    w_value,
    w_out,
    gain_mlp,
    w_gate,
    w_up,
    w_down,
    cotangent,
):
    piece, width = tokens.shape[1:]
    nq, nk = w_query.shape[1] // HEAD, w_key.shape[1] // HEAD
    qw, kw = nq * HEAD, nk * HEAD
    wide = qw + 2 * kw
    ff = w_gate.shape[1]
    place = Place(dp)
    z = lax.axis_index("tensor")
    at = jnp.arange(tensor, dtype=jnp.int32) ^ z.astype(jnp.int32)
    across = lambda value, bit: swap(value, "tensor", tensor, bit)

    def exchange(block_for):
        got = {d: across(block_for(d), d) for d in reversed(range(1, tensor))}
        return [block_for(0)] + [got[d] for d in range(1, tensor)]

    def piece_of(value, d):
        return lax.dynamic_slice_in_dim(value, (z ^ d) * piece, piece, 0)

    select = np.zeros((wide, (nq + 2 * nk) * LANES), np.float32)
    select[:qw, : nq * LANES] = rotary_select(nq)
    select[qw : qw + kw, nq * LANES : (nq + nk) * LANES] = rotary_select(nk)
    select[qw + kw :, (nq + nk) * LANES :] = plain_select(nk)
    select = jnp.asarray(select, BF16)
    sel_plain, sel_turn = jnp.asarray(plain_select(nq), BF16), jnp.asarray(rotary_select(nq), BF16)

    v = Phases()
    heads = Gather(place, v, "heads")
    back = Gather(place, v, "back")
    own = Gather(place, v, "own")
    d_own = Scatter(place, v, "d_own")
    d_out = Scatter(place, v, "d_out")
    d_attn = Scatter(place, v, "d_attn")

    all_tokens = lax.all_gather(tokens[0], "tensor", axis=0, tiled=True)
    gains = jnp.pad(jnp.stack([gain_attn, gain_mlp], axis=1), ((0, 0), (0, LANES - 2)))
    w_heads = jnp.concatenate([w_query, w_key, w_value], axis=1)
    spread = dot(w_heads, select).astype(BF16)
    heads.shard(jnp.concatenate([spread, gains], axis=1))
    heads.put(1, heads.near())
    mlp_shard = jnp.concatenate([w_gate, w_up, w_down.T], axis=1)
    own.shard(mlp_shard)
    v.step(tokens=tokens[0], cot=cotangent[0], at=at, out_turned=w_out.T)

    heads.put(10, heads.halves())
    heads.put(3, heads.far())
    own_near = own.near()
    cosine, sine = rotary_tables(positions[0])
    v.step(cosine=cosine, sine=sine, segc=segments[0][:, None], segr=segments)

    half = piece // 2
    cot_low = lax.all_gather(v["cot"][:half], "tensor", axis=0, tiled=False)
    heads.put(5, heads.stack())
    heads.put(6, heads.cores())
    w_spread = heads.whole()
    own.put(1, own_near)
    v.step(w_spread=w_spread)

    out_blocks = exchange(lambda d: v["out_turned"])
    own.put(10, own.halves())
    own.put(3, own.far())
    picked = dot(jnp.eye(8, LANES, dtype=BF16), v["w_spread"][:, spread.shape[1] :], NT).astype(BF16)
    v.step(all_tokens=all_tokens, gain_first=picked[:1], gain_second=picked[1:2])

    normed, q, k, val = qkv(v["all_tokens"], v["gain_first"], v["w_spread"], v["cosine"], v["sine"], nq, nk)
    att, lse = attn_fwd(q, k, val, v["segc"], v["segr"], sel_plain, nq, nk)
    own.put(5, own.stack())
    v.step(
        normed=normed, q=q, k=k, v=val, att=att, lse=lse, cot_low=cot_low, **{"out%d" % d: out_blocks[d] for d in range(tensor)}
    )

    att_all = lax.all_gather(v["att"], "tensor", axis=0, tiled=False)
    shard = jnp.zeros((w_out.shape[1], width), BF16)
    for d in range(tensor):
        shard = lax.dynamic_update_slice_in_dim(shard, v.pop("out%d" % d), (z ^ d) * qw, 1)
    back.shard(shard)
    back.put(1, back.near())
    own.put(6, own.cores())
    back.put(10, back.halves())
    back.put(3, back.far())
    back.put(5, back.stack())
    back.put(6, back.cores())
    w_own = own.whole()
    w_back = back.whole()
    v.step(att_all=att_all, w_back=w_back, w_own=w_own)

    cot_high = lax.all_gather(v["cot"][half:], "tensor", axis=0, tiled=False)
    me = z.astype(jnp.int32).reshape(1)
    normed_mlp, hidden = outproj(me, v["att_all"], v["w_back"], v["all_tokens"], v["gain_second"])
    v.step(normed_mlp=normed_mlp.reshape(tensor, piece, width), hidden=hidden)

    units_low, g_low = mlp(v["normed_mlp"], v["cot_low"], v["w_own"], 0)
    v.step(units_low=units_low, g_low=g_low, cot_high=cot_high)
    got_low = lax.psum_scatter(v["g_low"], "tensor", scatter_dimension=0, tiled=True)
    units_high, g_high = mlp(v["normed_mlp"], v["cot_high"], v["w_own"], 1)
    v.step(units_high=units_high, g_high=g_high)

    got_high = lax.psum_scatter(v["g_high"], "tensor", scatter_dimension=0, tiled=True)
    lefts, rights = [v["normed_mlp"], v["cot_low"], v["cot_high"]], [v["units_low"], v["units_high"]]
    gate_up = [[(0, h, 2, h, k) for h in range(2)] for k in range(2)]
    d_own.product(lefts, gate_up + [[(1 + h, 0, 1, h, 2) for h in range(2)]], rights)
    w_compact = dot(v["w_spread"][:, : spread.shape[1]], select, NT).astype(BF16)
    v.step(got_low=got_low, w_compact=w_compact)
    hidden_low, branch_low, att_low = branch(
        v["at"], v["got_low"], v["hidden"], v["cot"], v["gain_second"], v["w_back"], tensor, 0
    )
    v.step(hidden_low=hidden_low, branch_low=branch_low, att_low=att_low)
    blocks_low = exchange(lambda d: v["att_low"][d])
    d_own.cores()
    mixed_part = down(v["units_low"], v["units_high"], v["w_own"], tensor)
    v.step(mixed_part=mixed_part)
    d_own.add()
    v.step(got_high=got_high, **{"low%d" % d: blocks_low[d] for d in range(tensor)})

    mixed_got = lax.psum_scatter(v["mixed_part"].reshape(LEN, width), "tensor", scatter_dimension=0, tiled=True)
    near = d_own.near()
    hidden_high, branch_high, att_high = branch(
        v["at"], v["got_high"], v["hidden"], v["cot"], v["gain_second"], v["w_back"], tensor, 1
    )
    v.step(hidden_high=hidden_high, branch_high=branch_high, att_high=att_high)

    blocks_high = exchange(lambda d: v["att_high"][d])
    att_own = lax.dynamic_slice_in_dim(v["att_all"], z * piece, piece, 1)
    g_branch = jnp.concatenate([v["branch_low"], v["branch_high"]])
    d_out.product([g_branch[None]], [[(0, 0, 1, 0, k)] for k in range(tensor)], [att_own])
    d_own.put(2, near)
    v.step(g_heads=jnp.stack([jnp.concatenate([v.pop("low%d" % d), blocks_high[d]]) for d in range(tensor)]))
    d_own.add_near()
    v.step()

    d_out.cores()
    d_own.put(2, d_own.far())
    g_qkv = attn_bwd(
        v["at"], v["q"], v["k"], v["v"], v["segc"], v["segr"], v["lse"], v["att"], v["g_heads"], v["cosine"], v["sine"],
        sel_plain, sel_turn, nq, nk,
    )
    g_nattn = dot(g_qkv, v["w_compact"], NT).astype(BF16)
    v.step(g_qkv=g_qkv, g_nattn=g_nattn, mixed_got=mixed_got)

    g_nattn = lax.psum_scatter(v["g_nattn"], "tensor", scatter_dimension=0, tiled=True)
    d_out.add()
    v.step()
    d_out.put(2, d_out.near())
    d_attn.product([v["normed"][None]], [[(0, 0, 1, 0, None)]], [v["g_qkv"]])
    grads_own = d_own.total()
    v.step(grads_own=grads_own)

    def gain_part(weights, grads, gain):
        total = sum(jnp.sum(w.astype(F32) * g, axis=1) for w, g in zip(weights, grads))
        return total / gain.astype(F32)

    d_attn.cores()
    d_out.add_near()
    v.step()
    d_out.put(2, d_out.far())
    d_attn.add()
    g_gate, g_up, g_down = (v["grads_own"][:, i * ff : (i + 1) * ff] for i in range(3))
    mlp_gain = gain_part((w_gate, w_up), (g_gate, g_up), gain_mlp)
    v.step(mlp_gain=mlp_gain)
    d_attn.put(2, d_attn.near())
    grads_out = d_out.total()
    v.step(grads_out=grads_out)
    d_attn.add_near()
    out_block = lambda d: lax.dynamic_slice_in_dim(v["grads_out"], (z ^ d) * qw, qw, 1)
    out_blocks = exchange(lambda d: out_block(d).astype(F32 if d == 0 else BF16))
    mixed = (v["hidden"] + v["mixed_got"].astype(F32)).astype(BF16)
    v.step(mixed=mixed)
    d_attn.put(2, d_attn.far())
    v.step()
    grads_attn = d_attn.total()
    g_query, g_key, g_value = grads_attn[:, :qw], grads_attn[:, qw : qw + kw], grads_attn[:, qw + kw :]
    attn_gain = gain_part((w_query, w_key, w_value), (g_query, g_key, g_value), gain_attn)
    v.step(attn_gain=attn_gain, g_query=g_query, g_key=g_key, g_value=g_value, g_nattn=g_nattn)
    both = jnp.stack([v["attn_gain"], v["mlp_gain"]])
    step = 1
    while step < tensor:
        both = both + across(both, step)
        step *= 2
    tokens, gain_first = v["tokens"].astype(F32), v["gain_first"].astype(F32)
    g_tokens = (jnp.concatenate([v["hidden_low"], v["hidden_high"]]) + norm_back(v["g_nattn"].astype(F32), tokens, gain_first)).astype(BF16)
    return (
        v["mixed"][None],
        g_tokens[None],
        both[0],
        v["g_query"],
        v["g_key"],
        v["g_value"],
        sum(block.astype(F32) for block in out_blocks).T,
        both[1],
        g_gate,
        g_up,
        g_down.T,
    )


def solution(mesh):
    split, whole_rows = P("dp", "tensor", None), P("dp", None)
    by_row, by_column, gain = P("dp", "tensor"), P("tensor", "dp"), P("dp")
    weights = (by_row, by_row, by_row, by_column, gain, by_row, by_row, by_column)
    step = functools.partial(on_device, mesh.shape["dp"], mesh.shape["tensor"])
    return jax.shard_map(
        step,
        mesh=mesh,
        in_specs=(split, whole_rows, whole_rows, gain, *weights, split),
        out_specs=(split, split, gain, *weights),
        check_vma=False,
    )
```

```python
import functools
import jax
import jax.numpy as jnp
import numpy as np
from jax import lax
from jax.experimental import pallas as pl
from jax.experimental.pallas import tpu as pltpu
from jax.sharding import PartitionSpec as P

HEADS = 16
KV_HEADS = 8
HEAD = 96
HALF = 48
LANES = 128
LEN = 1024
QBLOCK = 256
EPSILON = 1e-05
ROTARY_BASE = 100000.0
MASKED = -1e30
SCALE = HEAD ** (-0.5)
LOG2E = 1.4426950408889634
VMEM = 56 * 2**20
F32 = jnp.float32
BF16 = jnp.bfloat16
NT = (((1,), (1,)), ((), ()))
TN = (((0,), (0,)), ((), ()))


def dot(a, b, dims=(((1,), (0,)), ((), ()))):
    return lax.dot_general(a, b, dims, preferred_element_type=F32)


def params():
    return pltpu.CompilerParams(vmem_limit_bytes=VMEM)


def rotary_select(heads):
    out = np.zeros((heads * HEAD, heads * LANES), np.float32)
    for h in range(heads):
        for i in range(HALF):
            out[h * HEAD + i, h * LANES + i] = 1
            out[h * HEAD + HALF + i, h * LANES + 64 + i] = 1
    return out


def plain_select(heads):
    out = np.zeros((heads * HEAD, heads * LANES), np.float32)
    for h in range(heads):
        for i in range(HEAD):
            out[h * HEAD + i, h * LANES + i] = 1
    return out


def rotary_tables(positions):
    halves = jnp.arange(HALF, dtype=F32)
    inverse = ROTARY_BASE ** (-2.0 * halves / HEAD)
    angles = positions.astype(F32)[:, None] * inverse
    cosine, sine = jnp.cos(angles), jnp.sin(angles)
    gap = jnp.zeros((positions.shape[0], 16), F32)
    return (
        jnp.concatenate([cosine, gap, cosine, gap], axis=1),
        jnp.concatenate([-sine, gap, sine, gap], axis=1),
    )


def turn(values, cosine, sine):
    return values * cosine + pltpu.roll(values, 64, 1) * sine


def qkv_kernel(tok_ref, gain_ref, w_ref, cos_ref, sin_ref, n_ref, q_ref, k_ref, v_ref):
    resid = tok_ref[...].astype(F32)
    scaling = lax.rsqrt(jnp.mean(resid * resid, axis=1, keepdims=True) + EPSILON)
    normed = (resid * scaling * gain_ref[...].astype(F32)).astype(BF16)
    n_ref[...] = normed
    raw = dot(normed, w_ref[...])
    cosine, sine = cos_ref[...], sin_ref[...]
    nq, nk = q_ref.shape[1] // LANES, k_ref.shape[1] // LANES
    for h in range(nq):
        part = raw[:, h * LANES : (h + 1) * LANES]
        q_ref[:, h * LANES : (h + 1) * LANES] = turn(part, cosine, sine).astype(BF16)
    for h in range(nk):
        part = raw[:, (nq + h) * LANES : (nq + h + 1) * LANES]
        k_ref[:, h * LANES : (h + 1) * LANES] = turn(part, cosine, sine).astype(BF16)
    v_ref[...] = raw[:, (nq + nk) * LANES :].astype(BF16)


def qkv(tokens, gain, weights, cosine, sine, nq, nk):
    rows, width = tokens.shape
    block = lambda n: pl.BlockSpec((256, n), lambda i: (i, 0))
    whole = lambda a: pl.BlockSpec(a.shape, lambda i: (0, 0))
    sizes = (width, nq * LANES, nk * LANES, nk * LANES)
    return pl.pallas_call(
        qkv_kernel,
        grid=(rows // 256,),
        in_specs=[
            block(width),
            whole(gain),
            pl.BlockSpec((width, (nq + 2 * nk) * LANES), lambda i: (0, 0)),
            block(LANES),
            block(LANES),
        ],
        out_specs=[block(n) for n in sizes],
        out_shape=[jax.ShapeDtypeStruct((rows, n), BF16) for n in sizes],
        compiler_params=params(),
        cost_estimate=pl.CostEstimate(
            flops=2 * rows * width * weights.shape[1], bytes_accessed=12 * 2**20, transcendentals=0
        ),
    )(tokens, gain, weights, cosine, sine)


def allowed(segc, segr, i, kn):
    same = segc == segr[:, :kn]
    rows = lax.broadcasted_iota(jnp.int32, (QBLOCK, kn), 0) + i * QBLOCK
    cols = lax.broadcasted_iota(jnp.int32, (QBLOCK, kn), 1)
    return same & (cols <= rows)


def attn_fwd_kernel(nq, nk, q_ref, k_ref, v_ref, segc_ref, segr_ref, sel_ref, o_ref, lse_ref):
    grouped = nq // nk

    def body(i):
        kn = (i + 1) * QBLOCK
        mask = allowed(segc_ref[...], segr_ref[...], i, kn)
        outs = []
        for h in range(nq):
            g = h // grouped
            lanes = slice(g * LANES, (g + 1) * LANES)
            raw = dot(q_ref[:, h * LANES : (h + 1) * LANES], k_ref[:kn, lanes], NT)
            raw = jnp.where(mask, raw, MASKED)
            top = jnp.max(raw, axis=1, keepdims=True)
            e = jnp.exp2((raw - top) * (SCALE * LOG2E))
            total = jnp.sum(e, axis=1, keepdims=True)
            p = (e * (1.0 / total)).astype(BF16)
            outs.append(dot(p, v_ref[:kn, lanes]).astype(BF16))
            lse_ref[:, h : h + 1] = top * (SCALE * LOG2E) + jnp.log2(total)
        o_ref[...] = dot(jnp.concatenate(outs, axis=1), sel_ref[...], NT).astype(BF16)

    for i in range(LEN // QBLOCK):
        pl.when(pl.program_id(0) == i)(functools.partial(body, i))


def attn_fwd(q, k, v, segc, segr, sel, nq, nk):
    block = lambda n: pl.BlockSpec((QBLOCK, n), lambda i: (i, 0))
    whole = lambda a: pl.BlockSpec(a.shape, lambda i: (0, 0))
    return pl.pallas_call(
        functools.partial(attn_fwd_kernel, nq, nk),
        grid=(LEN // QBLOCK,),
        in_specs=[block(nq * LANES), whole(k), whole(v), block(1), whole(segr), whole(sel)],
        out_specs=[block(nq * HEAD), block(8)],
        out_shape=[
            jax.ShapeDtypeStruct((LEN, nq * HEAD), BF16),
            jax.ShapeDtypeStruct((LEN, 8), F32),
        ],
        compiler_params=params(),
        cost_estimate=pl.CostEstimate(
            flops=4 * nq * LEN * LEN * LANES, bytes_accessed=6 * 2**20, transcendentals=nq * LEN * LEN
        ),
    )(q, k, v, segc, segr, sel)


def attn_bwd_kernel(
    nq, nk, at_ref, q_ref, k_ref, v_ref, segc_ref, segr_ref, lse_ref, o_ref, do_ref, cos_ref, sin_ref,
    cosa_ref, sina_ref, selv_ref, selr_ref, g_ref, dk_ref, dv_ref,
):
    grouped = nq // nk
    wide = nq * HEAD

    @pl.when(pl.program_id(0) == 0)
    def _():
        dk_ref[...] = jnp.zeros_like(dk_ref)
        dv_ref[...] = jnp.zeros_like(dv_ref)

    def body(i):
        kn = (i + 1) * QBLOCK
        mask = allowed(segc_ref[...], segr_ref[...], i, kn)
        mask = jnp.concatenate([mask] * grouped, axis=0)
        do_all = dot(do_ref[0], selv_ref[...]).astype(BF16)
        inner = do_all.astype(F32) * dot(o_ref[...], selv_ref[...])
        turned = []
        for g in range(nk):
            lanes = slice(g * LANES, (g + 1) * LANES)
            heads = range(g * grouped, (g + 1) * grouped)
            stack = lambda of: jnp.concatenate([of(slice(h * LANES, (h + 1) * LANES)) for h in heads], axis=0)
            q = stack(lambda part: q_ref[:, part])
            grad = stack(lambda part: do_all[:, part])
            delta = stack(lambda part: jnp.sum(inner[:, part], axis=1, keepdims=True))
            lse = jnp.concatenate([lse_ref[:, h : h + 1] for h in heads], axis=0)
            raw = dot(q, k_ref[:kn, lanes], NT)
            p = jnp.where(mask, jnp.exp2(raw * (SCALE * LOG2E) - lse), 0.0)
            ds = (p * (dot(grad, v_ref[:kn, lanes], NT) - delta)).astype(BF16)
            dq = dot(ds, k_ref[:kn, lanes]) * SCALE
            for j in range(grouped):
                rows = slice(j * QBLOCK, (j + 1) * QBLOCK)
                turned.append(turn(dq[rows], cos_ref[...], -sin_ref[...]).astype(BF16))
            dk_ref[:kn, lanes] += dot(ds, q, TN)
            dv_ref[:kn, lanes] += dot(p.astype(BF16), grad, TN)
        rows = slice(i * QBLOCK, (i + 1) * QBLOCK)
        g_ref[rows, :wide] = dot(jnp.concatenate(turned, axis=1), selr_ref[...], NT).astype(BF16)

    blocks = LEN // QBLOCK
    for i in range(blocks):
        pl.when(pl.program_id(0) == i)(functools.partial(body, i))

    @pl.when(pl.program_id(0) == blocks - 1)
    def _():
        turned = []
        for g in range(nk):
            lanes = slice(g * LANES, (g + 1) * LANES)
            turned.append(turn(dk_ref[:, lanes] * SCALE, cosa_ref[...], -sina_ref[...]).astype(BF16))
        kw = nk * HEAD
        gk = dot(jnp.concatenate(turned, axis=1), selr_ref[:kw, : nk * LANES], NT)
        gv = dot(dv_ref[...].astype(BF16), selv_ref[:kw, : nk * LANES], NT)
        g_ref[:, wide:] = jnp.concatenate([gk, gv], axis=1).astype(BF16)


def attn_bwd(at, q, k, v, segc, segr, lse, o, do, cosine, sine, selv, selr, nq, nk):
    block = lambda n: pl.BlockSpec((QBLOCK, n), lambda i, at: (i, 0))
    whole = lambda a: pl.BlockSpec(a.shape, lambda i, at: (0, 0))
    total = (nq + 2 * nk) * HEAD
    return pl.pallas_call(
        functools.partial(attn_bwd_kernel, nq, nk),
        grid_spec=pltpu.PrefetchScalarGridSpec(
            num_scalar_prefetch=1,
            grid=(LEN // QBLOCK,),
            in_specs=[
                block(nq * LANES), whole(k), whole(v), block(1), whole(segr), block(8), block(nq * HEAD),
                pl.BlockSpec((1, QBLOCK, nq * HEAD), lambda i, at: (at[i], 0, 0)),
                block(LANES), block(LANES), whole(cosine), whole(sine), whole(selv), whole(selr),
            ],
            out_specs=pl.BlockSpec((LEN, total), lambda i, at: (0, 0)),
            scratch_shapes=[pltpu.VMEM((LEN, nk * LANES), F32), pltpu.VMEM((LEN, nk * LANES), F32)],
        ),
        out_shape=jax.ShapeDtypeStruct((LEN, total), BF16),
        compiler_params=params(),
        cost_estimate=pl.CostEstimate(
            flops=10 * nq * LEN * LEN * LANES, bytes_accessed=8 * 2**20, transcendentals=nq * LEN * LEN
        ),
    )(at, q, k, v, segc, segr, lse, o, do, cosine, sine, cosine, sine, selv, selr)


def cost(flops, megabytes):
    return pl.CostEstimate(flops=flops, bytes_accessed=megabytes * 2**20, transcendentals=0)


def outproj_kernel(me_ref, att_ref, w_ref, tok_ref, gain_ref, n_ref, hid_ref):
    hidden = tok_ref[...].astype(F32)
    wide = att_ref.shape[2]
    for z in range(att_ref.shape[0]):
        hidden = hidden + dot(att_ref[z], w_ref[:, z * wide : (z + 1) * wide], NT)
    scaling = lax.rsqrt(jnp.mean(hidden * hidden, axis=1, keepdims=True) + EPSILON)
    n_ref[...] = (hidden * scaling * gain_ref[...].astype(F32)).astype(BF16)
    hid_ref[...] = hidden


def outproj(me, att, weights, tokens, gain):
    parts, rows, wide = att.shape
    width = tokens.shape[1]
    piece = rows // parts
    at = lambda i, me: lax.rem(me[0] + 1 + i, parts)
    return pl.pallas_call(
        outproj_kernel,
        grid_spec=pltpu.PrefetchScalarGridSpec(
            num_scalar_prefetch=1,
            grid=(parts,),
            in_specs=[
                pl.BlockSpec((parts, piece, wide), lambda i, me: (0, at(i, me), 0)),
                pl.BlockSpec((width, parts * wide), lambda i, me: (0, 0)),
                pl.BlockSpec((piece, width), lambda i, me: (at(i, me), 0)),
                pl.BlockSpec(gain.shape, lambda i, me: (0, 0)),
            ],
            out_specs=[
                pl.BlockSpec((piece, width), lambda i, me: (at(i, me), 0)),
                pl.BlockSpec((piece, width), lambda i, me: (0, 0)),
            ],
        ),
        out_shape=[jax.ShapeDtypeStruct((rows, width), BF16), jax.ShapeDtypeStruct((piece, width), F32)],
        compiler_params=params(),
        cost_estimate=cost(2 * rows * width * width, 16),
    )(me, att, weights, tokens, gain)


def mlp_kernel(n_ref, cot_ref, wg_ref, wu_ref, wd_ref, out_ref, gn_ref, sum_ref):
    step = pl.program_id(0)
    rows, width = sum_ref.shape
    normed = n_ref[...].reshape(rows, width)
    gate = dot(normed, wg_ref[...])
    upward = dot(normed, wu_ref[...])
    g_act = dot(cot_ref[...].reshape(rows, width), wd_ref[...])
    sigma = jax.nn.sigmoid(gate)
    silu = gate * sigma
    out_ref[2] = (silu * upward).astype(BF16)
    g_gate = (g_act * upward * (sigma + silu * (1.0 - sigma))).astype(BF16)
    g_up = (g_act * silu).astype(BF16)
    out_ref[0] = g_gate
    out_ref[1] = g_up
    part = dot(g_gate, wg_ref[...], NT) + dot(g_up, wu_ref[...], NT)

    @pl.when(step == 0)
    def _():
        sum_ref[...] = part

    @pl.when(step > 0)
    def _():
        sum_ref[...] += part

    @pl.when(step == pl.num_programs(0) - 1)
    def _():
        gn_ref[...] = sum_ref[...].astype(BF16)


def mlp(normed, cot, weights, half):
    parts, piece, width = normed.shape
    rows = parts * piece // 2
    units = weights.shape[1] // 3
    chunk = 512
    steps = units // chunk
    some = pl.BlockSpec((parts, piece // 2, width), lambda j: (0, half, 0))
    column = lambda k: pl.BlockSpec((width, chunk), lambda j: (0, k * steps + j))
    return pl.pallas_call(
        mlp_kernel,
        grid=(steps,),
        in_specs=[some, pl.BlockSpec(cot.shape, lambda j: (0, 0, 0)), column(0), column(1), column(2)],
        out_specs=[
            pl.BlockSpec((3, rows, chunk), lambda j: (0, 0, j)),
            pl.BlockSpec((rows, width), lambda j: (0, 0)),
        ],
        out_shape=[
            jax.ShapeDtypeStruct((3, rows, units), BF16),
            jax.ShapeDtypeStruct((rows, width), BF16),
        ],
        scratch_shapes=[pltpu.VMEM((rows, width), F32)],
        compiler_params=params(),
        cost_estimate=cost(10 * rows * width * units, 24),
    )(normed, cot, weights, weights, weights)


def down_kernel(low_ref, high_ref, w_ref, out_ref):
    @pl.when(pl.program_id(0) == 0)
    def _():
        out_ref[...] = dot(low_ref[0], w_ref[...], NT).astype(BF16).reshape(out_ref.shape)

    @pl.when(pl.program_id(0) == 1)
    def _():
        out_ref[...] = dot(high_ref[0], w_ref[...], NT).astype(BF16).reshape(out_ref.shape)


def down(low, high, weights, parts):
    rows, units = low.shape[1:]
    width = weights.shape[0]
    piece = 2 * rows // parts
    return pl.pallas_call(
        down_kernel,
        grid=(2,),
        in_specs=[
            pl.BlockSpec((1, rows, units), lambda h: (2, 0, 0)),
            pl.BlockSpec((1, rows, units), lambda h: (2, 0, 0)),
            pl.BlockSpec((width, units), lambda h: (0, 2)),
        ],
        out_specs=pl.BlockSpec((parts, piece // 2, width), lambda h: (0, h, 0)),
        out_shape=jax.ShapeDtypeStruct((parts, piece, width), BF16),
        compiler_params=params(),
        cost_estimate=cost(4 * rows * width * units, 12),
    )(low, high, weights)


def norm_back(incoming, values, gain):
    scaling = lax.rsqrt(jnp.mean(values * values, axis=1, keepdims=True) + EPSILON)
    unit = values * scaling
    tilted = incoming * gain
    return scaling * (tilted - unit * jnp.mean(tilted * unit, axis=1, keepdims=True))


def branch_kernel(at_ref, got_ref, hid_ref, cot_ref, gain_ref, w_ref, gh_ref, gb_ref, ga_ref):
    @pl.when(pl.program_id(0) == 0)
    def _():
        back = norm_back(got_ref[...].astype(F32), hid_ref[...], gain_ref[...].astype(F32))
        g_hidden = cot_ref[...].astype(F32) + back
        gh_ref[...] = g_hidden
        gb_ref[...] = g_hidden.astype(BF16)

    ga_ref[0] = dot(gb_ref[...], w_ref[...]).astype(BF16)


def branch(at, got, hidden, cot, gain, weights, parts, half):
    rows, width = got.shape
    wide = weights.shape[1] // parts
    whole = pl.BlockSpec((rows, width), lambda i, at: (0, 0))
    some = pl.BlockSpec((rows, width), lambda i, at: (half, 0))
    return pl.pallas_call(
        branch_kernel,
        grid_spec=pltpu.PrefetchScalarGridSpec(
            num_scalar_prefetch=1,
            grid=(parts,),
            in_specs=[
                whole,
                some,
                some,
                pl.BlockSpec(gain.shape, lambda i, at: (0, 0)),
                pl.BlockSpec((width, wide), lambda i, at: (0, at[i])),
            ],
            out_specs=[whole, whole, pl.BlockSpec((1, rows, wide), lambda i, at: (i, 0, 0))],
        ),
        out_shape=[
            jax.ShapeDtypeStruct((rows, width), F32),
            jax.ShapeDtypeStruct((rows, width), BF16),
            jax.ShapeDtypeStruct((parts, rows, wide), BF16),
        ],
        compiler_params=params(),
        cost_estimate=cost(2 * rows * width * parts * wide, 10),
    )(at, got, hidden, cot, gain, weights)


def wgrad_kernel(uses, count, core_ref, *refs):
    keep_ref, send_ref = refs[-2:]
    lefts, rights = refs[:count], refs[count:-2]
    half = keep_ref.shape[1]
    at = 0
    for terms in uses:
        total = None
        for left, part, parts, right, k in terms:
            rows = lefts[left].shape[1] // parts
            a = lefts[left][:, part * rows : (part + 1) * rows].reshape(-1, lefts[left].shape[2])
            b = rights[right][...] if k is None else rights[right][k]
            product = dot(a, b, TN)
            total = product if total is None else total + product
        block = total.astype(BF16)
        columns = slice(at, at + block.shape[1])

        @pl.when(core_ref[0] == 0)
        def _():
            keep_ref[0, :, columns] = block[:half]
            send_ref[0, :, columns] = block[half:]

        @pl.when(core_ref[0] == 1)
        def _():
            keep_ref[0, :, columns] = block[half:]
            send_ref[0, :, columns] = block[:half]

        at += block.shape[1]


def wgrad(core, lefts, uses, rights, dp):
    pieces, rows, width = lefts[0].shape
    shard = width // dp
    columns = sum(rights[terms[0][3]].shape[-1] for terms in uses)
    pairs = dp // 2
    out = jax.ShapeDtypeStruct((pairs, shard, columns), BF16)
    out_spec = pl.BlockSpec((1, shard, columns), lambda i, core: (i, 0, 0))
    return pl.pallas_call(
        functools.partial(wgrad_kernel, uses, len(lefts)),
        grid_spec=pltpu.PrefetchScalarGridSpec(
            num_scalar_prefetch=1,
            grid=(pairs,),
            in_specs=[pl.BlockSpec((*a.shape[:2], 2 * shard), lambda i, core: (0, 0, i)) for a in lefts]
            + [pl.BlockSpec(r.shape, lambda i, core, d=r.ndim: (0,) * d) for r in rights],
            out_specs=[out_spec, out_spec],
        ),
        out_shape=[out, out],
        compiler_params=params(),
        cost_estimate=cost(2 * pieces * rows * width * columns, 16),
    )(core, *lefts, *rights)


def assemble_kernel(at_ref, *refs):
    pieces, out_ref = refs[:-1], refs[-1]
    for i, piece in enumerate(pieces):
        rows = piece.shape[0]
        out_ref[pl.ds(pl.multiple_of(at_ref[i], rows), rows)] = piece[...]


def assemble(starts, pieces):
    rows, columns = sum(p.shape[0] for p in pieces), pieces[0].shape[1]
    chunk = max(c for c in range(128, 769, 128) if columns % c == 0)
    block = lambda n: pl.BlockSpec((n, chunk), lambda j, at: (0, j))
    return pl.pallas_call(
        assemble_kernel,
        grid_spec=pltpu.PrefetchScalarGridSpec(
            num_scalar_prefetch=1,
            grid=(columns // chunk,),
            in_specs=[block(p.shape[0]) for p in pieces],
            out_specs=block(rows),
        ),
        out_shape=jax.ShapeDtypeStruct((rows, columns), pieces[0].dtype),
        compiler_params=params(),
        cost_estimate=pl.CostEstimate(flops=0, bytes_accessed=4 * rows * columns, transcendentals=0),
    )(jnp.stack(starts).astype(jnp.int32), *pieces)


def blend_kernel(core_ref, mine_ref, other_ref, out_ref):
    half = mine_ref.shape[0]

    @pl.when(core_ref[0] == 0)
    def _():
        out_ref[:half] = mine_ref[...]
        out_ref[half:] = other_ref[...]

    @pl.when(core_ref[0] == 1)
    def _():
        out_ref[:half] = other_ref[...]
        out_ref[half:] = mine_ref[...]


def blend(core, mine, other, chips):
    rows, columns = mine.shape
    shard = rows // chips
    block = pl.BlockSpec((shard, columns), lambda i, core: (i, 0))
    return pl.pallas_call(
        blend_kernel,
        grid_spec=pltpu.PrefetchScalarGridSpec(
            num_scalar_prefetch=1,
            grid=(chips,),
            in_specs=[block, block],
            out_specs=pl.BlockSpec((2 * shard, columns), lambda i, core: (i, 0)),
        ),
        out_shape=jax.ShapeDtypeStruct((2 * rows, columns), mine.dtype),
        compiler_params=params(),
        cost_estimate=pl.CostEstimate(flops=0, bytes_accessed=8 * rows * columns, transcendentals=0),
    )(core, mine, other)


def swap(value, axis, size, bit):
    return lax.ppermute(value, axis, [(k, k ^ bit) for k in range(size)])


class Phases(dict):
    def step(self, **more):
        self.update(more)
        names = [name for name in self if self[name] is not None]
        self.update(zip(names, lax.optimization_barrier([self[name] for name in names])))

    def drop(self, *names):
        for name in names:
            del self[name]


class Gather:
    def __init__(self, place, v, name):
        self.place, self.v, self.names = place, v, [name + str(i) for i in range(12)]

    def get(self, first, last):
        return [self.v[name] for name in self.names[first:last]]

    def put(self, first, values):
        self.v.update(zip(self.names[first:], values))

    def shard(self, value):
        self.put(0, [value])

    def near(self):
        if not self.place.grid:
            return []
        (value,) = self.get(0, 1)
        return [swap(value, "dp", 8, 2), swap(value, "dp", 8, 4)]

    def halves(self):
        if not self.place.grid:
            return []
        by_x, by_y = self.get(1, 3)
        half = by_x.shape[0] // 2
        return [by_x[:half], by_y[half:]]

    def far(self):
        if not self.place.grid:
            return []
        top, low = self.get(10, 12)
        self.v.drop(*self.names[10:12])
        return [swap(top, "dp", 8, 4), swap(low, "dp", 8, 2)]

    def stack(self):
        if not self.place.grid:
            return []
        pieces = self.get(0, 5)
        rows = pieces[0].shape[0]
        x, y = self.place.x, self.place.y
        chips = [2 * y + x, 2 * y + 1 - x, 2 - 2 * y + x, 3 - 2 * y - x, 3 - 2 * y - x]
        below = [0, 0, 0, 0, rows // 2]
        self.v.drop(*self.names[1:5])
        return [assemble([chip * rows + low for chip, low in zip(chips, below)], pieces)]

    def cores(self):
        return [swap(self.get(5, 6)[0], "dp", 8, 1)] if self.place.grid else []

    def each(self, first, last):
        return [swap(value, "dp", 8, 1) for value in self.get(first, last)] if self.place.grid else []

    def whole_of_pieces(self):
        if not self.place.grid:
            return lax.all_gather(self.get(0, 1)[0], "dp", axis=0, tiled=True)
        pieces = self.get(0, 10)
        rows = pieces[0].shape[0]
        x, y, core = self.place.x, self.place.y, self.place.core
        chips = [2 * y + x, 2 * y + 1 - x, 2 - 2 * y + x, 3 - 2 * y - x, 3 - 2 * y - x]
        below = [0, 0, 0, 0, rows // 2]
        starts = [(2 * chip + core) * rows + low for chip, low in zip(chips, below)]
        starts += [(2 * chip + 1 - core) * rows + low for chip, low in zip(chips, below)]
        self.v.drop(*self.names)
        return assemble(starts, pieces)

    def whole(self):
        if not self.place.grid:
            return lax.all_gather(self.get(0, 1)[0], "dp", axis=0, tiled=True)
        mine, other = self.get(5, 7)
        self.v.drop(*self.names[5:7])
        return blend(self.place.core.astype(jnp.int32).reshape(1), mine, other, 4)


class Scatter:
    def __init__(self, place, v, name):
        self.place, self.v, self.names = place, v, [name + str(i) for i in range(4)]

    def get(self, count):
        return [self.v[name] for name in self.names[:count]]

    def put(self, first, values):
        self.v.update(zip(self.names[first:], values))

    def product(self, lefts, uses, rights):
        if self.place.grid:
            core = self.place.core.astype(jnp.int32).reshape(1)
            self.put(0, wgrad(core, lefts, uses, rights, 8))
            return
        groups = []
        for terms in uses:
            total = 0.0
            for left, part, parts, right, k in terms:
                rows = lefts[left].shape[1] // parts
                a = lefts[left][:, part * rows : (part + 1) * rows].reshape(-1, lefts[left].shape[2])
                total = total + dot(a, rights[right] if k is None else rights[right][k], TN)
            groups.append(total.astype(BF16))
        self.put(0, [jnp.concatenate(groups, axis=1)])

    def cores(self):
        if self.place.grid:
            self.put(1, [swap(self.get(2)[1], "dp", 8, 1)])

    def add(self):
        if not self.place.grid:
            return
        keep, got = self.get(2)
        both = (keep.astype(F32) + got.astype(F32)).astype(BF16)
        rows, columns = both.shape[1:]
        both = both.reshape(2, 2, rows, columns)
        left, right = both[..., : columns // 2], both[..., columns // 2 :]
        x, y = self.place.x, self.place.y
        self.put(0, [pick(left, x, 1), pick(right, y, 0), pick(left, 1 - x, 1), pick(right, 1 - y, 0)])

    def near(self):
        if not self.place.grid:
            return []
        _, _, left, right = self.get(4)
        return [swap(left, "dp", 8, 2), swap(right, "dp", 8, 4)]

    def add_near(self):
        if not self.place.grid:
            return
        left, right, got_left, got_right = self.get(4)
        left = (left.astype(F32) + got_left.astype(F32)).astype(BF16)
        right = (right.astype(F32) + got_right.astype(F32)).astype(BF16)
        x, y = self.place.x, self.place.y
        self.put(0, [pick(left, y, 0), pick(right, x, 0), pick(left, 1 - y, 0), pick(right, 1 - x, 0)])

    def far(self):
        if not self.place.grid:
            return []
        _, _, left, right = self.get(4)
        return [swap(left, "dp", 8, 4), swap(right, "dp", 8, 2)]

    def total(self):
        if not self.place.grid:
            whole = self.get(1)[0]
            return lax.psum_scatter(whole, "dp", scatter_dimension=0, tiled=True).astype(F32)
        left, right, got_left, got_right = (value.astype(F32) for value in self.get(4))
        self.v.drop(*self.names)
        return jnp.concatenate([left + got_left, right + got_right], axis=1)


def pick(value, index, axis):
    return lax.dynamic_index_in_dim(value, index, axis, keepdims=False)


class Place:
    def __init__(self, size):
        index = lax.axis_index("dp")
        self.grid = size == 8
        self.core = lax.rem(index, 2)
        self.x = lax.rem(index // 2, 2)
        self.y = index // 4


def on_device(
    dp,
    tensor,
    tokens,
    segments,
    positions,
    gain_attn,
    w_query,
    w_key,
    w_value,
    w_out,
    gain_mlp,
    w_gate,
    w_up,
    w_down,
    cotangent,
):
    piece, width = tokens.shape[1:]
    nq, nk = w_query.shape[1] // HEAD, w_key.shape[1] // HEAD
    qw, kw = nq * HEAD, nk * HEAD
    wide = qw + 2 * kw
    ff = w_gate.shape[1]
    place = Place(dp)
    z = lax.axis_index("tensor")
    at = jnp.arange(tensor, dtype=jnp.int32) ^ z.astype(jnp.int32)
    across = lambda value, bit: swap(value, "tensor", tensor, bit)

    def exchange(block_for):
        got = {d: across(block_for(d), d) for d in reversed(range(1, tensor))}
        return [block_for(0)] + [got[d] for d in range(1, tensor)]

    def piece_of(value, d):
        return lax.dynamic_slice_in_dim(value, (z ^ d) * piece, piece, 0)

    select = np.zeros((wide, (nq + 2 * nk) * LANES), np.float32)
    select[:qw, : nq * LANES] = rotary_select(nq)
    select[qw : qw + kw, nq * LANES : (nq + nk) * LANES] = rotary_select(nk)
    select[qw + kw :, (nq + nk) * LANES :] = plain_select(nk)
    select = jnp.asarray(select, BF16)
    sel_plain, sel_turn = jnp.asarray(plain_select(nq), BF16), jnp.asarray(rotary_select(nq), BF16)

    v = Phases()
    heads = Gather(place, v, "heads")
    back = Gather(place, v, "back")
    own = Gather(place, v, "own")
    d_own = Scatter(place, v, "d_own")
    d_out = Scatter(place, v, "d_out")
    d_attn = Scatter(place, v, "d_attn")

    all_tokens = lax.all_gather(tokens[0], "tensor", axis=0, tiled=True)
    gains = jnp.pad(jnp.stack([gain_attn, gain_mlp], axis=1), ((0, 0), (0, LANES - 2)))
    w_heads = jnp.concatenate([w_query, w_key, w_value], axis=1)
    spread = dot(w_heads, select).astype(BF16)
    heads.shard(jnp.concatenate([spread, gains], axis=1))
    heads.put(1, heads.near())
    mlp_shard = jnp.concatenate([w_gate, w_up, w_down.T], axis=1)
    own.shard(mlp_shard)
    v.step(tokens=tokens[0], cot=cotangent[0], at=at, out_turned=w_out.T)

    heads.put(10, heads.halves())
    heads.put(3, heads.far())
    own_near = own.near()
    cosine, sine = rotary_tables(positions[0])
    v.step(cosine=cosine, sine=sine, segc=segments[0][:, None], segr=segments)

    half = piece // 2
    cot_low = lax.all_gather(v["cot"][:half], "tensor", axis=0, tiled=False)
    heads.put(5, heads.stack())
    heads.put(6, heads.cores())
    w_spread = heads.whole()
    own.put(1, own_near)
    v.step(w_spread=w_spread)

    out_blocks = exchange(lambda d: v["out_turned"])
    own.put(10, own.halves())
    own.put(3, own.far())
    picked = dot(jnp.eye(8, LANES, dtype=BF16), v["w_spread"][:, spread.shape[1] :], NT).astype(BF16)
    v.step(all_tokens=all_tokens, gain_first=picked[:1], gain_second=picked[1:2])

    normed, q, k, val = qkv(v["all_tokens"], v["gain_first"], v["w_spread"], v["cosine"], v["sine"], nq, nk)
    att, lse = attn_fwd(q, k, val, v["segc"], v["segr"], sel_plain, nq, nk)
    own.put(5, own.stack())
    v.step(
        normed=normed, q=q, k=k, v=val, att=att, lse=lse, cot_low=cot_low, **{"out%d" % d: out_blocks[d] for d in range(tensor)}
    )

    att_all = lax.all_gather(v["att"], "tensor", axis=0, tiled=False)
    shard = jnp.zeros((w_out.shape[1], width), BF16)
    for d in range(tensor):
        shard = lax.dynamic_update_slice_in_dim(shard, v.pop("out%d" % d), (z ^ d) * qw, 1)
    back.shard(shard)
    back.put(1, back.near())
    own.put(6, own.cores())
    back.put(10, back.halves())
    back.put(3, back.far())
    back.put(5, back.stack())
    back.put(6, back.cores())
    w_own = own.whole()
    w_back = back.whole()
    v.step(att_all=att_all, w_back=w_back, w_own=w_own)

    cot_high = lax.all_gather(v["cot"][half:], "tensor", axis=0, tiled=False)
    me = z.astype(jnp.int32).reshape(1)
    normed_mlp, hidden = outproj(me, v["att_all"], v["w_back"], v["all_tokens"], v["gain_second"])
    v.step(normed_mlp=normed_mlp.reshape(tensor, piece, width), hidden=hidden)

    units_low, g_low = mlp(v["normed_mlp"], v["cot_low"], v["w_own"], 0)
    v.step(units_low=units_low, g_low=g_low, cot_high=cot_high)
    got_low = lax.psum_scatter(v["g_low"], "tensor", scatter_dimension=0, tiled=True)
    units_high, g_high = mlp(v["normed_mlp"], v["cot_high"], v["w_own"], 1)
    v.step(units_high=units_high, g_high=g_high)

    got_high = lax.psum_scatter(v["g_high"], "tensor", scatter_dimension=0, tiled=True)
    lefts, rights = [v["normed_mlp"], v["cot_low"], v["cot_high"]], [v["units_low"], v["units_high"]]
    gate_up = [[(0, h, 2, h, k) for h in range(2)] for k in range(2)]
    d_own.product(lefts, gate_up + [[(1 + h, 0, 1, h, 2) for h in range(2)]], rights)
    w_compact = dot(v["w_spread"][:, : spread.shape[1]], select, NT).astype(BF16)
    v.step(got_low=got_low, w_compact=w_compact)
    hidden_low, branch_low, att_low = branch(
        v["at"], v["got_low"], v["hidden"], v["cot"], v["gain_second"], v["w_back"], tensor, 0
    )
    v.update(hidden_low=hidden_low, branch_low=branch_low)
    blocks_low = exchange(lambda d: att_low[d])
    d_own.cores()
    mixed_part = down(v["units_low"], v["units_high"], v["w_own"], tensor)
    v.update(mixed_part=mixed_part)
    d_own.add()
    v.step(got_high=got_high, **{"low%d" % d: blocks_low[d] for d in range(tensor)})

    mixed_got = lax.psum_scatter(v["mixed_part"].reshape(LEN, width), "tensor", scatter_dimension=0, tiled=True)
    near = d_own.near()
    hidden_high, branch_high, att_high = branch(
        v["at"], v["got_high"], v["hidden"], v["cot"], v["gain_second"], v["w_back"], tensor, 1
    )
    v.step(hidden_high=hidden_high, branch_high=branch_high, att_high=att_high)

    blocks_high = exchange(lambda d: v["att_high"][d])
    att_own = lax.dynamic_slice_in_dim(v["att_all"], z * piece, piece, 1)
    g_branch = jnp.concatenate([v["branch_low"], v["branch_high"]])
    d_out.product([g_branch[None]], [[(0, 0, 1, 0, k)] for k in range(tensor)], [att_own])
    d_own.put(2, near)
    v.step(g_heads=jnp.stack([jnp.concatenate([v.pop("low%d" % d), blocks_high[d]]) for d in range(tensor)]))
    d_own.add_near()
    v.step()

    d_out.cores()
    d_own.put(2, d_own.far())
    g_qkv = attn_bwd(
        v["at"], v["q"], v["k"], v["v"], v["segc"], v["segr"], v["lse"], v["att"], v["g_heads"], v["cosine"], v["sine"],
        sel_plain, sel_turn, nq, nk,
    )
    g_nattn = dot(g_qkv, v["w_compact"], NT).astype(BF16)
    v.step(g_qkv=g_qkv, g_nattn=g_nattn)

    g_nattn = lax.psum_scatter(v["g_nattn"], "tensor", scatter_dimension=0, tiled=True)
    d_out.add()
    v.step()
    d_out.put(2, d_out.near())
    d_attn.product([v["normed"][None]], [[(0, 0, 1, 0, None)]], [v["g_qkv"]])
    grads_own = d_own.total()
    v.step(grads_own=grads_own)

    def gain_part(weights, grads, gain):
        total = sum(jnp.sum(w.astype(F32) * g, axis=1) for w, g in zip(weights, grads))
        return total / gain.astype(F32)

    d_attn.cores()
    d_out.add_near()
    v.step()
    d_out.put(2, d_out.far())
    d_attn.add()
    g_gate, g_up, g_down = (v["grads_own"][:, i * ff : (i + 1) * ff] for i in range(3))
    mlp_gain = gain_part((w_gate, w_up), (g_gate, g_up), gain_mlp)
    v.step(mlp_gain=mlp_gain)
    d_attn.put(2, d_attn.near())
    grads_out = d_out.total()
    v.step(grads_out=grads_out)
    d_attn.add_near()
    out_block = lambda d: lax.dynamic_slice_in_dim(v["grads_out"], (z ^ d) * qw, qw, 1)
    mixed = (v["hidden"] + mixed_got.astype(F32)).astype(BF16)
    v.step(mixed=mixed)
    d_attn.put(2, d_attn.far())
    v.step()
    grads_attn = d_attn.total()
    g_query, g_key, g_value = grads_attn[:, :qw], grads_attn[:, qw : qw + kw], grads_attn[:, qw + kw :]
    attn_gain = gain_part((w_query, w_key, w_value), (g_query, g_key, g_value), gain_attn)
    v.step(attn_gain=attn_gain, g_query=g_query, g_key=g_key, g_value=g_value, g_nattn=g_nattn)
    out_blocks = exchange(lambda d: out_block(d).astype(F32 if d == 0 else BF16))
    both = jnp.stack([v["attn_gain"], v["mlp_gain"]])
    step = 1
    while step < tensor:
        both = both + across(both, step)
        step *= 2
    tokens, gain_first = v["tokens"].astype(F32), v["gain_first"].astype(F32)
    g_tokens = (jnp.concatenate([v["hidden_low"], v["hidden_high"]]) + norm_back(v["g_nattn"].astype(F32), tokens, gain_first)).astype(BF16)
    return (
        v["mixed"][None],
        g_tokens[None],
        both[0],
        v["g_query"],
        v["g_key"],
        v["g_value"],
        sum(block.astype(F32) for block in out_blocks).T,
        both[1],
        g_gate,
        g_up,
        g_down.T,
    )


def solution(mesh):
    split, whole_rows = P("dp", "tensor", None), P("dp", None)
    by_row, by_column, gain = P("dp", "tensor"), P("tensor", "dp"), P("dp")
    weights = (by_row, by_row, by_row, by_column, gain, by_row, by_row, by_column)
    step = functools.partial(on_device, mesh.shape["dp"], mesh.shape["tensor"])
    return jax.shard_map(
        step,
        mesh=mesh,
        in_specs=(split, whole_rows, whole_rows, gain, *weights, split),
        out_specs=(split, split, gain, *weights),
        check_vma=False,
    )
```

```python
import functools
import jax
import jax.numpy as jnp
import numpy as np
from jax import lax
from jax.experimental import pallas as pl
from jax.experimental.pallas import tpu as pltpu
from jax.sharding import PartitionSpec as P

HEADS = 16
KV_HEADS = 8
HEAD = 96
HALF = 48
LANES = 128
LEN = 1024
QBLOCK = 256
EPSILON = 1e-05
ROTARY_BASE = 100000.0
MASKED = -1e30
SCALE = HEAD ** (-0.5)
LOG2E = 1.4426950408889634
VMEM = 56 * 2**20
F32 = jnp.float32
BF16 = jnp.bfloat16
NT = (((1,), (1,)), ((), ()))
TN = (((0,), (0,)), ((), ()))


def dot(a, b, dims=(((1,), (0,)), ((), ()))):
    return lax.dot_general(a, b, dims, preferred_element_type=F32)


def params():
    return pltpu.CompilerParams(vmem_limit_bytes=VMEM)


def rotary_select(heads):
    out = np.zeros((heads * HEAD, heads * LANES), np.float32)
    for h in range(heads):
        for i in range(HALF):
            out[h * HEAD + i, h * LANES + i] = 1
            out[h * HEAD + HALF + i, h * LANES + 64 + i] = 1
    return out


def plain_select(heads):
    out = np.zeros((heads * HEAD, heads * LANES), np.float32)
    for h in range(heads):
        for i in range(HEAD):
            out[h * HEAD + i, h * LANES + i] = 1
    return out


def rotary_tables(positions):
    halves = jnp.arange(HALF, dtype=F32)
    inverse = ROTARY_BASE ** (-2.0 * halves / HEAD)
    angles = positions.astype(F32)[:, None] * inverse
    cosine, sine = jnp.cos(angles), jnp.sin(angles)
    gap = jnp.zeros((positions.shape[0], 16), F32)
    return (
        jnp.concatenate([cosine, gap, cosine, gap], axis=1),
        jnp.concatenate([-sine, gap, sine, gap], axis=1),
    )


def turn(values, cosine, sine):
    return values * cosine + pltpu.roll(values, 64, 1) * sine


def qkv_kernel(tok_ref, gain_ref, w_ref, cos_ref, sin_ref, n_ref, q_ref, k_ref, v_ref):
    resid = tok_ref[...].astype(F32)
    scaling = lax.rsqrt(jnp.mean(resid * resid, axis=1, keepdims=True) + EPSILON)
    normed = (resid * scaling * gain_ref[...].astype(F32)).astype(BF16)
    n_ref[...] = normed
    raw = dot(normed, w_ref[...])
    cosine, sine = cos_ref[...], sin_ref[...]
    nq, nk = q_ref.shape[1] // LANES, k_ref.shape[1] // LANES
    for h in range(nq):
        part = raw[:, h * LANES : (h + 1) * LANES]
        q_ref[:, h * LANES : (h + 1) * LANES] = turn(part, cosine, sine).astype(BF16)
    for h in range(nk):
        part = raw[:, (nq + h) * LANES : (nq + h + 1) * LANES]
        k_ref[:, h * LANES : (h + 1) * LANES] = turn(part, cosine, sine).astype(BF16)
    v_ref[...] = raw[:, (nq + nk) * LANES :].astype(BF16)


def qkv(tokens, gain, weights, cosine, sine, nq, nk):
    rows, width = tokens.shape
    block = lambda n: pl.BlockSpec((256, n), lambda i: (i, 0))
    whole = lambda a: pl.BlockSpec(a.shape, lambda i: (0, 0))
    sizes = (width, nq * LANES, nk * LANES, nk * LANES)
    return pl.pallas_call(
        qkv_kernel,
        grid=(rows // 256,),
        in_specs=[
            block(width),
            whole(gain),
            pl.BlockSpec((width, (nq + 2 * nk) * LANES), lambda i: (0, 0)),
            block(LANES),
            block(LANES),
        ],
        out_specs=[block(n) for n in sizes],
        out_shape=[jax.ShapeDtypeStruct((rows, n), BF16) for n in sizes],
        compiler_params=params(),
        cost_estimate=pl.CostEstimate(
            flops=2 * rows * width * weights.shape[1], bytes_accessed=12 * 2**20, transcendentals=0
        ),
    )(tokens, gain, weights, cosine, sine)


def allowed(segc, segr, i, kn):
    same = segc == segr[:, :kn]
    rows = lax.broadcasted_iota(jnp.int32, (QBLOCK, kn), 0) + i * QBLOCK
    cols = lax.broadcasted_iota(jnp.int32, (QBLOCK, kn), 1)
    return same & (cols <= rows)


def attn_fwd_kernel(nq, nk, q_ref, k_ref, v_ref, segc_ref, segr_ref, sel_ref, o_ref, lse_ref):
    grouped = nq // nk

    def body(i):
        kn = (i + 1) * QBLOCK
        mask = allowed(segc_ref[...], segr_ref[...], i, kn)
        outs = []
        for h in range(nq):
            g = h // grouped
            lanes = slice(g * LANES, (g + 1) * LANES)
            raw = dot(q_ref[:, h * LANES : (h + 1) * LANES], k_ref[:kn, lanes], NT)
            raw = jnp.where(mask, raw, MASKED)
            top = jnp.max(raw, axis=1, keepdims=True)
            e = jnp.exp2((raw - top) * (SCALE * LOG2E))
            total = jnp.sum(e, axis=1, keepdims=True)
            p = (e * (1.0 / total)).astype(BF16)
            outs.append(dot(p, v_ref[:kn, lanes]).astype(BF16))
            lse_ref[:, h : h + 1] = top * (SCALE * LOG2E) + jnp.log2(total)
        o_ref[...] = dot(jnp.concatenate(outs, axis=1), sel_ref[...], NT).astype(BF16)

    for i in range(LEN // QBLOCK):
        pl.when(pl.program_id(0) == i)(functools.partial(body, i))


def attn_fwd(q, k, v, segc, segr, sel, nq, nk):
    block = lambda n: pl.BlockSpec((QBLOCK, n), lambda i: (i, 0))
    whole = lambda a: pl.BlockSpec(a.shape, lambda i: (0, 0))
    return pl.pallas_call(
        functools.partial(attn_fwd_kernel, nq, nk),
        grid=(LEN // QBLOCK,),
        in_specs=[block(nq * LANES), whole(k), whole(v), block(1), whole(segr), whole(sel)],
        out_specs=[block(nq * HEAD), block(8)],
        out_shape=[
            jax.ShapeDtypeStruct((LEN, nq * HEAD), BF16),
            jax.ShapeDtypeStruct((LEN, 8), F32),
        ],
        compiler_params=params(),
        cost_estimate=pl.CostEstimate(
            flops=4 * nq * LEN * LEN * LANES, bytes_accessed=6 * 2**20, transcendentals=nq * LEN * LEN
        ),
    )(q, k, v, segc, segr, sel)


def attn_bwd_kernel(
    nq, nk, at_ref, q_ref, k_ref, v_ref, segc_ref, segr_ref, lse_ref, o_ref, do_ref, cos_ref, sin_ref,
    cosa_ref, sina_ref, selv_ref, selr_ref, g_ref, dk_ref, dv_ref,
):
    grouped = nq // nk
    wide = nq * HEAD

    @pl.when(pl.program_id(0) == 0)
    def _():
        dk_ref[...] = jnp.zeros_like(dk_ref)
        dv_ref[...] = jnp.zeros_like(dv_ref)

    def body(i):
        kn = (i + 1) * QBLOCK
        mask = allowed(segc_ref[...], segr_ref[...], i, kn)
        mask = jnp.concatenate([mask] * grouped, axis=0)
        do_all = dot(do_ref[0], selv_ref[...]).astype(BF16)
        inner = do_all.astype(F32) * dot(o_ref[...], selv_ref[...])
        turned = []
        for g in range(nk):
            lanes = slice(g * LANES, (g + 1) * LANES)
            heads = range(g * grouped, (g + 1) * grouped)
            stack = lambda of: jnp.concatenate([of(slice(h * LANES, (h + 1) * LANES)) for h in heads], axis=0)
            q = stack(lambda part: q_ref[:, part])
            grad = stack(lambda part: do_all[:, part])
            delta = stack(lambda part: jnp.sum(inner[:, part], axis=1, keepdims=True))
            lse = jnp.concatenate([lse_ref[:, h : h + 1] for h in heads], axis=0)
            raw = dot(q, k_ref[:kn, lanes], NT)
            p = jnp.where(mask, jnp.exp2(raw * (SCALE * LOG2E) - lse), 0.0)
            ds = (p * (dot(grad, v_ref[:kn, lanes], NT) - delta)).astype(BF16)
            dq = dot(ds, k_ref[:kn, lanes]) * SCALE
            for j in range(grouped):
                rows = slice(j * QBLOCK, (j + 1) * QBLOCK)
                turned.append(turn(dq[rows], cos_ref[...], -sin_ref[...]).astype(BF16))
            dk_ref[:kn, lanes] += dot(ds, q, TN)
            dv_ref[:kn, lanes] += dot(p.astype(BF16), grad, TN)
        rows = slice(i * QBLOCK, (i + 1) * QBLOCK)
        g_ref[rows, :wide] = dot(jnp.concatenate(turned, axis=1), selr_ref[...], NT).astype(BF16)

    blocks = LEN // QBLOCK
    for i in range(blocks):
        pl.when(pl.program_id(0) == i)(functools.partial(body, i))

    @pl.when(pl.program_id(0) == blocks - 1)
    def _():
        turned = []
        for g in range(nk):
            lanes = slice(g * LANES, (g + 1) * LANES)
            turned.append(turn(dk_ref[:, lanes] * SCALE, cosa_ref[...], -sina_ref[...]).astype(BF16))
        kw = nk * HEAD
        gk = dot(jnp.concatenate(turned, axis=1), selr_ref[:kw, : nk * LANES], NT)
        gv = dot(dv_ref[...].astype(BF16), selv_ref[:kw, : nk * LANES], NT)
        g_ref[:, wide:] = jnp.concatenate([gk, gv], axis=1).astype(BF16)


def attn_bwd(at, q, k, v, segc, segr, lse, o, do, cosine, sine, selv, selr, nq, nk):
    block = lambda n: pl.BlockSpec((QBLOCK, n), lambda i, at: (i, 0))
    whole = lambda a: pl.BlockSpec(a.shape, lambda i, at: (0, 0))
    total = (nq + 2 * nk) * HEAD
    return pl.pallas_call(
        functools.partial(attn_bwd_kernel, nq, nk),
        grid_spec=pltpu.PrefetchScalarGridSpec(
            num_scalar_prefetch=1,
            grid=(LEN // QBLOCK,),
            in_specs=[
                block(nq * LANES), whole(k), whole(v), block(1), whole(segr), block(8), block(nq * HEAD),
                pl.BlockSpec((1, QBLOCK, nq * HEAD), lambda i, at: (at[i], 0, 0)),
                block(LANES), block(LANES), whole(cosine), whole(sine), whole(selv), whole(selr),
            ],
            out_specs=pl.BlockSpec((LEN, total), lambda i, at: (0, 0)),
            scratch_shapes=[pltpu.VMEM((LEN, nk * LANES), F32), pltpu.VMEM((LEN, nk * LANES), F32)],
        ),
        out_shape=jax.ShapeDtypeStruct((LEN, total), BF16),
        compiler_params=params(),
        cost_estimate=pl.CostEstimate(
            flops=10 * nq * LEN * LEN * LANES, bytes_accessed=8 * 2**20, transcendentals=nq * LEN * LEN
        ),
    )(at, q, k, v, segc, segr, lse, o, do, cosine, sine, cosine, sine, selv, selr)


def cost(flops, megabytes):
    return pl.CostEstimate(flops=flops, bytes_accessed=megabytes * 2**20, transcendentals=0)


def outproj_kernel(me_ref, att_ref, w_ref, tok_ref, gain_ref, n_ref, hid_ref):
    hidden = tok_ref[...].astype(F32)
    wide = att_ref.shape[2]
    for z in range(att_ref.shape[0]):
        hidden = hidden + dot(att_ref[z], w_ref[:, z * wide : (z + 1) * wide], NT)
    scaling = lax.rsqrt(jnp.mean(hidden * hidden, axis=1, keepdims=True) + EPSILON)
    n_ref[...] = (hidden * scaling * gain_ref[...].astype(F32)).astype(BF16)
    hid_ref[...] = hidden


def outproj(me, att, weights, tokens, gain):
    parts, rows, wide = att.shape
    width = tokens.shape[1]
    piece = rows // parts
    at = lambda i, me: lax.rem(me[0] + 1 + i, parts)
    return pl.pallas_call(
        outproj_kernel,
        grid_spec=pltpu.PrefetchScalarGridSpec(
            num_scalar_prefetch=1,
            grid=(parts,),
            in_specs=[
                pl.BlockSpec((parts, piece, wide), lambda i, me: (0, at(i, me), 0)),
                pl.BlockSpec((width, parts * wide), lambda i, me: (0, 0)),
                pl.BlockSpec((piece, width), lambda i, me: (at(i, me), 0)),
                pl.BlockSpec(gain.shape, lambda i, me: (0, 0)),
            ],
            out_specs=[
                pl.BlockSpec((piece, width), lambda i, me: (at(i, me), 0)),
                pl.BlockSpec((piece, width), lambda i, me: (0, 0)),
            ],
        ),
        out_shape=[jax.ShapeDtypeStruct((rows, width), BF16), jax.ShapeDtypeStruct((piece, width), F32)],
        compiler_params=params(),
        cost_estimate=cost(2 * rows * width * width, 16),
    )(me, att, weights, tokens, gain)


def mlp_kernel(n_ref, cot_ref, wg_ref, wu_ref, wd_ref, out_ref, gn_ref, sum_ref):
    step = pl.program_id(0)
    rows, width = sum_ref.shape
    normed = n_ref[...].reshape(rows, width)
    gate = dot(normed, wg_ref[...])
    upward = dot(normed, wu_ref[...])
    g_act = dot(cot_ref[...].reshape(rows, width), wd_ref[...])
    sigma = jax.nn.sigmoid(gate)
    silu = gate * sigma
    out_ref[2] = (silu * upward).astype(BF16)
    g_gate = (g_act * upward * (sigma + silu * (1.0 - sigma))).astype(BF16)
    g_up = (g_act * silu).astype(BF16)
    out_ref[0] = g_gate
    out_ref[1] = g_up
    part = dot(g_gate, wg_ref[...], NT) + dot(g_up, wu_ref[...], NT)

    @pl.when(step == 0)
    def _():
        sum_ref[...] = part

    @pl.when(step > 0)
    def _():
        sum_ref[...] += part

    @pl.when(step == pl.num_programs(0) - 1)
    def _():
        gn_ref[...] = sum_ref[...].astype(BF16)


def mlp(normed, cot, weights, index):
    parts, size, width = cot.shape
    rows = parts * size
    units = weights.shape[1] // 3
    chunk = 512
    steps = units // chunk
    some = pl.BlockSpec((parts, size, width), lambda j: (0, index, 0))
    column = lambda k: pl.BlockSpec((width, chunk), lambda j: (0, k * steps + j))
    return pl.pallas_call(
        mlp_kernel,
        grid=(steps,),
        in_specs=[some, pl.BlockSpec(cot.shape, lambda j: (0, 0, 0)), column(0), column(1), column(2)],
        out_specs=[
            pl.BlockSpec((3, rows, chunk), lambda j: (0, 0, j)),
            pl.BlockSpec((rows, width), lambda j: (0, 0)),
        ],
        out_shape=[
            jax.ShapeDtypeStruct((3, rows, units), BF16),
            jax.ShapeDtypeStruct((rows, width), BF16),
        ],
        scratch_shapes=[pltpu.VMEM((rows, width), F32)],
        compiler_params=params(),
        cost_estimate=cost(10 * rows * width * units, 24),
    )(normed, cot, weights, weights, weights)


def down_kernel(most_ref, few_ref, w_ref, out_ref):
    cut = most_ref.shape[1] // out_ref.shape[0]
    for u_ref, rows in ((most_ref, slice(0, cut)), (few_ref, slice(cut, None))):
        out = dot(u_ref[0], w_ref[...], NT).astype(BF16)
        out_ref[:, rows] = out.reshape(out_ref.shape[0], -1, out_ref.shape[2])


def down(most, few, weights, parts):
    units = most.shape[2]
    width = weights.shape[0]
    piece = (most.shape[1] + few.shape[1]) // parts
    return pl.pallas_call(
        down_kernel,
        grid=(1,),
        in_specs=[
            pl.BlockSpec((1, most.shape[1], units), lambda h: (2, 0, 0)),
            pl.BlockSpec((1, few.shape[1], units), lambda h: (2, 0, 0)),
            pl.BlockSpec((width, units), lambda h: (0, 2)),
        ],
        out_specs=pl.BlockSpec((parts, piece, width), lambda h: (0, 0, 0)),
        out_shape=jax.ShapeDtypeStruct((parts, piece, width), BF16),
        compiler_params=params(),
        cost_estimate=cost(2 * parts * piece * width * units, 12),
    )(most, few, weights)


def norm_back(incoming, values, gain):
    scaling = lax.rsqrt(jnp.mean(values * values, axis=1, keepdims=True) + EPSILON)
    unit = values * scaling
    tilted = incoming * gain
    return scaling * (tilted - unit * jnp.mean(tilted * unit, axis=1, keepdims=True))


def branch_kernel(at_ref, got_ref, hid_ref, cot_ref, gain_ref, w_ref, gh_ref, gb_ref, ga_ref):
    @pl.when(pl.program_id(0) == 0)
    def _():
        back = norm_back(got_ref[...].astype(F32), hid_ref[...], gain_ref[...].astype(F32))
        g_hidden = cot_ref[...].astype(F32) + back
        gh_ref[...] = g_hidden
        gb_ref[...] = g_hidden.astype(BF16)

    ga_ref[0] = dot(gb_ref[...], w_ref[...]).astype(BF16)


def branch(at, got, hidden, cot, gain, weights, parts, index):
    rows, width = got.shape
    wide = weights.shape[1] // parts
    whole = pl.BlockSpec((rows, width), lambda i, at: (0, 0))
    some = pl.BlockSpec((rows, width), lambda i, at: (index, 0))
    return pl.pallas_call(
        branch_kernel,
        grid_spec=pltpu.PrefetchScalarGridSpec(
            num_scalar_prefetch=1,
            grid=(parts,),
            in_specs=[
                whole,
                some,
                some,
                pl.BlockSpec(gain.shape, lambda i, at: (0, 0)),
                pl.BlockSpec((width, wide), lambda i, at: (0, at[i])),
            ],
            out_specs=[whole, whole, pl.BlockSpec((1, rows, wide), lambda i, at: (i, 0, 0))],
        ),
        out_shape=[
            jax.ShapeDtypeStruct((rows, width), F32),
            jax.ShapeDtypeStruct((rows, width), BF16),
            jax.ShapeDtypeStruct((parts, rows, wide), BF16),
        ],
        compiler_params=params(),
        cost_estimate=cost(2 * rows * width * parts * wide, 10),
    )(at, got, hidden, cot, gain, weights)


def wgrad_kernel(uses, count, core_ref, *refs):
    keep_ref, send_ref = refs[-2:]
    lefts, rights = refs[:count], refs[count:-2]
    half = keep_ref.shape[1]
    at = 0
    for terms in uses:
        total = None
        for left, rows, right, k in terms:
            a = lefts[left][:, rows].reshape(-1, lefts[left].shape[2])
            b = rights[right][...] if k is None else rights[right][k]
            product = dot(a, b, TN)
            total = product if total is None else total + product
        block = total.astype(BF16)
        columns = slice(at, at + block.shape[1])

        @pl.when(core_ref[0] == 0)
        def _():
            keep_ref[0, :, columns] = block[:half]
            send_ref[0, :, columns] = block[half:]

        @pl.when(core_ref[0] == 1)
        def _():
            keep_ref[0, :, columns] = block[half:]
            send_ref[0, :, columns] = block[:half]

        at += block.shape[1]


def wgrad(core, lefts, uses, rights, dp):
    pieces, rows, width = lefts[0].shape
    shard = width // dp
    columns = sum(rights[terms[0][2]].shape[-1] for terms in uses)
    pairs = dp // 2
    out = jax.ShapeDtypeStruct((pairs, shard, columns), BF16)
    out_spec = pl.BlockSpec((1, shard, columns), lambda i, core: (i, 0, 0))
    return pl.pallas_call(
        functools.partial(wgrad_kernel, uses, len(lefts)),
        grid_spec=pltpu.PrefetchScalarGridSpec(
            num_scalar_prefetch=1,
            grid=(pairs,),
            in_specs=[pl.BlockSpec((*a.shape[:2], 2 * shard), lambda i, core: (0, 0, i)) for a in lefts]
            + [pl.BlockSpec(r.shape, lambda i, core, d=r.ndim: (0,) * d) for r in rights],
            out_specs=[out_spec, out_spec],
        ),
        out_shape=[out, out],
        compiler_params=params(),
        cost_estimate=cost(2 * pieces * rows * width * columns, 16),
    )(core, *lefts, *rights)


def assemble_kernel(at_ref, *refs):
    pieces, out_ref = refs[:-1], refs[-1]
    for i, piece in enumerate(pieces):
        rows = piece.shape[0]
        out_ref[pl.ds(pl.multiple_of(at_ref[i], rows), rows)] = piece[...]


def assemble(starts, pieces):
    rows, columns = sum(p.shape[0] for p in pieces), pieces[0].shape[1]
    chunk = max(c for c in range(128, 769, 128) if columns % c == 0)
    block = lambda n: pl.BlockSpec((n, chunk), lambda j, at: (0, j))
    return pl.pallas_call(
        assemble_kernel,
        grid_spec=pltpu.PrefetchScalarGridSpec(
            num_scalar_prefetch=1,
            grid=(columns // chunk,),
            in_specs=[block(p.shape[0]) for p in pieces],
            out_specs=block(rows),
        ),
        out_shape=jax.ShapeDtypeStruct((rows, columns), pieces[0].dtype),
        compiler_params=params(),
        cost_estimate=pl.CostEstimate(flops=0, bytes_accessed=4 * rows * columns, transcendentals=0),
    )(jnp.stack(starts).astype(jnp.int32), *pieces)


def blend_kernel(core_ref, mine_ref, other_ref, out_ref):
    half = mine_ref.shape[0]

    @pl.when(core_ref[0] == 0)
    def _():
        out_ref[:half] = mine_ref[...]
        out_ref[half:] = other_ref[...]

    @pl.when(core_ref[0] == 1)
    def _():
        out_ref[:half] = other_ref[...]
        out_ref[half:] = mine_ref[...]


def blend(core, mine, other, chips):
    rows, columns = mine.shape
    shard = rows // chips
    block = pl.BlockSpec((shard, columns), lambda i, core: (i, 0))
    return pl.pallas_call(
        blend_kernel,
        grid_spec=pltpu.PrefetchScalarGridSpec(
            num_scalar_prefetch=1,
            grid=(chips,),
            in_specs=[block, block],
            out_specs=pl.BlockSpec((2 * shard, columns), lambda i, core: (i, 0)),
        ),
        out_shape=jax.ShapeDtypeStruct((2 * rows, columns), mine.dtype),
        compiler_params=params(),
        cost_estimate=pl.CostEstimate(flops=0, bytes_accessed=8 * rows * columns, transcendentals=0),
    )(core, mine, other)


def swap(value, axis, size, bit):
    return lax.ppermute(value, axis, [(k, k ^ bit) for k in range(size)])


class Phases(dict):
    def step(self, **more):
        self.update(more)
        names = [name for name in self if self[name] is not None]
        self.update(zip(names, lax.optimization_barrier([self[name] for name in names])))

    def drop(self, *names):
        for name in names:
            del self[name]


class Gather:
    def __init__(self, place, v, name):
        self.place, self.v, self.names = place, v, [name + str(i) for i in range(12)]

    def get(self, first, last):
        return [self.v[name] for name in self.names[first:last]]

    def put(self, first, values):
        self.v.update(zip(self.names[first:], values))

    def shard(self, value):
        self.put(0, [value])

    def near(self):
        if not self.place.grid:
            return []
        (value,) = self.get(0, 1)
        return [swap(value, "dp", 8, 2), swap(value, "dp", 8, 4)]

    def halves(self):
        if not self.place.grid:
            return []
        by_x, by_y = self.get(1, 3)
        half = by_x.shape[0] // 2
        return [by_x[:half], by_y[half:]]

    def far(self):
        if not self.place.grid:
            return []
        top, low = self.get(10, 12)
        self.v.drop(*self.names[10:12])
        return [swap(top, "dp", 8, 4), swap(low, "dp", 8, 2)]

    def stack(self):
        if not self.place.grid:
            return []
        pieces = self.get(0, 5)
        rows = pieces[0].shape[0]
        x, y = self.place.x, self.place.y
        chips = [2 * y + x, 2 * y + 1 - x, 2 - 2 * y + x, 3 - 2 * y - x, 3 - 2 * y - x]
        below = [0, 0, 0, 0, rows // 2]
        self.v.drop(*self.names[1:5])
        return [assemble([chip * rows + low for chip, low in zip(chips, below)], pieces)]

    def cores(self):
        return [swap(self.get(5, 6)[0], "dp", 8, 1)] if self.place.grid else []

    def each(self, first, last):
        return [swap(value, "dp", 8, 1) for value in self.get(first, last)] if self.place.grid else []

    def whole_of_pieces(self):
        if not self.place.grid:
            return lax.all_gather(self.get(0, 1)[0], "dp", axis=0, tiled=True)
        pieces = self.get(0, 10)
        rows = pieces[0].shape[0]
        x, y, core = self.place.x, self.place.y, self.place.core
        chips = [2 * y + x, 2 * y + 1 - x, 2 - 2 * y + x, 3 - 2 * y - x, 3 - 2 * y - x]
        below = [0, 0, 0, 0, rows // 2]
        starts = [(2 * chip + core) * rows + low for chip, low in zip(chips, below)]
        starts += [(2 * chip + 1 - core) * rows + low for chip, low in zip(chips, below)]
        self.v.drop(*self.names)
        return assemble(starts, pieces)

    def whole(self):
        if not self.place.grid:
            return lax.all_gather(self.get(0, 1)[0], "dp", axis=0, tiled=True)
        mine, other = self.get(5, 7)
        self.v.drop(*self.names[5:7])
        return blend(self.place.core.astype(jnp.int32).reshape(1), mine, other, 4)


class Scatter:
    def __init__(self, place, v, name):
        self.place, self.v, self.names = place, v, [name + str(i) for i in range(4)]

    def get(self, count):
        return [self.v[name] for name in self.names[:count]]

    def put(self, first, values):
        self.v.update(zip(self.names[first:], values))

    def product(self, lefts, uses, rights):
        if self.place.grid:
            core = self.place.core.astype(jnp.int32).reshape(1)
            self.put(0, wgrad(core, lefts, uses, rights, 8))
            return
        groups = []
        for terms in uses:
            total = 0.0
            for left, rows, right, k in terms:
                a = lefts[left][:, rows].reshape(-1, lefts[left].shape[2])
                total = total + dot(a, rights[right] if k is None else rights[right][k], TN)
            groups.append(total.astype(BF16))
        self.put(0, [jnp.concatenate(groups, axis=1)])

    def cores(self):
        if self.place.grid:
            self.put(1, [swap(self.get(2)[1], "dp", 8, 1)])

    def add(self):
        if not self.place.grid:
            return
        keep, got = self.get(2)
        both = (keep.astype(F32) + got.astype(F32)).astype(BF16)
        rows, columns = both.shape[1:]
        both = both.reshape(2, 2, rows, columns)
        left, right = both[..., : columns // 2], both[..., columns // 2 :]
        x, y = self.place.x, self.place.y
        self.put(0, [pick(left, x, 1), pick(right, y, 0), pick(left, 1 - x, 1), pick(right, 1 - y, 0)])

    def near(self):
        if not self.place.grid:
            return []
        _, _, left, right = self.get(4)
        return [swap(left, "dp", 8, 2), swap(right, "dp", 8, 4)]

    def add_near(self):
        if not self.place.grid:
            return
        left, right, got_left, got_right = self.get(4)
        left = (left.astype(F32) + got_left.astype(F32)).astype(BF16)
        right = (right.astype(F32) + got_right.astype(F32)).astype(BF16)
        x, y = self.place.x, self.place.y
        self.put(0, [pick(left, y, 0), pick(right, x, 0), pick(left, 1 - y, 0), pick(right, 1 - x, 0)])

    def far(self):
        if not self.place.grid:
            return []
        _, _, left, right = self.get(4)
        return [swap(left, "dp", 8, 4), swap(right, "dp", 8, 2)]

    def total(self):
        if not self.place.grid:
            whole = self.get(1)[0]
            return lax.psum_scatter(whole, "dp", scatter_dimension=0, tiled=True).astype(F32)
        left, right, got_left, got_right = (value.astype(F32) for value in self.get(4))
        self.v.drop(*self.names)
        return jnp.concatenate([left + got_left, right + got_right], axis=1)


def pick(value, index, axis):
    return lax.dynamic_index_in_dim(value, index, axis, keepdims=False)


class Place:
    def __init__(self, size):
        index = lax.axis_index("dp")
        self.grid = size == 8
        self.core = lax.rem(index, 2)
        self.x = lax.rem(index // 2, 2)
        self.y = index // 4


def on_device(
    dp,
    tensor,
    tokens,
    segments,
    positions,
    gain_attn,
    w_query,
    w_key,
    w_value,
    w_out,
    gain_mlp,
    w_gate,
    w_up,
    w_down,
    cotangent,
):
    piece, width = tokens.shape[1:]
    nq, nk = w_query.shape[1] // HEAD, w_key.shape[1] // HEAD
    qw, kw = nq * HEAD, nk * HEAD
    wide = qw + 2 * kw
    ff = w_gate.shape[1]
    place = Place(dp)
    z = lax.axis_index("tensor")
    at = jnp.arange(tensor, dtype=jnp.int32) ^ z.astype(jnp.int32)
    across = lambda value, bit: swap(value, "tensor", tensor, bit)

    def exchange(block_for):
        got = {d: across(block_for(d), d) for d in reversed(range(1, tensor))}
        return [block_for(0)] + [got[d] for d in range(1, tensor)]

    def piece_of(value, d):
        return lax.dynamic_slice_in_dim(value, (z ^ d) * piece, piece, 0)

    select = np.zeros((wide, (nq + 2 * nk) * LANES), np.float32)
    select[:qw, : nq * LANES] = rotary_select(nq)
    select[qw : qw + kw, nq * LANES : (nq + nk) * LANES] = rotary_select(nk)
    select[qw + kw :, (nq + nk) * LANES :] = plain_select(nk)
    select = jnp.asarray(select, BF16)
    sel_plain, sel_turn = jnp.asarray(plain_select(nq), BF16), jnp.asarray(rotary_select(nq), BF16)

    v = Phases()
    heads = Gather(place, v, "heads")
    back = Gather(place, v, "back")
    own = Gather(place, v, "own")
    d_own = Scatter(place, v, "d_own")
    d_out = Scatter(place, v, "d_out")
    d_attn = Scatter(place, v, "d_attn")

    all_tokens = lax.all_gather(tokens[0], "tensor", axis=0, tiled=True)
    gains = jnp.pad(jnp.stack([gain_attn, gain_mlp], axis=1), ((0, 0), (0, LANES - 2)))
    w_heads = jnp.concatenate([w_query, w_key, w_value], axis=1)
    spread = dot(w_heads, select).astype(BF16)
    heads.shard(jnp.concatenate([spread, gains], axis=1))
    heads.put(1, heads.near())
    mlp_shard = jnp.concatenate([w_gate, w_up, w_down.T], axis=1)
    own.shard(mlp_shard)
    v.step(tokens=tokens[0], cot=cotangent[0], at=at, out_turned=w_out.T)

    heads.put(10, heads.halves())
    heads.put(3, heads.far())
    own_near = own.near()
    cosine, sine = rotary_tables(positions[0])
    v.step(cosine=cosine, sine=sine, segc=segments[0][:, None], segr=segments)

    cut = 5 * piece // 8
    cot_low = lax.all_gather(v["cot"][:cut], "tensor", axis=0, tiled=False)
    heads.put(5, heads.stack())
    heads.put(6, heads.cores())
    w_spread = heads.whole()
    own.put(1, own_near)
    v.step(w_spread=w_spread)

    out_blocks = exchange(lambda d: v["out_turned"])
    own.put(10, own.halves())
    own.put(3, own.far())
    picked = dot(jnp.eye(8, LANES, dtype=BF16), v["w_spread"][:, spread.shape[1] :], NT).astype(BF16)
    v.step(all_tokens=all_tokens, gain_first=picked[:1], gain_second=picked[1:2])

    normed, q, k, val = qkv(v["all_tokens"], v["gain_first"], v["w_spread"], v["cosine"], v["sine"], nq, nk)
    att, lse = attn_fwd(q, k, val, v["segc"], v["segr"], sel_plain, nq, nk)
    own.put(5, own.stack())
    v.step(
        normed=normed, q=q, k=k, v=val, att=att, lse=lse, cot_low=cot_low, **{"out%d" % d: out_blocks[d] for d in range(tensor)}
    )

    att_all = lax.all_gather(v["att"], "tensor", axis=0, tiled=False)
    shard = jnp.zeros((w_out.shape[1], width), BF16)
    for d in range(tensor):
        shard = lax.dynamic_update_slice_in_dim(shard, v.pop("out%d" % d), (z ^ d) * qw, 1)
    back.shard(shard)
    back.put(1, back.near())
    own.put(6, own.cores())
    back.put(10, back.halves())
    back.put(3, back.far())
    back.put(5, back.stack())
    back.put(6, back.cores())
    w_own = own.whole()
    w_back = back.whole()
    v.step(att_all=att_all, w_back=w_back, w_own=w_own)

    cot_high = lax.all_gather(v["cot"][cut:], "tensor", axis=0, tiled=False)
    me = z.astype(jnp.int32).reshape(1)
    normed_mlp, hidden = outproj(me, v["att_all"], v["w_back"], v["all_tokens"], v["gain_second"])
    v.step(normed_mlp=normed_mlp.reshape(tensor, piece, width), hidden=hidden)

    units_low, g_low = mlp(v["normed_mlp"], v["cot_low"], v["w_own"], 0)
    v.step(units_low=units_low, g_low=g_low, cot_high=cot_high)
    got_low = lax.psum_scatter(v["g_low"], "tensor", scatter_dimension=0, tiled=True)
    units_high, g_high = mlp(v["normed_mlp"][:, cut:], v["cot_high"], v["w_own"], 0)
    v.step(units_high=units_high, g_high=g_high)

    got_high = lax.psum_scatter(v["g_high"], "tensor", scatter_dimension=0, tiled=True)
    lefts, rights = [v["normed_mlp"], v["cot_low"], v["cot_high"]], [v["units_low"], v["units_high"]]
    every, first_rows, last_rows = slice(None), slice(0, cut), slice(cut, None)
    gate_up = [[(0, first_rows, 0, k), (0, last_rows, 1, k)] for k in range(2)]
    d_own.product(lefts, gate_up + [[(1, every, 0, 2), (2, every, 1, 2)]], rights)
    w_compact = dot(v["w_spread"][:, : spread.shape[1]], select, NT).astype(BF16)
    v.step(got_low=got_low, w_compact=w_compact)
    hidden_low, branch_low, att_low = branch(
        v["at"], v["got_low"], v["hidden"], v["cot"], v["gain_second"], v["w_back"], tensor, 0
    )
    v.update(hidden_low=hidden_low, branch_low=branch_low)
    blocks_low = exchange(lambda d: att_low[d])
    d_own.cores()
    mixed_part = down(v["units_low"], v["units_high"], v["w_own"], tensor)
    v.update(mixed_part=mixed_part)
    d_own.add()
    v.step(got_high=got_high, **{"low%d" % d: blocks_low[d] for d in range(tensor)})

    mixed_got = lax.psum_scatter(v["mixed_part"].reshape(LEN, width), "tensor", scatter_dimension=0, tiled=True)
    near = d_own.near()
    hidden_high, branch_high, att_high = branch(
        v["at"], v["got_high"], v["hidden"][cut:], v["cot"][cut:], v["gain_second"], v["w_back"], tensor, 0
    )
    v.step(hidden_high=hidden_high, branch_high=branch_high, att_high=att_high)

    blocks_high = exchange(lambda d: v["att_high"][d])
    att_own = lax.dynamic_slice_in_dim(v["att_all"], z * piece, piece, 1)
    g_branch = jnp.concatenate([v["branch_low"], v["branch_high"]])
    d_out.product([g_branch[None]], [[(0, every, 0, k)] for k in range(tensor)], [att_own])
    d_own.put(2, near)
    v.step(g_heads=jnp.stack([jnp.concatenate([v.pop("low%d" % d), blocks_high[d]]) for d in range(tensor)]))
    d_own.add_near()
    v.step()

    d_out.cores()
    d_own.put(2, d_own.far())
    g_qkv = attn_bwd(
        v["at"], v["q"], v["k"], v["v"], v["segc"], v["segr"], v["lse"], v["att"], v["g_heads"], v["cosine"], v["sine"],
        sel_plain, sel_turn, nq, nk,
    )
    g_nattn = dot(g_qkv, v["w_compact"], NT).astype(BF16)
    v.step(g_qkv=g_qkv, g_nattn=g_nattn)

    g_nattn = lax.psum_scatter(v["g_nattn"], "tensor", scatter_dimension=0, tiled=True)
    d_out.add()
    v.step()
    d_out.put(2, d_out.near())
    d_attn.product([v["normed"][None]], [[(0, every, 0, None)]], [v["g_qkv"]])
    grads_own = d_own.total()
    v.step(grads_own=grads_own)

    def gain_part(weights, grads, gain):
        total = sum(jnp.sum(w.astype(F32) * g, axis=1) for w, g in zip(weights, grads))
        return total / gain.astype(F32)

    d_attn.cores()
    d_out.add_near()
    v.step()
    d_out.put(2, d_out.far())
    d_attn.add()
    g_gate, g_up, g_down = (v["grads_own"][:, i * ff : (i + 1) * ff] for i in range(3))
    mlp_gain = gain_part((w_gate, w_up), (g_gate, g_up), gain_mlp)
    v.step(mlp_gain=mlp_gain)
    d_attn.put(2, d_attn.near())
    grads_out = d_out.total()
    v.step(grads_out=grads_out)
    d_attn.add_near()
    out_block = lambda d: lax.dynamic_slice_in_dim(v["grads_out"], (z ^ d) * qw, qw, 1)
    mixed = (v["hidden"] + mixed_got.astype(F32)).astype(BF16)
    v.step(mixed=mixed)
    d_attn.put(2, d_attn.far())
    v.step()
    grads_attn = d_attn.total()
    g_query, g_key, g_value = grads_attn[:, :qw], grads_attn[:, qw : qw + kw], grads_attn[:, qw + kw :]
    attn_gain = gain_part((w_query, w_key, w_value), (g_query, g_key, g_value), gain_attn)
    v.step(attn_gain=attn_gain, g_query=g_query, g_key=g_key, g_value=g_value, g_nattn=g_nattn)
    out_blocks = exchange(lambda d: out_block(d).astype(F32 if d == 0 else BF16))
    both = jnp.stack([v["attn_gain"], v["mlp_gain"]])
    step = 1
    while step < tensor:
        both = both + across(both, step)
        step *= 2
    tokens, gain_first = v["tokens"].astype(F32), v["gain_first"].astype(F32)
    g_tokens = (jnp.concatenate([v["hidden_low"], v["hidden_high"]]) + norm_back(v["g_nattn"].astype(F32), tokens, gain_first)).astype(BF16)
    return (
        v["mixed"][None],
        g_tokens[None],
        both[0],
        v["g_query"],
        v["g_key"],
        v["g_value"],
        sum(block.astype(F32) for block in out_blocks).T,
        both[1],
        g_gate,
        g_up,
        g_down.T,
    )


def solution(mesh):
    split, whole_rows = P("dp", "tensor", None), P("dp", None)
    by_row, by_column, gain = P("dp", "tensor"), P("tensor", "dp"), P("dp")
    weights = (by_row, by_row, by_row, by_column, gain, by_row, by_row, by_column)
    step = functools.partial(on_device, mesh.shape["dp"], mesh.shape["tensor"])
    return jax.shard_map(
        step,
        mesh=mesh,
        in_specs=(split, whole_rows, whole_rows, gain, *weights, split),
        out_specs=(split, split, gain, *weights),
        check_vma=False,
    )
```
